32 devices in a mesh: fsdp: 2 (over x), ctx: 4 (over y, core), tp: 4 (over z).
Axes of the slice: x: 2, y: 2, z: 4, core: 2. Of those that a mesh axis runs over, the one named last changes fastest.
Arguments:
- tokens: bfloat16 [8192, 2048], P(('fsdp', 'ctx'), 'tp'), may hold values from -6 to 6
- memory: bfloat16 [8192, 4096], P(('fsdp', 'ctx'), 'tp'), may hold values from -6 to 6
- dealing: int32 [8192], P(('fsdp', 'ctx')), may hold values from 0 to 8191, as said below
- cotangent: bfloat16 [8192, 2048], P(('fsdp', 'ctx'), 'tp'), may hold values from -6 to 6
- gain_first: float32 [2048], replicated, may hold values from 0.25 to 1.75
- gain_second: float32 [2048], replicated, may hold values from 0.25 to 1.75
- memory_gate: bfloat16 [2048, 4096], P(('fsdp', 'ctx'), 'tp'), may hold values from -0.125 to 0.125
- memory_out: bfloat16 [4096, 2048], P('tp', ('fsdp', 'ctx')), may hold values from -0.09375 to 0.09375
- hidden_gate: bfloat16 [2048, 8192], P(('fsdp', 'ctx'), 'tp'), may hold values from -0.125 to 0.125
- hidden_up: bfloat16 [2048, 8192], P(('fsdp', 'ctx'), 'tp'), may hold values from -0.125 to 0.125
- hidden_down: bfloat16 [8192, 2048], P('tp', ('fsdp', 'ctx')), may hold values from -0.0625 to 0.0625
Outputs:
- block_out: bfloat16 [8192, 2048], P(('fsdp', 'ctx'), 'tp')
- grad_tokens: float32 [8192, 2048], P(('fsdp', 'ctx'), 'tp')
- grad_memory: float32 [8192, 4096], P(('fsdp', 'ctx'), 'tp')
- grad_gain_first: float32 [2048], replicated
- grad_gain_second: float32 [2048], replicated
- grad_memory_gate: float32 [2048, 4096], P(('fsdp', 'ctx'), 'tp')
- grad_memory_out: float32 [4096, 2048], P('tp', ('fsdp', 'ctx'))
- grad_hidden_gate: float32 [2048, 8192], P(('fsdp', 'ctx'), 'tp')
- grad_hidden_up: float32 [2048, 8192], P(('fsdp', 'ctx'), 'tp')
- grad_hidden_down: float32 [8192, 2048], P('tp', ('fsdp', 'ctx'))
The draws below stay inside these ranges and needn't reach their ends.
Inputs may be any that keep to these rules, and one draw needn't show every extreme that they name: dealing holds every number of 0 to 8191 once; the 1024 slots of each index of fsdp+ctx hold exactly 128 tokens of each index's own block of 1024 initial tokens.
All inputs are finite; a program needn't handle non-finite values.
Results may differ from the reference program's by a relative error of at most 0.0075.
Values may be sent and summed in bfloat16 or wider, within the bound.
A program may use at most 256 MiB of HBM per device.

```python
import jax
import jax.numpy as jnp
from jax import lax

D = 2048
C = 4096
FF = 8192
TOK_DEV = 1024
TOKENS = 8192
N_FSDP = 2
N_CTX = 4


def draw_dealing(key, part):
    groups = N_FSDP * N_CTX
    block = TOK_DEV // groups
    keys = jax.random.split(jax.random.fold_in(key, 11), 2 * groups)
    source = jax.vmap(lambda one: jax.random.permutation(one, TOK_DEV))(keys[:groups]).astype(jnp.int32)
    source = source + (jnp.arange(groups, dtype=jnp.int32) * TOK_DEV)[:, None]
    target = source.reshape(groups, groups, block).transpose(1, 0, 2).reshape(groups, TOK_DEV)
    shuffle = jax.vmap(lambda one: jax.random.permutation(one, TOK_DEV))(keys[groups:]).astype(jnp.int32)
    dealt = jnp.take_along_axis(target, shuffle, axis=1)
    return dealt.reshape(-1)


def steps_of(key, shape, cuts, smallest, top_value):
    def one(axis_at, shards_of):
        steps = jax.random.uniform(jax.random.fold_in(jax.random.fold_in(key, 6), axis_at), (shards_of,), jnp.float32, smallest / len(cuts), top_value / len(cuts))
        return jnp.repeat(jnp.exp(steps), shape[axis_at] // shards_of).reshape((-1,) + (1,) * (len(shape) - axis_at - 1))

    factor_of = one(*cuts[0])
    for cut in cuts[1:]:
        factor_of = factor_of * one(*cut)
    return factor_of


def scatter_about(key, shape, spread, limit, cuts=(), kind=jnp.bfloat16):
    drawn = jax.random.normal(key, shape, jnp.float32) * spread
    if len(cuts) > 0:
        drawn = steps_of(key, shape, cuts, -0.22, 0.18) * drawn
    return jnp.clip(drawn, min=-limit, max=limit).astype(kind)


def setup_inputs(seed: int = 0) -> dict:
    key_of = jax.random.split(jax.random.key(seed), 12)
    return {
        "tokens": scatter_about(key_of[0], (TOKENS, D), 1.0, 6.0, ((0, 8), (1, 4))),
        "memory": scatter_about(key_of[1], (TOKENS, C), 1.0, 6.0, ((0, 8), (1, 4))),
        "dealing": draw_dealing(jax.random.fold_in(key_of[11], 71), 0),
        "cotangent": scatter_about(key_of[3], (TOKENS, D), 1.0, 6.0, ((0, 8), (1, 4))),
        "gain_first": jnp.clip(1.0 + 0.15 * jax.random.normal(key_of[4], (D,), jnp.float32), 0.25, 1.75),
        "gain_second": jnp.clip(1.0 + 0.15 * jax.random.normal(key_of[5], (D,), jnp.float32), 0.25, 1.75),
        "memory_gate": scatter_about(key_of[6], (D, C), D ** -0.5, 0.125, ((0, 8), (1, 4))),
        "memory_out": scatter_about(key_of[7], (C, D), C ** -0.5, 0.09375, ((0, 4), (1, 8))),
        "hidden_gate": scatter_about(key_of[8], (D, FF), D ** -0.5, 0.125, ((0, 8), (1, 4))),
        "hidden_up": scatter_about(key_of[9], (D, FF), D ** -0.5, 0.125, ((0, 8), (1, 4))),
        "hidden_down": scatter_about(key_of[10], (FF, D), FF ** -0.5, 0.0625, ((0, 4), (1, 8))),
    }


@jax.custom_vjp
def low(v):
    return lax.optimization_barrier(v.astype(jnp.bfloat16)).astype(jnp.float32)

@jax.custom_vjp
def low_back(v):
    return v

def low_keep(v):
    return (low(v), None)

def low_pass(kept, grad):
    return (grad,)

def back_keep(v):
    return (v, None)

def back_low(kept, grad):
    return (low(grad),)
low.defvjp(low_keep, low_pass)
low_back.defvjp(back_keep, back_low)
EPS = 1e-06

def normed(values, gain):
    return values * lax.rsqrt(lax.optimization_barrier(jnp.mean(values * values, axis=-1, keepdims=True)) + EPS) * gain

def matmul(left, right):
    return jnp.dot(left, right, precision=lax.Precision.HIGHEST, preferred_element_type=jnp.float32)

def layer(inputs, memory_tokens, gain_first, gain_second, memory_gate, memory_out, hidden_gate, hidden_up, hidden_down):
    first = low(normed(inputs, gain_first))
    gate_pre = low_back(matmul(first, memory_gate))
    mixed = low(memory_tokens * jax.nn.silu(gate_pre))
    middle = inputs + low_back(matmul(mixed, memory_out))
    second = low(normed(middle, gain_second))
    up_a = low_back(matmul(second, hidden_gate))
    up_b = low_back(matmul(second, hidden_up))
    swished = low(jax.nn.silu(up_a) * up_b)
    return middle + matmul(swished, hidden_down)

def reference(tokens, memory, dealing, cotangent, gain_first, gain_second, memory_gate, memory_out, hidden_gate, hidden_up, hidden_down):
    memory_f = memory.astype(jnp.float32)
    memory_tokens = jnp.zeros_like(memory_f).at[dealing].set(memory_f)
    primal = (tokens.astype(jnp.float32), memory_tokens, gain_first, gain_second, memory_gate.astype(jnp.float32), memory_out.astype(jnp.float32), hidden_gate.astype(jnp.float32), hidden_up.astype(jnp.float32), hidden_down.astype(jnp.float32))
    output, pullback = jax.vjp(layer, *primal)
    grads = pullback(cotangent.astype(jnp.float32))
    grad_memory = grads[1][dealing]
    return (output.astype(jnp.bfloat16), grads[0], grad_memory, grads[2], grads[3], grads[4], grads[5], grads[6], grads[7], grads[8])
```

```python
import jax
import jax.numpy as jnp
from jax import lax
from jax.sharding import PartitionSpec as P

EPS = 1e-06


def silu_grad(values):
    sigma = jax.nn.sigmoid(values)
    return sigma * (1.0 + values * (1.0 - sigma))


def normalize(values):
    inverse = lax.rsqrt(jnp.mean(values * values, axis=-1, keepdims=True) + EPS)
    return (values * inverse, inverse)


def contract_rows(left, right):
    return lax.dot_general(
        left, right, (((0,), (0,)), ((), ())), preferred_element_type=jnp.float32
    )


def contract_cols(left, right):
    return lax.dot_general(
        left, right, (((1,), (1,)), ((), ())), preferred_element_type=jnp.float32
    )


def sum_scatter(part):
    return lax.psum_scatter(
        part.astype(jnp.bfloat16), "tp", scatter_dimension=1, tiled=True
    ).astype(jnp.float32)


def mean_over(values, features):
    return lax.psum(jnp.sum(values, axis=-1, keepdims=True), "tp") / features


def grad_scatter(part, dimension):
    return lax.psum_scatter(
        part.astype(jnp.bfloat16), ("fsdp", "ctx"), scatter_dimension=dimension, tiled=True
    ).astype(jnp.float32)


def shards(
    tokens,
    memory,
    dealing,
    cotangent,
    gain_first,
    gain_second,
    memory_gate,
    memory_out,
    hidden_gate,
    hidden_up,
    hidden_down,
):
    groups = lax.axis_size(("fsdp", "ctx"))
    group_index = lax.axis_index(("fsdp", "ctx"))
    rows = dealing.shape[0]
    block = rows // groups
    order = jnp.argsort(dealing)
    sent_rows = memory[order].reshape(groups, block, memory.shape[1])
    arrived = lax.all_to_all(sent_rows, ("fsdp", "ctx"), split_axis=0, concat_axis=0, tiled=True)
    arrived_ids = lax.all_to_all(
        dealing[order].reshape(groups, block),
        ("fsdp", "ctx"),
        split_axis=0,
        concat_axis=0,
        tiled=True,
    )
    places = arrived_ids.reshape(rows) - group_index * rows
    memory_tokens = arrived.reshape(rows, memory.shape[1])[jnp.argsort(places)]
    memory_f = memory_tokens.astype(jnp.float32)
    gathered = (
        lax.all_gather(memory_gate, ("fsdp", "ctx"), axis=0, tiled=True),
        lax.all_gather(memory_out, ("fsdp", "ctx"), axis=1, tiled=True),
        lax.all_gather(hidden_gate, ("fsdp", "ctx"), axis=0, tiled=True),
        lax.all_gather(hidden_up, ("fsdp", "ctx"), axis=0, tiled=True),
        lax.all_gather(hidden_down, ("fsdp", "ctx"), axis=1, tiled=True),
    )
    gate_w, out_w, up_a_w, up_b_w, down_w = gathered
    width = tokens.shape[1]
    column = lax.axis_index("tp") * width
    full_tokens, full_cot = (
        lax.all_gather(tokens, "tp", axis=1, tiled=True),
        lax.all_gather(cotangent, "tp", axis=1, tiled=True),
    )
    inputs = full_tokens.astype(jnp.float32)
    unit_first, inv_first = normalize(inputs)
    first = (unit_first * gain_first).astype(jnp.bfloat16)
    gate_pre = jnp.dot(first, gate_w, preferred_element_type=jnp.float32)
    activated = jax.nn.silu(gate_pre)
    mixed = (memory_f * activated).astype(jnp.bfloat16)
    features = full_tokens.shape[1]
    own = lambda array: lax.dynamic_slice_in_dim(array, column, width, array.ndim - 1)
    gain_one, gain_two = own(gain_first), own(gain_second)
    shard_tokens = tokens.astype(jnp.float32)
    middle = shard_tokens + sum_scatter(jnp.dot(mixed, out_w, preferred_element_type=jnp.float32))
    inv_second = lax.rsqrt(mean_over(middle * middle, features) + EPS)
    unit_second = middle * inv_second
    second = lax.all_gather((unit_second * gain_two).astype(jnp.bfloat16), "tp", axis=1, tiled=True)
    up_a = jnp.dot(second, up_a_w, preferred_element_type=jnp.float32)
    up_b = jnp.dot(second, up_b_w, preferred_element_type=jnp.float32)
    swish_a = jax.nn.silu(up_a)
    swished = (swish_a * up_b).astype(jnp.bfloat16)
    output = middle + sum_scatter(jnp.dot(swished, down_w, preferred_element_type=jnp.float32))
    block_out = output.astype(jnp.bfloat16)
    d_swished = contract_cols(full_cot, down_w)
    grad_down = contract_rows(swished, full_cot)
    d_a = (d_swished * up_b * silu_grad(up_a)).astype(jnp.bfloat16)
    d_b = (d_swished * swish_a).astype(jnp.bfloat16)
    grad_up_a = contract_rows(second, d_a)
    grad_up_b = contract_rows(second, d_b)
    d_second = sum_scatter(contract_cols(d_a, up_a_w) + contract_cols(d_b, up_b_w))
    scaled = d_second * gain_two
    middle_norm = inv_second * (scaled - unit_second * mean_over(scaled * unit_second, features))
    gain_two_part = jnp.sum(d_second * unit_second, axis=0)
    d_middle = cotangent.astype(jnp.float32) + middle_norm
    d_branch = lax.all_gather(d_middle.astype(jnp.bfloat16), "tp", axis=1, tiled=True)
    d_mixed = contract_cols(d_branch, out_w)
    grad_out = contract_rows(mixed, d_branch)
    memory_term = d_mixed * activated
    d_gate = (d_mixed * memory_f * silu_grad(gate_pre)).astype(jnp.bfloat16)
    grad_gate = contract_rows(first, d_gate)
    d_first = sum_scatter(contract_cols(d_gate, gate_w))
    unit_own = shard_tokens * inv_first
    scaled = d_first * gain_one
    input_norm = inv_first * (scaled - unit_own * mean_over(scaled * unit_own, features))
    gain_one_part = jnp.sum(d_first * unit_own, axis=0)
    grad_inputs = d_middle + input_norm
    parts = lax.psum(jnp.stack([gain_one_part, gain_two_part]), ("fsdp", "ctx"))
    gains = lax.all_gather(parts, "tp", axis=1, tiled=True)
    grad_gain_first, grad_gain_second = gains[0], gains[1]
    back_rows = memory_term.astype(jnp.bfloat16)[places].reshape(groups, block, memory.shape[1])
    returned = lax.all_to_all(back_rows, ("fsdp", "ctx"), split_axis=0, concat_axis=0, tiled=True)
    grad_memory = returned.reshape(rows, memory.shape[1])[jnp.argsort(order)].astype(jnp.float32)
    sums = (
        grad_scatter(grad_gate, 0),
        grad_scatter(grad_out, 1),
        grad_scatter(grad_up_a, 0),
        grad_scatter(grad_up_b, 0),
        grad_scatter(grad_down, 1),
    )
    return (
        block_out,
        grad_inputs,
        grad_memory,
        grad_gain_first,
        grad_gain_second,
        sums[0],
        sums[1],
        sums[2],
        sums[3],
        sums[4],
    )


def solution(mesh):
    in_specs = (
        P(("fsdp", "ctx"), "tp"),
        P(("fsdp", "ctx"), "tp"),
        P(("fsdp", "ctx")),
        P(("fsdp", "ctx"), "tp"),
        P(),
        P(),
        P(("fsdp", "ctx"), "tp"),
        P("tp", ("fsdp", "ctx")),
        P(("fsdp", "ctx"), "tp"),
        P(("fsdp", "ctx"), "tp"),
        P("tp", ("fsdp", "ctx")),
    )
    out_specs = (
        P(("fsdp", "ctx"), "tp"),
        P(("fsdp", "ctx"), "tp"),
        P(("fsdp", "ctx"), "tp"),
        P(),
        P(),
        P(("fsdp", "ctx"), "tp"),
        P("tp", ("fsdp", "ctx")),
        P(("fsdp", "ctx"), "tp"),
        P(("fsdp", "ctx"), "tp"),
        P("tp", ("fsdp", "ctx")),
    )
    return jax.shard_map(shards, mesh=mesh, in_specs=in_specs, out_specs=out_specs, check_vma=False)
```

```python
import jax
import jax.numpy as jnp
from jax import lax
from jax.experimental import pallas as pl
from jax.experimental.pallas import tpu as pltpu
from jax.sharding import PartitionSpec as P

EPS = 1e-06
VMEM_LIMIT = 60 * 2**20


MESH = pl.DeviceIdType.MESH
JOBS = 8


def dot_nt(left, right):
    return lax.dot_general(left, right, (((1,), (1,)), ((), ())), preferred_element_type=jnp.float32)


def dot_tn(left, right):
    return lax.dot_general(left, right, (((0,), (0,)), ((), ())), preferred_element_type=jnp.float32)


class Place:
    def __init__(self):
        self.f, self.c, self.t = lax.axis_index("fsdp"), lax.axis_index("ctx"), lax.axis_index("tp")
        self.y, self.k = self.c // 2, self.c % 2

    def at(self, flip_f, flip_y, flip_k):
        f = self.f + flip_f * (1 - 2 * self.f)
        y = self.y + flip_y * (1 - 2 * self.y)
        k = self.k + flip_k * (1 - 2 * self.k)
        return f, y * 2 + k

    def sibling(self):
        return (*self.at(0, 0, 1), self.t)

    def first(self):
        return (*self.at(1 - self.k, self.k, 0), self.t)

    def second(self):
        return (*self.at(self.k, 1 - self.k, 0), self.t)

    def along(self, t):
        return (self.f, self.c, t)

    def owner(self, slot, flip_k):
        alpha, beta = 1 - slot // 2, 1 - slot % 2
        parity = self.k + flip_k * (1 - 2 * self.k)
        f, c = self.at(alpha * (1 - parity) + beta * parity, beta * (1 - parity) + alpha * parity, flip_k)
        return f * 4 + c


def remote(source, target, send, recv, device):
    return pltpu.make_async_remote_copy(
        src_ref=source, dst_ref=target, send_sem=send, recv_sem=recv, device_id=device, device_id_type=MESH
    )


def greet(place):
    barrier = pltpu.get_barrier_semaphore()
    for partner in (place.sibling(), place.first(), place.second()):
        pl.semaphore_signal(barrier, inc=1, device_id=partner, device_id_type=MESH)
    for step in range(1, 4):
        pl.semaphore_signal(barrier, inc=1, device_id=place.along((place.t + step) % 4), device_id_type=MESH)
    pl.semaphore_wait(barrier, 6)


class Gather:
    def __init__(self, place, full, send, recv, rows, width):
        self.place, self.full, self.send, self.recv, self.rows, self.width = place, full, send, recv, rows, width

    def copy(self, chunk, shard, way, hop):
        view = self.full.at[pl.ds(chunk * self.rows, self.rows), pl.ds(pl.multiple_of(shard * self.width, self.width), self.width)]
        device = self.place.along(self.place.t + 1 - 2 * way)
        return remote(view, view, self.send.at[chunk, way, hop], self.recv.at[chunk, shard], device)

    def step(self, chunk, hop):
        t = self.place.t

        @pl.when(t - hop >= 0)
        def _():
            if hop > 0:
                self.copy(chunk, t - hop, 0, hop).wait_recv()
            if hop < 3:
                @pl.when(t < 3)
                def _():
                    self.copy(chunk, t - hop, 0, hop).start()

        @pl.when(t + hop <= 3)
        def _():
            if hop > 0:
                self.copy(chunk, t + hop, 1, hop).wait_recv()
            if hop < 3:
                @pl.when(t > 0)
                def _():
                    self.copy(chunk, t + hop, 1, hop).start()

    def finish(self, chunk):
        t = self.place.t
        for hop in range(3):
            @pl.when((t - hop >= 0) & (t < 3))
            def _():
                self.copy(chunk, t - hop, 0, hop).wait_send()

            @pl.when((t + hop <= 3) & (t > 0))
            def _():
                self.copy(chunk, t + hop, 1, hop).wait_send()


class Scatter:
    def __init__(self, place, slots, send, recv):
        self.place, self.slots, self.send, self.recv = place, slots, send, recv

    def block(self, step):
        t = self.place.t
        low, high = t % 2, t // 2
        return (3 * (1 - high), 2 - 2 * low + high, 1 + low, t)[step]

    def copy(self, chunk, step):
        t, block = self.place.t, self.block(step)
        up = (block > t).astype(jnp.int32)
        last_down = (block == t - 1).astype(jnp.int32)
        slot = block + last_down * (4 - block)
        device = self.place.along(t - 1 + 2 * up)
        return remote(self.slots.at[chunk, block], self.slots.at[chunk, slot], self.send.at[chunk, step], self.recv.at[chunk, slot], device)

    def arrived(self, chunk, slot):
        view = self.slots.at[chunk, slot]
        remote(view, view, self.send.at[chunk, 0], self.recv.at[chunk, slot], self.place.along(self.place.t)).wait_recv()

    def step(self, chunk, step, part):
        t, block = self.place.t, self.block(step)
        inner = ((block > t) & (t > 0)) | ((block < t) & (t < 3))

        @pl.when(inner)
        def _():
            self.arrived(chunk, block)
            self.slots[chunk, block] = (part() + self.slots[chunk, block].astype(jnp.float32)).astype(jnp.bfloat16)

        @pl.when(jnp.logical_not(inner))
        def _():
            self.slots[chunk, block] = part().astype(jnp.bfloat16)

        self.copy(chunk, step).start()

    def own(self, chunk, held):
        t = self.place.t

        @pl.when(t > 0)
        def _():
            self.arrived(chunk, t)
            held[...] += self.slots[chunk, t].astype(jnp.float32)

        @pl.when(t < 3)
        def _():
            self.arrived(chunk, 4)
            held[...] += self.slots[chunk, 4].astype(jnp.float32)

    def finish(self, chunk):
        for step in range(3):
            self.copy(chunk, step).wait_send()


def to_row(column):
    return jnp.broadcast_to(column, (column.shape[0], 128)).T[:8]


def back_kernel(
    branch_own, cot_in, swi_in, h2_in, da_in, db_in, mixed_in, h1_in, gate_in, mem_in, out_w_in, gate_w_in, xhat_in, gain_ref, gg2_ref,
    dh1_out, term_out, hd_out, hg_out, hu_out, mo_out, mg_out, gains_out, stats_out,
    A1, A2, B1, B2, MX, DB, DG, WO, WG, SR, SS, H1S, H1R, H2S, H2R, OS, RZ, GP, MT, TS, XH, HO, GV, GR, GA, SV, SA,
    load_sem, gate_sem, ag_send, ag_recv, rs_send, rs_recv, sib_send, sib_recv, h1_send, h1_recv, h2_send, h2_recv,
    out_sem, small_send, small_recv, sib_free, first_free, second_free,
):
    place = Place()
    t = place.t
    chunk_rows, width = XH.shape
    slab = OS.shape[0]
    span = OS.shape[1]
    cols = span // 2
    chunks = 4

    loads = {}

    def load(name, source, target, slot):
        loads[name] = pltpu.make_async_copy(source, target, load_sem.at[slot])
        loads[name].start()

    def need(*names):
        for name in names:
            if name in loads:
                loads.pop(name).wait()

    own_columns = pl.ds(pl.multiple_of(t * width, width), width)
    load("branch", branch_own, DB.at[:, own_columns], 0)
    load("cot", cot_in, A1, 1)
    load("swi", swi_in, B1, 2)
    load("h2", h2_in, A2, 3)
    load("da", da_in, B2, 4)
    load("out_w", out_w_in, WO, 5)
    load("gate_w", gate_w_in, WG, 6)
    load("mixed", mixed_in, MX, 7)
    greet(place)

    gather = Gather(place, DB, ag_send, ag_recv, chunk_rows, width)
    scatter = Scatter(place, RZ, rs_send, rs_recv)
    need("branch")
    for chunk in range(chunks):
        gather.step(chunk, 0)

    jobs = [
        (A1, B1, 0, hd_out, 0), (A1, B1, span, hd_out, span), (A2, B2, 0, hg_out, 0), (A2, B2, span, hg_out, span),
        (A2, B1, 0, hu_out, 0), (A2, B1, span, hu_out, span), (DB, MX, 0, mo_out, 0), (A1, DG, 0, mg_out, 0),
    ]

    def tile(job, group, half):
        left, right, offset = jobs[job][:3]
        columns = pl.ds(pl.multiple_of(offset + half * cols, cols), cols)
        return dot_tn(left[:, pl.ds(pl.multiple_of(group * slab, slab), slab)], right[:, columns])

    def each_half(body):
        @pl.loop(0, 2)
        def _(half):
            body(half, pl.ds(pl.multiple_of(half * cols, cols), cols))

    def sib_copy(job, slot):
        return remote(SS.at[slot], SR.at[job % 2, slot], sib_send.at[slot], sib_recv.at[job, slot], place.sibling())

    def h1_copy(job, slot):
        return remote(H1S.at[job % 2, slot], H1R.at[job % 2, slot], h1_send.at[job % 2, slot], h1_recv.at[job, slot], place.first())

    def h2_copy(job):
        return remote(H2S.at[job % 2], H2R.at[job % 2], h2_send.at[job % 2], h2_recv.at[job], place.second())

    def to_sibling(job):
        if job >= 2:
            pl.semaphore_wait(sib_free, 1)

        @pl.loop(0, 4)
        def _(slot):
            if job >= 1:
                sib_copy(job - 1, slot).wait_send()
            group = place.owner(slot, 1)

            def body(half, at):
                SS[slot, :, at] = tile(job, group, half).astype(jnp.bfloat16)

            each_half(body)
            sib_copy(job, slot).start()

    def to_first(job):
        if job >= 2:
            pl.semaphore_wait(first_free, 1)

        @pl.loop(0, 2)
        def _(slot):
            if job >= 2:
                h1_copy(job - 2, slot).wait_send()
            group = place.owner(slot, 0)
            sib_copy(job, slot).wait_recv()

            def body(half, at):
                H1S[job % 2, slot, :, at] = (tile(job, group, half) + SR[job % 2, slot, :, at].astype(jnp.float32)).astype(jnp.bfloat16)

            each_half(body)
            h1_copy(job, slot).start()

    def to_second(job):
        if job >= 2:
            pl.semaphore_wait(second_free, 1)
            h2_copy(job - 2).wait_send()
        group = place.owner(2, 0)
        sib_copy(job, 2).wait_recv()
        h1_copy(job, 0).wait_recv()

        def body(half, at):
            H2S[job % 2, :, at] = (
                tile(job, group, half) + SR[job % 2, 2, :, at].astype(jnp.float32) + H1R[job % 2, 0, :, at].astype(jnp.float32)
            ).astype(jnp.bfloat16)

        each_half(body)
        h2_copy(job).start()

    def out_copy(job):
        return pltpu.make_async_copy(OS, jobs[job][3].at[:, pl.ds(jobs[job][4], span)], out_sem)

    def to_output(job):
        group = place.owner(3, 0)
        sib_copy(job, 3).wait_recv()
        h1_copy(job, 1).wait_recv()
        h2_copy(job).wait_recv()
        if job >= 1:
            out_copy(job - 1).wait()

        def body(half, at):
            OS[:, at] = (
                tile(job, group, half) + SR[job % 2, 3, :, at].astype(jnp.float32)
                + H1R[job % 2, 1, :, at].astype(jnp.float32) + H2R[job % 2, :, at].astype(jnp.float32)
            )

        each_half(body)
        out_copy(job).start()
        if job + 2 < JOBS:
            for free, device in ((sib_free, place.sibling()), (first_free, place.first()), (second_free, place.second())):
                pl.semaphore_signal(free, inc=1, device_id=device, device_id_type=MESH)

    def gate_loads(chunk):
        rows = pl.ds(chunk * chunk_rows, chunk_rows)
        return (
            pltpu.make_async_copy(gate_in.at[rows], GP, gate_sem.at[0]),
            pltpu.make_async_copy(mem_in.at[rows], MT, gate_sem.at[1]),
        )

    def term_store(chunk):
        return pltpu.make_async_copy(TS, term_out.at[pl.ds(chunk * chunk_rows, chunk_rows)], gate_sem.at[2])

    def channels(chunk):
        rows = pl.ds(chunk * chunk_rows, chunk_rows)
        for copy in gate_loads(chunk):
            copy.wait()
        if chunk > 0:
            term_store(chunk - 1).wait()

        def body(half, at):
            d_mixed = dot_nt(DB[rows, :], WO[at, :])
            pre = GP[:, at]
            sigma = jax.nn.sigmoid(pre)
            TS[:, at] = (d_mixed * (pre * sigma)).astype(jnp.bfloat16)
            DG[rows, at] = (d_mixed * MT[:, at].astype(jnp.float32) * (sigma * (1.0 + pre * (1.0 - sigma)))).astype(jnp.bfloat16)

        each_half(body)
        term_store(chunk).start()
        if chunk + 1 < chunks:
            for copy in gate_loads(chunk + 1):
                copy.start()

    def first_part(chunk, block):
        return dot_nt(DG[pl.ds(chunk * chunk_rows, chunk_rows), :], WG[pl.ds(pl.multiple_of(block * width, width), width), :])

    def first_step(chunk, step):
        scatter.step(chunk, step, lambda: first_part(chunk, scatter.block(step)))

    def own_copies(chunk):
        rows = pl.ds(chunk * chunk_rows, chunk_rows)
        return (
            pltpu.make_async_copy(xhat_in.at[rows], XH, gate_sem.at[3]),
            pltpu.make_async_copy(HO, dh1_out.at[rows], gate_sem.at[4]),
        )

    def own_step(chunk):
        load_xhat, store = own_copies(chunk)
        load_xhat.start()
        if chunk > 0:
            own_copies(chunk - 1)[1].wait()
        HO[...] = first_part(chunk, t)
        scatter.own(chunk, HO)
        load_xhat.wait()
        product = HO[...] * XH[...]
        if chunk == 0:
            GV[0, 0:1] = jnp.sum(product, axis=0, keepdims=True)
        else:
            GV[0, 0:1] += jnp.sum(product, axis=0, keepdims=True)
        SV[:, pl.ds(chunk * chunk_rows, chunk_rows)] = to_row(jnp.sum(product * gain_ref[...], axis=1, keepdims=True))
        store.start()

    def sum_copy(step):
        device = (place.sibling(), place.first(), place.second())[step]
        return remote(GV.at[step], GR.at[step], small_send.at[step], small_recv.at[step], device)

    def to_line(step, what):
        device = place.along((t + step) % 4)
        if what == 0:
            return remote(SV, SA.at[t], small_send.at[2 + step], small_recv.at[2 + step], device)
        return remote(GV.at[3], GA.at[t], small_send.at[5 + step], small_recv.at[5 + step], device)

    for copy in gate_loads(0):
        copy.start()

    def events(iteration):
        if iteration == 0:
            for chunk in range(2):
                gather.step(chunk, 1)
        if iteration == 1:
            for chunk in range(2, 4):
                gather.step(chunk, 1)
            for chunk in range(2):
                gather.step(chunk, 2)
        if iteration == 2:
            for chunk in range(2, 4):
                gather.step(chunk, 2)
            gather.step(0, 3)
            gather.step(1, 3)
        if iteration == 3:
            need("out_w", "gate_w")
            gather.step(2, 3)
            gather.step(3, 3)
            for chunk in range(4):
                channels(chunk)
                first_step(chunk, 0)
        if iteration == 4:
            for chunk in range(4):
                first_step(chunk, 1)
        if iteration == 5:
            for chunk in range(4):
                first_step(chunk, 2)
        if iteration == 6:
            for chunk in range(4):
                own_step(chunk)
            for step in range(1, 4):
                to_line(step, 0).start()
            GV[0, 1:2] = gg2_ref[...]
            sum_copy(0).start()
        if 7 <= iteration < 10:
            step = iteration - 7
            sum_copy(step).wait_recv()
            GV[step + 1] = GV[step] + GR[step]
            if step < 2:
                sum_copy(step + 1).start()
            else:
                for ahead in range(1, 4):
                    to_line(ahead, 1).start()

    GV[0] = jnp.zeros_like(GV[0])
    for iteration in range(JOBS + 2):
        if iteration >= 2:
            to_output(iteration - 2)
            if iteration == 3:
                load("db", db_in, B1, 2)
                load("h1", h1_in, A1, 1)
        if iteration < JOBS:
            need(*{0: ("cot", "swi"), 2: ("h2", "da"), 4: ("db",), 6: ("mixed",), 7: ("h1",)}.get(iteration, ()))
            to_sibling(iteration)
            to_first(iteration)
        if 1 <= iteration <= JOBS:
            to_second(iteration - 1)
        events(iteration)

    for step in range(1, 4):
        to_line(step, 0).wait()
        to_line(step, 1).wait()
    SA[t] = SV[...]
    GA[t] = GV[3]
    stats_out[...] = SA[0] + SA[1] + SA[2] + SA[3]
    gains_out[...] = GA[...]
    for chunk in range(4):
        gather.finish(chunk)
        scatter.finish(chunk)
    for step in range(3):
        sum_copy(step).wait_send()
    for slot in range(4):
        sib_copy(JOBS - 1, slot).wait_send()
    for job in (JOBS - 2, JOBS - 1):
        for slot in range(2):
            h1_copy(job, slot).wait_send()
        h2_copy(job).wait_send()
    term_store(3).wait()
    own_copies(3)[1].wait()
    out_copy(JOBS - 1).wait()


def back_call(branch_own, cot, swi, h2, da, db, mixed, h1, gate, mem, out_w, gate_w, xhat, gain, gg2):
    rows, features = cot.shape
    channels, hidden = mixed.shape[1], swi.shape[1]
    width, slab, part = features // 4, features // 8, rows // 4
    bf, f32 = jnp.bfloat16, jnp.float32
    shape = jax.ShapeDtypeStruct
    anywhere, vmem = pl.BlockSpec(memory_space=pl.ANY), pl.BlockSpec(memory_space=pltpu.VMEM)
    dma = pltpu.SemaphoreType.DMA
    regular = pltpu.SemaphoreType.REGULAR
    V = pltpu.VMEM
    macs = rows * features * (3 * hidden + 4 * channels)
    return pl.pallas_call(
        back_kernel,
        name="backward",
        out_shape=(
            shape((rows, width), f32), shape((rows, channels), bf), shape((slab, hidden), f32), shape((slab, hidden), f32),
            shape((slab, hidden), f32), shape((slab, channels), f32), shape((slab, channels), f32), shape((4, 8, width), f32),
            shape((8, rows), f32),
        ),
        in_specs=[anywhere] * 13 + [vmem] * 2,
        out_specs=(anywhere,) * 7 + (vmem,) * 2,
        scratch_shapes=[
            V((rows, features), bf), V((rows, features), bf), V((rows, hidden), bf), V((rows, hidden), bf), V((rows, channels), bf),
            V((rows, features), bf), V((rows, channels), bf), V((channels, features), bf), V((features, channels), bf),
            V((2, 4, slab, channels), bf), V((4, slab, channels), bf), V((2, 2, slab, channels), bf), V((2, 2, slab, channels), bf),
            V((2, slab, channels), bf), V((2, slab, channels), bf), V((slab, channels), f32), V((4, 5, part, width), bf),
            V((part, channels), f32), V((part, channels), bf), V((part, channels), bf), V((part, width), f32), V((part, width), f32),
            V((4, 8, width), f32), V((3, 8, width), f32), V((4, 8, width), f32), V((8, rows), f32), V((4, 8, rows), f32),
            dma((8,)), dma((5,)), dma((4, 2, 3)), dma((4, 4)), dma((4, 3)), dma((4, 5)), dma((4,)), dma((JOBS, 4)), dma((2, 2)),
            dma((JOBS, 2)), dma((2,)), dma((JOBS,)), dma, dma((9,)), dma((9,)), regular, regular, regular,
        ],
        compiler_params=pltpu.CompilerParams(collective_id=1, has_side_effects=True, vmem_limit_bytes=VMEM_LIMIT),
        cost_estimate=pl.CostEstimate(flops=2 * macs, bytes_accessed=64 * 2**20, transcendentals=rows * channels),
    )(branch_own, cot, swi, h2, da, db, mixed, h1, gate, mem, out_w, gate_w, xhat, gain, gg2)


def silu_grad(values):
    sigma = jax.nn.sigmoid(values)
    return sigma * (1.0 + values * (1.0 - sigma))


def normalize(values):
    inverse = lax.rsqrt(jnp.mean(values * values, axis=-1, keepdims=True) + EPS)
    return (values * inverse, inverse)


def contract_rows(left, right):
    return lax.dot_general(
        left, right, (((0,), (0,)), ((), ())), preferred_element_type=jnp.float32
    )


def contract_cols(left, right):
    return lax.dot_general(
        left, right, (((1,), (1,)), ((), ())), preferred_element_type=jnp.float32
    )


def sum_scatter(part):
    return lax.psum_scatter(
        part.astype(jnp.bfloat16), "tp", scatter_dimension=1, tiled=True
    ).astype(jnp.float32)


def mean_over(values, features):
    return lax.psum(jnp.sum(values, axis=-1, keepdims=True), "tp") / features


def grad_scatter(part, dimension):
    return lax.psum_scatter(
        part.astype(jnp.bfloat16), ("fsdp", "ctx"), scatter_dimension=dimension, tiled=True
    ).astype(jnp.float32)


def shards(
    tokens,
    memory,
    dealing,
    cotangent,
    gain_first,
    gain_second,
    memory_gate,
    memory_out,
    hidden_gate,
    hidden_up,
    hidden_down,
):
    groups = lax.axis_size(("fsdp", "ctx"))
    group_index = lax.axis_index(("fsdp", "ctx"))
    rows = dealing.shape[0]
    block = rows // groups
    order = jnp.argsort(dealing)
    sent_rows = memory[order].reshape(groups, block, memory.shape[1])
    arrived = lax.all_to_all(sent_rows, ("fsdp", "ctx"), split_axis=0, concat_axis=0, tiled=True)
    arrived_ids = lax.all_to_all(
        dealing[order].reshape(groups, block),
        ("fsdp", "ctx"),
        split_axis=0,
        concat_axis=0,
        tiled=True,
    )
    places = arrived_ids.reshape(rows) - group_index * rows
    memory_tokens = arrived.reshape(rows, memory.shape[1])[jnp.argsort(places)]
    memory_f = memory_tokens.astype(jnp.float32)
    gathered = (
        lax.all_gather(memory_gate, ("fsdp", "ctx"), axis=0, tiled=True),
        lax.all_gather(memory_out, ("fsdp", "ctx"), axis=1, tiled=True),
        lax.all_gather(hidden_gate, ("fsdp", "ctx"), axis=0, tiled=True),
        lax.all_gather(hidden_up, ("fsdp", "ctx"), axis=0, tiled=True),
        lax.all_gather(hidden_down, ("fsdp", "ctx"), axis=1, tiled=True),
    )
    gate_w, out_w, up_a_w, up_b_w, down_w = gathered
    width = tokens.shape[1]
    column = lax.axis_index("tp") * width
    full_tokens, full_cot = (
        lax.all_gather(tokens, "tp", axis=1, tiled=True),
        lax.all_gather(cotangent, "tp", axis=1, tiled=True),
    )
    inputs = full_tokens.astype(jnp.float32)
    unit_first, inv_first = normalize(inputs)
    first = (unit_first * gain_first).astype(jnp.bfloat16)
    gate_pre = jnp.dot(first, gate_w, preferred_element_type=jnp.float32)
    activated = jax.nn.silu(gate_pre)
    mixed = (memory_f * activated).astype(jnp.bfloat16)
    features = full_tokens.shape[1]
    own = lambda array: lax.dynamic_slice_in_dim(array, column, width, array.ndim - 1)
    gain_one, gain_two = own(gain_first), own(gain_second)
    shard_tokens = tokens.astype(jnp.float32)
    middle = shard_tokens + sum_scatter(jnp.dot(mixed, out_w, preferred_element_type=jnp.float32))
    inv_second = lax.rsqrt(mean_over(middle * middle, features) + EPS)
    unit_second = middle * inv_second
    second = lax.all_gather((unit_second * gain_two).astype(jnp.bfloat16), "tp", axis=1, tiled=True)
    up_a = jnp.dot(second, up_a_w, preferred_element_type=jnp.float32)
    up_b = jnp.dot(second, up_b_w, preferred_element_type=jnp.float32)
    swish_a = jax.nn.silu(up_a)
    swished = (swish_a * up_b).astype(jnp.bfloat16)
    output = middle + sum_scatter(jnp.dot(swished, down_w, preferred_element_type=jnp.float32))
    block_out = output.astype(jnp.bfloat16)
    d_swished = contract_cols(full_cot, down_w)
    d_a = (d_swished * up_b * silu_grad(up_a)).astype(jnp.bfloat16)
    d_b = (d_swished * swish_a).astype(jnp.bfloat16)
    d_second = sum_scatter(contract_cols(d_a, up_a_w) + contract_cols(d_b, up_b_w))
    scaled = d_second * gain_two
    middle_norm = inv_second * (scaled - unit_second * mean_over(scaled * unit_second, features))
    gain_two_part = jnp.sum(d_second * unit_second, axis=0)
    d_middle = cotangent.astype(jnp.float32) + middle_norm
    unit_own = shard_tokens * inv_first
    if lax.axis_size("fsdp") == 2 and lax.axis_size("ctx") == 4 and lax.axis_size("tp") == 4:
        (
            d_first, back, grad_down, grad_up_a, grad_up_b, grad_out, grad_gate, gains, stats,
        ) = back_call(
            d_middle.astype(jnp.bfloat16), full_cot, swished, second, d_a, d_b, mixed, first, gate_pre, memory_tokens,
            out_w, gate_w, unit_own, gain_one[None], gain_two_part[None],
        )
        input_norm = inv_first * (d_first * gain_one - unit_own * (stats[0][:, None] / features))
        grad_gain_first, grad_gain_second = gains[:, 0].reshape(features), gains[:, 1].reshape(features)
        sums = (grad_gate, grad_out.T, grad_up_a, grad_up_b, grad_down.T)
    else:
        d_branch = lax.all_gather(d_middle.astype(jnp.bfloat16), "tp", axis=1, tiled=True)
        d_mixed = contract_cols(d_branch, out_w)
        back = (d_mixed * activated).astype(jnp.bfloat16)
        d_gate = (d_mixed * memory_f * silu_grad(gate_pre)).astype(jnp.bfloat16)
        d_first = sum_scatter(contract_cols(d_gate, gate_w))
        scaled = d_first * gain_one
        input_norm = inv_first * (scaled - unit_own * mean_over(scaled * unit_own, features))
        gain_one_part = jnp.sum(d_first * unit_own, axis=0)
        parts = lax.psum(jnp.stack([gain_one_part, gain_two_part]), ("fsdp", "ctx"))
        gains = lax.all_gather(parts, "tp", axis=1, tiled=True)
        grad_gain_first, grad_gain_second = gains[0], gains[1]
        sums = (
            grad_scatter(contract_rows(first, d_gate), 0),
            grad_scatter(contract_rows(mixed, d_branch), 1),
            grad_scatter(contract_rows(second, d_a), 0),
            grad_scatter(contract_rows(second, d_b), 0),
            grad_scatter(contract_rows(swished, full_cot), 1),
        )
    grad_inputs = d_middle + input_norm
    back_rows = back[places].reshape(groups, block, memory.shape[1])
    returned = lax.all_to_all(back_rows, ("fsdp", "ctx"), split_axis=0, concat_axis=0, tiled=True)
    grad_memory = returned.reshape(rows, memory.shape[1])[jnp.argsort(order)].astype(jnp.float32)
    return (
        block_out,
        grad_inputs,
        grad_memory,
        grad_gain_first,
        grad_gain_second,
        sums[0],
        sums[1],
        sums[2],
        sums[3],
        sums[4],
    )


def solution(mesh):
    in_specs = (
        P(("fsdp", "ctx"), "tp"),
        P(("fsdp", "ctx"), "tp"),
        P(("fsdp", "ctx")),
        P(("fsdp", "ctx"), "tp"),
        P(),
        P(),
        P(("fsdp", "ctx"), "tp"),
        P("tp", ("fsdp", "ctx")),
        P(("fsdp", "ctx"), "tp"),
        P(("fsdp", "ctx"), "tp"),
        P("tp", ("fsdp", "ctx")),
    )
    out_specs = (
        P(("fsdp", "ctx"), "tp"),
        P(("fsdp", "ctx"), "tp"),
        P(("fsdp", "ctx"), "tp"),
        P(),
        P(),
        P(("fsdp", "ctx"), "tp"),
        P("tp", ("fsdp", "ctx")),
        P(("fsdp", "ctx"), "tp"),
        P(("fsdp", "ctx"), "tp"),
        P("tp", ("fsdp", "ctx")),
    )
    return jax.shard_map(shards, mesh=mesh, in_specs=in_specs, out_specs=out_specs, check_vma=False)
```

```python
import jax
import jax.numpy as jnp
from jax import lax
from jax.experimental import pallas as pl
from jax.experimental.pallas import tpu as pltpu
from jax.sharding import PartitionSpec as P

EPS = 1e-06
VMEM_LIMIT = 62 * 2**20


MESH = pl.DeviceIdType.MESH
JOBS = 8


def dot_nt(left, right):
    return lax.dot_general(left, right, (((1,), (1,)), ((), ())), preferred_element_type=jnp.float32)


def dot_tn(left, right):
    return lax.dot_general(left, right, (((0,), (0,)), ((), ())), preferred_element_type=jnp.float32)


class Place:
    def __init__(self):
        self.f, self.c, self.t = lax.axis_index("fsdp"), lax.axis_index("ctx"), lax.axis_index("tp")
        self.y, self.k = self.c // 2, self.c % 2

    def at(self, flip_f, flip_y, flip_k):
        f = self.f + flip_f * (1 - 2 * self.f)
        y = self.y + flip_y * (1 - 2 * self.y)
        k = self.k + flip_k * (1 - 2 * self.k)
        return f, y * 2 + k

    def sibling(self):
        return (*self.at(0, 0, 1), self.t)

    def first(self):
        return (*self.at(1 - self.k, self.k, 0), self.t)

    def second(self):
        return (*self.at(self.k, 1 - self.k, 0), self.t)

    def along(self, t):
        return (self.f, self.c, t)

    def owner(self, slot, flip_k):
        alpha, beta = 1 - slot // 2, 1 - slot % 2
        parity = self.k + flip_k * (1 - 2 * self.k)
        f, c = self.at(alpha * (1 - parity) + beta * parity, beta * (1 - parity) + alpha * parity, flip_k)
        return f * 4 + c


def remote(source, target, send, recv, device):
    return pltpu.make_async_remote_copy(
        src_ref=source, dst_ref=target, send_sem=send, recv_sem=recv, device_id=device, device_id_type=MESH
    )


def greet(place):
    barrier = pltpu.get_barrier_semaphore()
    for partner in (place.sibling(), place.first(), place.second()):
        pl.semaphore_signal(barrier, inc=1, device_id=partner, device_id_type=MESH)
    for step in range(1, 4):
        pl.semaphore_signal(barrier, inc=1, device_id=place.along((place.t + step) % 4), device_id_type=MESH)
    pl.semaphore_wait(barrier, 6)


class Gather:
    def __init__(self, place, full, send, recv, rows, width, own=None):
        self.place, self.full, self.send, self.recv, self.rows, self.width, self.mine = place, full, send, recv, rows, width, own

    def copy(self, chunk, shard, way, hop):
        view = self.full.at[pl.ds(chunk * self.rows, self.rows), pl.ds(pl.multiple_of(shard * self.width, self.width), self.width)]
        device = self.place.along(self.place.t + 1 - 2 * way)
        source = view if hop > 0 or self.mine is None else self.mine.at[pl.ds(chunk * self.rows, self.rows)]
        return remote(source, view, self.send.at[chunk, way, hop], self.recv.at[chunk, shard], device)

    def step(self, chunk, hop):
        t = self.place.t

        @pl.when(t - hop >= 0)
        def _():
            if hop > 0:
                self.copy(chunk, t - hop, 0, hop).wait_recv()
            if hop < 3:
                @pl.when(t < 3)
                def _():
                    self.copy(chunk, t - hop, 0, hop).start()

        @pl.when(t + hop <= 3)
        def _():
            if hop > 0:
                self.copy(chunk, t + hop, 1, hop).wait_recv()
            if hop < 3:
                @pl.when(t > 0)
                def _():
                    self.copy(chunk, t + hop, 1, hop).start()

    def finish(self, chunk):
        t = self.place.t
        for hop in range(3):
            @pl.when((t - hop >= 0) & (t < 3))
            def _():
                self.copy(chunk, t - hop, 0, hop).wait_send()

            @pl.when((t + hop <= 3) & (t > 0))
            def _():
                self.copy(chunk, t + hop, 1, hop).wait_send()


class Scatter:
    def __init__(self, place, slots, send, recv):
        self.place, self.slots, self.send, self.recv = place, slots, send, recv
        self.ring = slots.shape[0]

    def block(self, step):
        t = self.place.t
        low, high = t % 2, t // 2
        return (3 * (1 - high), 2 - 2 * low + high, 1 + low, t)[step]

    def copy(self, chunk, step):
        t, block, ring = self.place.t, self.block(step), chunk % self.ring
        up = (block > t).astype(jnp.int32)
        last_down = (block == t - 1).astype(jnp.int32)
        slot = block + last_down * (4 - block)
        device = self.place.along(t - 1 + 2 * up)
        return remote(self.slots.at[ring, block], self.slots.at[ring, slot], self.send.at[chunk, step], self.recv.at[chunk, slot], device)

    def arrived(self, chunk, slot):
        view = self.slots.at[chunk % self.ring, slot]
        remote(view, view, self.send.at[chunk, 0], self.recv.at[chunk, slot], self.place.along(self.place.t)).wait_recv()

    def step(self, chunk, step, part, inside):
        block, ring = self.block(step), chunk % self.ring
        value = part(block)
        if inside:
            self.arrived(chunk, block)
            value += self.slots[ring, block].astype(jnp.float32)
        self.slots[ring, block] = value.astype(jnp.bfloat16)
        self.copy(chunk, step).start()

    def own(self, chunk, held):
        t, ring = self.place.t, chunk % self.ring

        @pl.when(t > 0)
        def _():
            self.arrived(chunk, t)
            held[...] += self.slots[ring, t].astype(jnp.float32)

        @pl.when(t < 3)
        def _():
            self.arrived(chunk, 4)
            held[...] += self.slots[ring, 4].astype(jnp.float32)

    def finish(self, chunk):
        for step in range(3):
            self.copy(chunk, step).wait_send()


def by_place(place, ends, inside):
    is_end = (place.t == 0) | (place.t == 3)
    pl.when(is_end)(ends)
    pl.when(jnp.logical_not(is_end))(inside)


def to_row(column):
    return jnp.broadcast_to(column, (column.shape[0], 128)).T[:8]


def back_kernel(
    branch_own, cot_in, swi_in, h2_in, da_in, db_in, mixed_in, h1_in, gate_in, mem_in, out_w_in, gate_w_in, xhat_in, gain_ref, gg2_ref,
    dh1_out, term_out, hd_out, hg_out, hu_out, mo_out, mg_out, gains_out, stats_out,
    A1, A2, B1, B2, MX, DB, DG, WO, WG, SR, SS, H1S, H1R, H2S, H2R, OS, RZ, GP, MT, TS, XH, HO, GV, GR, GA, SV, SA,
    load_sem, gate_sem, ag_send, ag_recv, rs_send, rs_recv, sib_send, sib_recv, h1_send, h1_recv, h2_send, h2_recv,
    out_sem, small_send, small_recv, sib_free, first_free, second_free,
):
    place = Place()
    t = place.t
    chunk_rows, width = XH.shape
    slab = OS.shape[0]
    span = OS.shape[1]
    cols = span // 2
    chunks = 4

    loads = {}

    def load(name, source, target, slot):
        loads[name] = pltpu.make_async_copy(source, target, load_sem.at[slot])
        loads[name].start()

    def need(*names):
        for name in names:
            if name in loads:
                loads.pop(name).wait()

    own_columns = pl.ds(pl.multiple_of(t * width, width), width)
    load("branch", branch_own, DB.at[:, own_columns], 0)
    load("cot", cot_in, A1, 1)
    load("swi", swi_in, B1, 2)
    load("h2", h2_in, A2, 3)
    load("da", da_in, B2, 4)
    load("out_w", out_w_in, WO, 5)
    load("gate_w", gate_w_in, WG, 6)
    load("mixed", mixed_in, MX, 7)
    greet(place)

    gather = Gather(place, DB, ag_send, ag_recv, chunk_rows, width)
    scatter = Scatter(place, RZ, rs_send, rs_recv)
    need("branch")
    for chunk in range(chunks):
        gather.step(chunk, 0)

    jobs = [
        (A1, B1, 0, hd_out, 0), (A1, B1, span, hd_out, span), (A2, B2, 0, hg_out, 0), (A2, B2, span, hg_out, span),
        (A2, B1, 0, hu_out, 0), (A2, B1, span, hu_out, span), (DB, MX, 0, mo_out, 0), (A1, DG, 0, mg_out, 0),
    ]

    def tile(job, group, half):
        left, right, offset = jobs[job][:3]
        columns = pl.ds(pl.multiple_of(offset + half * cols, cols), cols)
        return dot_tn(left[:, pl.ds(pl.multiple_of(group * slab, slab), slab)], right[:, columns])

    def each_half(body):
        @pl.loop(0, 2)
        def _(half):
            body(half, pl.ds(pl.multiple_of(half * cols, cols), cols))

    def sib_copy(job, slot):
        return remote(SS.at[slot], SR.at[job % 3, slot], sib_send.at[slot], sib_recv.at[job, slot], place.sibling())

    def h1_copy(job, slot):
        return remote(H1S.at[job % 2, slot], H1R.at[job % 3, slot], h1_send.at[job % 2, slot], h1_recv.at[job, slot], place.first())

    def h2_copy(job):
        return remote(H2S.at[job % 2], H2R.at[job % 2], h2_send.at[job % 2], h2_recv.at[job], place.second())

    def to_sibling(job):
        if job >= 3:
            pl.semaphore_wait(sib_free, 1)

        @pl.loop(0, 4)
        def _(slot):
            if job >= 1:
                sib_copy(job - 1, slot).wait_send()
            group = place.owner(slot, 1)

            def body(half, at):
                SS[slot, :, at] = tile(job, group, half).astype(jnp.bfloat16)

            each_half(body)
            sib_copy(job, slot).start()

    def to_first(job):
        if job >= 3:
            pl.semaphore_wait(first_free, 1)

        @pl.loop(0, 2)
        def _(slot):
            if job >= 2:
                h1_copy(job - 2, slot).wait_send()
            group = place.owner(slot, 0)
            sib_copy(job, slot).wait_recv()

            def body(half, at):
                H1S[job % 2, slot, :, at] = (tile(job, group, half) + SR[job % 3, slot, :, at].astype(jnp.float32)).astype(jnp.bfloat16)

            each_half(body)
            h1_copy(job, slot).start()

    def to_second(job):
        if job >= 2:
            pl.semaphore_wait(second_free, 1)
            h2_copy(job - 2).wait_send()
        group = place.owner(2, 0)
        sib_copy(job, 2).wait_recv()
        h1_copy(job, 0).wait_recv()

        def body(half, at):
            H2S[job % 2, :, at] = (
                tile(job, group, half) + SR[job % 3, 2, :, at].astype(jnp.float32) + H1R[job % 3, 0, :, at].astype(jnp.float32)
            ).astype(jnp.bfloat16)

        each_half(body)
        h2_copy(job).start()

    def out_copy(job):
        return pltpu.make_async_copy(OS, jobs[job][3].at[:, pl.ds(jobs[job][4], span)], out_sem)

    def to_output(job):
        group = place.owner(3, 0)
        sib_copy(job, 3).wait_recv()
        h1_copy(job, 1).wait_recv()
        h2_copy(job).wait_recv()
        if job >= 1:
            out_copy(job - 1).wait()

        def body(half, at):
            OS[:, at] = (
                tile(job, group, half) + SR[job % 3, 3, :, at].astype(jnp.float32)
                + H1R[job % 3, 1, :, at].astype(jnp.float32) + H2R[job % 2, :, at].astype(jnp.float32)
            )

        each_half(body)
        out_copy(job).start()
        for ahead, free, device in ((3, sib_free, place.sibling()), (3, first_free, place.first()), (2, second_free, place.second())):
            if job + ahead < JOBS:
                pl.semaphore_signal(free, inc=1, device_id=device, device_id_type=MESH)

    def gate_loads(chunk):
        rows = pl.ds(chunk * chunk_rows, chunk_rows)
        return (
            pltpu.make_async_copy(gate_in.at[rows], GP, gate_sem.at[0]),
            pltpu.make_async_copy(mem_in.at[rows], MT, gate_sem.at[1]),
        )

    def term_store(chunk):
        return pltpu.make_async_copy(TS, term_out.at[pl.ds(chunk * chunk_rows, chunk_rows)], gate_sem.at[2])

    def channels(chunk):
        rows = pl.ds(chunk * chunk_rows, chunk_rows)
        for copy in gate_loads(chunk):
            copy.wait()
        if chunk > 0:
            term_store(chunk - 1).wait()

        def body(half, at):
            d_mixed = dot_nt(DB[rows, :], WO[at, :])
            pre = GP[:, at]
            sigma = jax.nn.sigmoid(pre)
            TS[:, at] = (d_mixed * (pre * sigma)).astype(jnp.bfloat16)
            DG[rows, at] = (d_mixed * MT[:, at].astype(jnp.float32) * (sigma * (1.0 + pre * (1.0 - sigma)))).astype(jnp.bfloat16)

        each_half(body)
        term_store(chunk).start()
        if chunk + 1 < chunks:
            for copy in gate_loads(chunk + 1):
                copy.start()

    def first_part(chunk, block):
        return dot_nt(DG[pl.ds(chunk * chunk_rows, chunk_rows), :], WG[pl.ds(pl.multiple_of(block * width, width), width), :])

    def first_step(chunk, step, inside):
        scatter.step(chunk, step, lambda block: first_part(chunk, block), inside)

    def own_copies(chunk):
        rows = pl.ds(chunk * chunk_rows, chunk_rows)
        return (
            pltpu.make_async_copy(xhat_in.at[rows], XH, gate_sem.at[3]),
            pltpu.make_async_copy(HO, dh1_out.at[rows], gate_sem.at[4]),
        )

    def own_step(chunk):
        load_xhat, store = own_copies(chunk)
        load_xhat.start()
        if chunk > 0:
            own_copies(chunk - 1)[1].wait()
        HO[...] = first_part(chunk, t)
        scatter.own(chunk, HO)
        load_xhat.wait()
        product = HO[...] * XH[...]
        if chunk == 0:
            GV[0, 0:1] = jnp.sum(product, axis=0, keepdims=True)
        else:
            GV[0, 0:1] += jnp.sum(product, axis=0, keepdims=True)
        SV[:, pl.ds(chunk * chunk_rows, chunk_rows)] = to_row(jnp.sum(product * gain_ref[...], axis=1, keepdims=True))
        store.start()

    def sum_copy(step):
        device = (place.sibling(), place.first(), place.second())[step]
        return remote(GV.at[step], GR.at[step], small_send.at[step], small_recv.at[step], device)

    def to_line(step, what):
        device = place.along((t + step) % 4)
        if what == 0:
            return remote(SV, SA.at[t], small_send.at[2 + step], small_recv.at[2 + step], device)
        return remote(GV.at[3], GA.at[t], small_send.at[5 + step], small_recv.at[5 + step], device)

    for copy in gate_loads(0):
        copy.start()

    def steps(ends, inside):
        def run(pairs, inner):
            for chunk, step in pairs:
                first_step(chunk, step, inner)

        by_place(place, lambda: run(ends, False), lambda: run(inside, True))

    def events(iteration, late):
        if (iteration, late) == (1, 0):
            gather.step(0, 1)
            gather.step(1, 1)
        if (iteration, late) == (1, 1):
            gather.step(2, 1)
            gather.step(3, 1)
        if (iteration, late) == (2, 1):
            gather.step(0, 2)
            gather.step(1, 2)
        if (iteration, late) == (3, 0):
            gather.step(2, 2)
            gather.step(3, 2)
            need("out_w", "gate_w")
            gather.step(0, 3)
            channels(0)
        if (iteration, late) == (3, 1):
            gather.step(1, 3)
            channels(1)
            steps([(0, 0), (1, 0)], [])
        if (iteration, late) == (4, 0):
            gather.step(2, 3)
            channels(2)
        if (iteration, late) == (4, 1):
            gather.step(3, 3)
            channels(3)
            steps([(2, 0), (3, 0)], [(0, 0), (1, 0)])
        if (iteration, late) == (5, 0):
            steps([(0, 1), (1, 1)], [(2, 0), (3, 0)])
        if (iteration, late) == (5, 1):
            steps([(2, 1), (3, 1)], [(0, 1), (1, 1)])
        if (iteration, late) == (6, 0):
            steps([(0, 2), (1, 2)], [(2, 1), (3, 1), (0, 2), (1, 2)])
        if (iteration, late) == (6, 1):
            steps([(2, 2), (3, 2)], [(2, 2), (3, 2)])
        if (iteration, late) == (7, 0):
            own_step(0)
            own_step(1)
        if (iteration, late) == (7, 1):
            own_step(2)
            own_step(3)
            for step in range(1, 4):
                to_line(step, 0).start()
            GV[0, 1:2] = gg2_ref[...]
            sum_copy(0).start()
        if late and 8 <= iteration < 11:
            step = iteration - 8
            sum_copy(step).wait_recv()
            GV[step + 1] = GV[step] + GR[step]
            if step < 2:
                sum_copy(step + 1).start()
            else:
                for ahead in range(1, 4):
                    to_line(ahead, 1).start()

    GV[0] = jnp.zeros_like(GV[0])
    for iteration in range(JOBS + 2):
        if iteration < JOBS:
            need(*{0: ("cot", "swi"), 2: ("h2", "da"), 4: ("db",), 6: ("mixed",), 7: ("h1",)}.get(iteration, ()))
            to_sibling(iteration)
            to_first(iteration)
        events(iteration, 0)
        if 1 <= iteration <= JOBS:
            to_second(iteration - 1)
        if iteration >= 2:
            to_output(iteration - 2)
            if iteration == 3:
                load("db", db_in, B1, 2)
                load("h1", h1_in, A1, 1)
        events(iteration, 1)
    events(10, 1)

    for step in range(1, 4):
        to_line(step, 0).wait()
        to_line(step, 1).wait()
    SA[t] = SV[...]
    GA[t] = GV[3]
    stats_out[...] = SA[0] + SA[1] + SA[2] + SA[3]
    gains_out[...] = GA[...]
    for chunk in range(4):
        gather.finish(chunk)
        scatter.finish(chunk)
    for step in range(3):
        sum_copy(step).wait_send()
    for slot in range(4):
        sib_copy(JOBS - 1, slot).wait_send()
    for job in (JOBS - 2, JOBS - 1):
        for slot in range(2):
            h1_copy(job, slot).wait_send()
        h2_copy(job).wait_send()
    term_store(3).wait()
    own_copies(3)[1].wait()
    out_copy(JOBS - 1).wait()


def back_call(branch_own, cot, swi, h2, da, db, mixed, h1, gate, mem, out_w, gate_w, xhat, gain, gg2):
    rows, features = cot.shape
    channels, hidden = mixed.shape[1], swi.shape[1]
    width, slab, part = features // 4, features // 8, rows // 4
    bf, f32 = jnp.bfloat16, jnp.float32
    shape = jax.ShapeDtypeStruct
    anywhere, vmem = pl.BlockSpec(memory_space=pl.ANY), pl.BlockSpec(memory_space=pltpu.VMEM)
    dma = pltpu.SemaphoreType.DMA
    regular = pltpu.SemaphoreType.REGULAR
    V = pltpu.VMEM
    macs = rows * features * (3 * hidden + 4 * channels)
    return pl.pallas_call(
        back_kernel,
        name="backward",
        out_shape=(
            shape((rows, width), f32), shape((rows, channels), bf), shape((slab, hidden), f32), shape((slab, hidden), f32),
            shape((slab, hidden), f32), shape((slab, channels), f32), shape((slab, channels), f32), shape((4, 8, width), f32),
            shape((8, rows), f32),
        ),
        in_specs=[anywhere] * 13 + [vmem] * 2,
        out_specs=(anywhere,) * 7 + (vmem,) * 2,
        scratch_shapes=[
            V((rows, features), bf), V((rows, features), bf), V((rows, hidden), bf), V((rows, hidden), bf), V((rows, channels), bf),
            V((rows, features), bf), V((rows, channels), bf), V((channels, features), bf), V((features, channels), bf),
            V((3, 4, slab, channels), bf), V((4, slab, channels), bf), V((2, 2, slab, channels), bf), V((3, 2, slab, channels), bf),
            V((2, slab, channels), bf), V((2, slab, channels), bf), V((slab, channels), f32), V((4, 5, part, width), bf),
            V((part, channels), f32), V((part, channels), bf), V((part, channels), bf), V((part, width), f32), V((part, width), f32),
            V((4, 8, width), f32), V((3, 8, width), f32), V((4, 8, width), f32), V((8, rows), f32), V((4, 8, rows), f32),
            dma((8,)), dma((5,)), dma((4, 2, 3)), dma((4, 4)), dma((4, 3)), dma((4, 5)), dma((4,)), dma((JOBS, 4)), dma((2, 2)),
            dma((JOBS, 2)), dma((2,)), dma((JOBS,)), dma, dma((9,)), dma((9,)), regular, regular, regular,
        ],
        compiler_params=pltpu.CompilerParams(collective_id=1, has_side_effects=True, vmem_limit_bytes=VMEM_LIMIT),
        cost_estimate=pl.CostEstimate(flops=2 * macs, bytes_accessed=64 * 2**20, transcendentals=rows * channels),
    )(branch_own, cot, swi, h2, da, db, mixed, h1, gate, mem, out_w, gate_w, xhat, gain, gg2)


class Spread:
    def __init__(self, place, index, shard, view, send, recv, local):
        self.place, self.index, self.shard, self.view, self.send, self.recv = place, index, shard, view, send, recv
        self.local = local

    def group(self, *flips):
        f, c = self.place.at(*flips)
        return f * 4 + c

    def copy(self, group, device, slot):
        view = self.view(group)
        source = self.shard if slot < 3 else view
        return remote(source, view, self.send.at[self.index, slot], self.recv.at[self.index, group], device)

    def routes(self):
        place = self.place
        me, both = self.group(0, 0, 0), self.group(1, 1, 0)
        first, second = self.group(1 - place.k, place.k, 0), self.group(place.k, 1 - place.k, 0)
        return (
            (me, place.first()), (me, place.second()), (me, place.sibling()), (second, place.first()), (first, place.sibling()),
            (second, place.sibling()), (both, place.sibling()),
        )

    def start(self, slot):
        group, device = self.routes()[slot]
        self.copy(group, device, slot).start()

    def arrived(self, group):
        self.copy(group, self.place.sibling(), 3).wait_recv()

    def stay(self):
        return pltpu.make_async_copy(self.shard, self.view(self.group(0, 0, 0)), self.local.at[self.index])

    def phase(self, number):
        routes = self.routes()
        if number == 0:
            for slot in range(3):
                self.start(slot)
            self.stay().start()
        if number == 1:
            self.arrived(routes[3][0])
            self.start(3)
            self.start(5)
            self.arrived(routes[4][0])
            self.start(4)
        if number == 2:
            self.arrived(routes[6][0])
            self.start(6)
        if number == 3:
            for flips in ((0, 0), (0, 1), (1, 0), (1, 1)):
                self.arrived(self.group(*flips, 1))
            self.stay().wait()

    def finish(self):
        for slot, (group, device) in enumerate(self.routes()):
            self.copy(group, device, slot).wait_send()


def to_column(row):
    return jnp.broadcast_to(row, (128, row.shape[1])).T[:, 0:1]


def front_kernel(
    tokens, cotangent, mem_in, gate_w, out_w, up_a_w, up_b_w, down_w, gain1, gain2,
    tok_full, cot_full, h2_full, h1_out, gate_out, mixed_out, swi_out, da_out, db_out, gate_w_out, out_w_out, block_out, dx1_out, branch_out,
    inv_out, gg2_out,
    WG, WO, WA, WB, WD, Z1, ZN, ZE, XC, CC, H1C, GPS, MXS, MT, SWI, DA, DB, X1, H2O, HO, DHQ, FS, BS, OWN, I2, SV, SA, SV2, SA2,
    load_sem, store_sem, stage_sem, t_send, t_recv, c_send, c_recv, h_send, h_recv, r_send, r_recv, n_send, n_recv, e_send, e_recv,
    w_send, w_recv, w_local, s_send, s_recv,
):
    place = Place()
    t = place.t
    rows, features = tok_full.shape
    chunk_rows, width = HO.shape
    channels, hidden = MXS.shape[2], SWI.shape[2]
    half = channels // 2
    slab = features // 8
    own_columns = pl.ds(pl.multiple_of(t * width, width), width)

    def rows_of(chunk):
        return pl.ds(chunk * chunk_rows, chunk_rows)

    def columns_of(block, size):
        return pl.ds(pl.multiple_of(block * size, size), size)

    def keep(index, source, target):
        return pltpu.make_async_copy(source, target, stage_sem.at[index])

    own_tokens = keep(0, tokens, tok_full.at[:, own_columns])
    own_cot = keep(1, cotangent, cot_full.at[:, own_columns])
    own_tokens.start()
    own_cot.start()
    greet(place)

    tok_gather = Gather(place, tok_full, t_send, t_recv, chunk_rows, width, tokens)
    cot_gather = Gather(place, cot_full, c_send, c_recv, chunk_rows, width, cotangent)
    h2_gather = Gather(place, h2_full, h_send, h_recv, chunk_rows, width, H2O)
    mix_scatter = Scatter(place, Z1, r_send, r_recv)
    down_scatter = Scatter(place, ZN, n_send, n_recv)
    up_scatter = Scatter(place, ZE, e_send, e_recv)
    spreads = [
        Spread(place, index, shard, view, w_send, w_recv, w_local)
        for index, (shard, view) in enumerate((
            (gate_w, lambda group: WG.at[columns_of(group, slab), :]),
            (out_w, lambda group: WO.at[:, columns_of(group, slab)]),
            (up_a_w, lambda group: WA.at[columns_of(group, slab), :]),
            (up_b_w, lambda group: WB.at[columns_of(group, slab), :]),
            (down_w, lambda group: WD.at[:, columns_of(group, slab)]),
        ))
    ]

    def mem_load(chunk):
        return pltpu.make_async_copy(mem_in.at[rows_of(chunk)], MT, load_sem.at[0])

    def h1_store(chunk):
        return pltpu.make_async_copy(H1C, h1_out.at[rows_of(chunk)], store_sem.at[0])

    def gate_store(chunk):
        return pltpu.make_async_copy(GPS, gate_out.at[rows_of(chunk)], store_sem.at[1])

    def mixed_store(chunk):
        return pltpu.make_async_copy(MXS.at[chunk % 2], mixed_out.at[rows_of(chunk)], store_sem.at[2 + chunk % 2])

    def hidden_stores(chunk):
        slot = chunk % 2
        return [
            pltpu.make_async_copy(source.at[slot], target.at[rows_of(chunk)], store_sem.at[4 + 2 * index + slot])
            for index, (source, target) in enumerate(((SWI, swi_out), (DA, da_out), (DB, db_out)))
        ]

    def own_h2_store(chunk):
        return pltpu.make_async_copy(H2O.at[rows_of(chunk)], h2_full.at[rows_of(chunk), own_columns], stage_sem.at[4 + chunk])

    def small_store(source, target, chunk, index):
        return pltpu.make_async_copy(source, target.at[rows_of(chunk)], store_sem.at[index])

    def fetch(source, target, index):
        copy = pltpu.make_async_copy(source, target, load_sem.at[index])
        copy.start()
        return copy

    def stat_copy(chunk, step, which):
        source, target = ((SV, SA), (SV2, SA2))[which]
        columns = rows_of(chunk)
        return remote(
            source.at[:, columns], target.at[t, :, columns], s_send.at[which, chunk, step - 1], s_recv.at[which, chunk, step - 1],
            place.along((t + step) % 4),
        )

    def stats(chunk, which):
        source, target = ((SV, SA), (SV2, SA2))[which]
        for step in range(1, 4):
            stat_copy(chunk, step, which).wait_recv()
        total = source[0:1, rows_of(chunk)]
        for step in range(1, 4):
            total = total + target[(t + step) % 4, 0:1, rows_of(chunk)]
        return to_column(total)

    def memory_unit(chunk):
        if chunk == 0:
            own_tokens.wait()
        load = fetch(tok_full.at[rows_of(chunk)], XC, 1)
        if chunk > 0:
            h1_store(chunk - 1).wait()
        load.wait()
        square = jnp.zeros((chunk_rows, 1), jnp.float32)
        for block in range(4):
            values = XC[:, block * width:(block + 1) * width].astype(jnp.float32)
            square += jnp.sum(values * values, axis=1, keepdims=True)
        inverse = lax.rsqrt(square / features + EPS)
        inv_out[rows_of(chunk)] = inverse
        for block in range(4):
            at = slice(block * width, (block + 1) * width)
            H1C[:, at] = (XC[:, at].astype(jnp.float32) * inverse * gain1[:, at]).astype(jnp.bfloat16)
        h1_store(chunk).start()
        mem_load(chunk).wait()
        if chunk > 0:
            gate_store(chunk - 1).wait()
        if chunk > 1:
            mixed_store(chunk - 2).wait()

        @pl.loop(0, 2)
        def _(part):
            at = columns_of(part, half)
            pre = jnp.dot(H1C[...], WG[:, at], preferred_element_type=jnp.float32)
            GPS[:, at] = pre
            MXS[chunk % 2, :, at] = (MT[:, at].astype(jnp.float32) * (pre * jax.nn.sigmoid(pre))).astype(jnp.bfloat16)

        gate_store(chunk).start()
        mixed_store(chunk).start()
        if chunk + 1 < 4:
            mem_load(chunk + 1).start()

    def mix_part(chunk, block):
        return jnp.dot(MXS[chunk % 2], WO[:, columns_of(block, width)], preferred_element_type=jnp.float32)

    def mix_own(chunk):
        load = fetch(tokens.at[rows_of(chunk)], OWN, 2)
        HO[...] = mix_part(chunk, t)
        mix_scatter.own(chunk, HO)
        load.wait()
        middle = OWN[...].astype(jnp.float32) + HO[...]
        X1[rows_of(chunk)] = middle
        H2O[rows_of(chunk)] = (middle * gain2[...]).astype(jnp.bfloat16)
        own_h2_store(chunk).start()
        SV[:, rows_of(chunk)] = to_row(jnp.sum(middle * middle, axis=1, keepdims=True))
        mix_scatter.finish(chunk)
        h2_gather.step(chunk, 0)
        for step in range(1, 4):
            stat_copy(chunk, step, 0).start()

    def feed_forward(chunk):
        own_h2_store(chunk).wait()
        if chunk == 0:
            own_cot.wait()
        loads = [fetch(h2_full.at[rows_of(chunk)], XC, 1), fetch(cot_full.at[rows_of(chunk)], CC, 3)]
        inverse = lax.rsqrt(stats(chunk, 0) / features + EPS)
        I2[rows_of(chunk)] = inverse
        if chunk > 1:
            for store in hidden_stores(chunk - 2):
                store.wait()
        for load in loads:
            load.wait()

        @pl.loop(0, 4)
        def _(part):
            at = columns_of(part, hidden // 4)
            up_a = jnp.dot(XC[...], WA[:, at], preferred_element_type=jnp.float32) * inverse
            up_b = jnp.dot(XC[...], WB[:, at], preferred_element_type=jnp.float32) * inverse
            d_swi = dot_nt(CC[...], WD[at, :])
            sigma = jax.nn.sigmoid(up_a)
            swish = up_a * sigma
            SWI[chunk % 2, :, at] = (swish * up_b).astype(jnp.bfloat16)
            d_swi = d_swi * inverse
            DA[chunk % 2, :, at] = (d_swi * up_b * (sigma * (1.0 + up_a * (1.0 - sigma)))).astype(jnp.bfloat16)
            DB[chunk % 2, :, at] = (d_swi * swish).astype(jnp.bfloat16)

        for store in hidden_stores(chunk):
            store.start()

    def down_part(chunk, block):
        return jnp.dot(SWI[chunk % 2], WD[:, columns_of(block, width)], preferred_element_type=jnp.float32)

    def up_part(chunk, block):
        at = columns_of(block, width)
        return dot_nt(DA[chunk % 2], WA[at, :]) + dot_nt(DB[chunk % 2], WB[at, :])

    def hidden_own(chunk):
        if chunk > 0:
            small_store(BS.at[0], block_out, chunk - 1, 10).wait()
        HO[...] = up_part(chunk, t)
        up_scatter.own(chunk, HO)
        middle = X1[rows_of(chunk)]
        d_second = HO[...]
        grads = jnp.sum(d_second * middle, axis=0, keepdims=True)
        if chunk == 0:
            gg2_out[...] = grads
        else:
            gg2_out[...] += grads
        scaled = d_second * gain2[...]
        DHQ[...] = scaled
        SV2[:, rows_of(chunk)] = to_row(jnp.sum(scaled * middle, axis=1, keepdims=True) * I2[rows_of(chunk)])
        HO[...] = down_part(chunk, t)
        down_scatter.own(chunk, HO)
        BS[0] = (middle + HO[...]).astype(jnp.bfloat16)
        small_store(BS.at[0], block_out, chunk, 10).start()
        up_scatter.finish(chunk)
        down_scatter.finish(chunk)
        for step in range(1, 4):
            stat_copy(chunk, step, 1).start()

    def close(chunk):
        load = fetch(cotangent.at[rows_of(chunk)], OWN, 2)
        mean = stats(chunk, 1) / features
        if chunk > 0:
            small_store(FS, dx1_out, chunk - 1, 11).wait()
            small_store(BS.at[1], branch_out, chunk - 1, 12).wait()
        load.wait()
        unit = X1[rows_of(chunk)] * I2[rows_of(chunk)]
        total = OWN[...].astype(jnp.float32) + DHQ[...] - unit * mean
        FS[...] = total
        BS[1] = total.astype(jnp.bfloat16)
        small_store(FS, dx1_out, chunk, 11).start()
        small_store(BS.at[1], branch_out, chunk, 12).start()

    def mix_steps(chunk, ends, inside):
        def run(steps, inner):
            for step in steps:
                mix_scatter.step(chunk, step, lambda block: mix_part(chunk, block), inner)

        by_place(place, lambda: run(ends, False), lambda: run(inside, True))

    def hidden_steps(chunk, ends, inside):
        def run(steps, inner):
            for step in steps:
                up_scatter.step(chunk, step, lambda block: up_part(chunk, block), inner)
                down_scatter.step(chunk, step, lambda block: down_part(chunk, block), inner)

        by_place(place, lambda: run(ends, False), lambda: run(inside, True))

    def pumps(turn):
        for index, number in {
            0: ((0, 0),), 1: ((0, 1), (1, 0)), 2: ((0, 2), (1, 1)), 3: ((0, 3), (1, 2), (2, 0), (1, 3)), 5: ((2, 1), (3, 0)),
            6: ((2, 2),), 7: ((2, 3), (3, 1), (4, 0)), 8: ((3, 2),), 9: ((3, 3), (4, 1), (4, 2), (4, 3)),
        }.get(turn, ()):
            spreads[index].phase(number)

    def hops(chunk, event):
        if event in (0, 1, 2):
            tok_gather.step(chunk, event)
        if event in (3, 4, 5, 6):
            cot_gather.step(chunk, event - 3)
        if event in (7, 8):
            h2_gather.step(chunk, event - 6)
        if event == 13:
            close(chunk)

    def light(chunk, event):
        if event == 4:
            mix_steps(chunk, (1,), (0,))
        if event == 5:
            mix_steps(chunk, (2,), (1, 2))
        if event == 6:
            mix_own(chunk)
        if event == 10:
            hidden_steps(chunk, (1,), (0,))
        if event == 11:
            hidden_steps(chunk, (2,), (1, 2))
        if event == 12:
            hidden_own(chunk)

    def heavy(chunk, event):
        if event == 3:
            tok_gather.step(chunk, 3)
            memory_unit(chunk)
            mix_steps(chunk, (0,), ())
        if event == 9:
            h2_gather.step(chunk, 3)
            feed_forward(chunk)
            hidden_steps(chunk, (0,), ())

    mem_load(0).start()
    weight_stores = [
        pltpu.make_async_copy(WG, gate_w_out, stage_sem.at[2]), pltpu.make_async_copy(WO, out_w_out, stage_sem.at[3]),
    ]
    for turn in range(20):
        pumps(turn)
        if turn == 3:
            for store in weight_stores:
                store.start()
        for action in (hops, light, heavy):
            for chunk in range(4):
                action(chunk, turn - 2 * chunk)

    for store in weight_stores:
        store.wait()
    for spread in spreads:
        spread.finish()
    for chunk in range(4):
        for gather in (tok_gather, cot_gather, h2_gather):
            gather.finish(chunk)
        for which in range(2):
            for step in range(1, 4):
                stat_copy(chunk, step, which).wait_send()
    h1_store(3).wait()
    gate_store(3).wait()
    for chunk in (2, 3):
        mixed_store(chunk).wait()
        for store in hidden_stores(chunk):
            store.wait()
    small_store(BS.at[0], block_out, 3, 10).wait()
    small_store(FS, dx1_out, 3, 11).wait()
    small_store(BS.at[1], branch_out, 3, 12).wait()


def front_call(tokens, cotangent, mem, gate_w, out_w, up_a_w, up_b_w, down_w, gain1, gain2):
    rows, width = tokens.shape
    features, channels, hidden = 4 * width, mem.shape[1], up_a_w.shape[1]
    part = rows // 4
    bf, f32 = jnp.bfloat16, jnp.float32
    shape = jax.ShapeDtypeStruct
    anywhere, vmem = pl.BlockSpec(memory_space=pl.ANY), pl.BlockSpec(memory_space=pltpu.VMEM)
    dma = pltpu.SemaphoreType.DMA
    V = pltpu.VMEM
    macs = rows * features * (6 * hidden + 2 * channels)
    return pl.pallas_call(
        front_kernel,
        name="forward",
        out_shape=(
            shape((rows, features), bf), shape((rows, features), bf), shape((rows, features), bf), shape((rows, features), bf),
            shape((rows, channels), f32), shape((rows, channels), bf), shape((rows, hidden), bf), shape((rows, hidden), bf),
            shape((rows, hidden), bf), shape((features, channels), bf), shape((channels, features), bf), shape((rows, width), bf),
            shape((rows, width), f32), shape((rows, width), bf), shape((rows, 1), f32), shape((1, width), f32),
        ),
        in_specs=[anywhere] * 8 + [vmem] * 2,
        out_specs=(anywhere,) * 14 + (vmem,) * 2,
        scratch_shapes=[
            V((features, channels), bf), V((channels, features), bf), V((features, hidden), bf), V((features, hidden), bf),
            V((hidden, features), bf), V((2, 5, part, width), bf), V((2, 5, part, width), bf), V((2, 5, part, width), bf),
            V((part, features), bf), V((part, features), bf), V((part, features), bf), V((part, channels), f32), V((2, part, channels), bf),
            V((part, channels), bf), V((2, part, hidden), bf), V((2, part, hidden), bf), V((2, part, hidden), bf), V((rows, width), f32),
            V((rows, width), bf), V((part, width), f32), V((part, width), f32), V((part, width), f32), V((2, part, width), bf),
            V((part, width), bf), V((rows, 1), f32), V((8, rows), f32), V((4, 8, rows), f32), V((8, rows), f32), V((4, 8, rows), f32),
            dma((4,)), dma((13,)), dma((8,)), dma((4, 2, 3)), dma((4, 4)), dma((4, 2, 3)), dma((4, 4)), dma((4, 2, 3)), dma((4, 4)),
            dma((4, 3)), dma((4, 5)), dma((4, 3)), dma((4, 5)), dma((4, 3)), dma((4, 5)), dma((5, 7)), dma((5, 8)), dma((5,)),
            dma((2, 4, 3)), dma((2, 4, 3)),
        ],
        compiler_params=pltpu.CompilerParams(collective_id=2, has_side_effects=True, vmem_limit_bytes=VMEM_LIMIT),
        cost_estimate=pl.CostEstimate(flops=2 * macs, bytes_accessed=96 * 2**20, transcendentals=rows * (channels + hidden)),
    )(tokens, cotangent, mem, gate_w, out_w, up_a_w, up_b_w, down_w, gain1, gain2)


def silu_grad(values):
    sigma = jax.nn.sigmoid(values)
    return sigma * (1.0 + values * (1.0 - sigma))


def normalize(values):
    inverse = lax.rsqrt(jnp.mean(values * values, axis=-1, keepdims=True) + EPS)
    return (values * inverse, inverse)


def contract_rows(left, right):
    return lax.dot_general(
        left, right, (((0,), (0,)), ((), ())), preferred_element_type=jnp.float32
    )


def contract_cols(left, right):
    return lax.dot_general(
        left, right, (((1,), (1,)), ((), ())), preferred_element_type=jnp.float32
    )


def sum_scatter(part):
    return lax.psum_scatter(
        part.astype(jnp.bfloat16), "tp", scatter_dimension=1, tiled=True
    ).astype(jnp.float32)


def mean_over(values, features):
    return lax.psum(jnp.sum(values, axis=-1, keepdims=True), "tp") / features


def grad_scatter(part, dimension):
    return lax.psum_scatter(
        part.astype(jnp.bfloat16), ("fsdp", "ctx"), scatter_dimension=dimension, tiled=True
    ).astype(jnp.float32)


def middle_of(tokens, memory_tokens, cotangent, gain_first, gain_second, memory_gate, memory_out, hidden_gate, hidden_up, hidden_down):
    memory_f = memory_tokens.astype(jnp.float32)
    gathered = (
        lax.all_gather(memory_gate, ("fsdp", "ctx"), axis=0, tiled=True),
        lax.all_gather(memory_out, ("fsdp", "ctx"), axis=1, tiled=True),
        lax.all_gather(hidden_gate, ("fsdp", "ctx"), axis=0, tiled=True),
        lax.all_gather(hidden_up, ("fsdp", "ctx"), axis=0, tiled=True),
        lax.all_gather(hidden_down, ("fsdp", "ctx"), axis=1, tiled=True),
    )
    gate_w, out_w, up_a_w, up_b_w, down_w = gathered
    width = tokens.shape[1]
    column = lax.axis_index("tp") * width
    full_tokens, full_cot = (
        lax.all_gather(tokens, "tp", axis=1, tiled=True),
        lax.all_gather(cotangent, "tp", axis=1, tiled=True),
    )
    inputs = full_tokens.astype(jnp.float32)
    unit_first, inv_first = normalize(inputs)
    first = (unit_first * gain_first).astype(jnp.bfloat16)
    gate_pre = jnp.dot(first, gate_w, preferred_element_type=jnp.float32)
    activated = jax.nn.silu(gate_pre)
    mixed = (memory_f * activated).astype(jnp.bfloat16)
    features = full_tokens.shape[1]
    own = lambda array: lax.dynamic_slice_in_dim(array, column, width, array.ndim - 1)
    gain_one, gain_two = own(gain_first), own(gain_second)
    shard_tokens = tokens.astype(jnp.float32)
    middle = shard_tokens + sum_scatter(jnp.dot(mixed, out_w, preferred_element_type=jnp.float32))
    inv_second = lax.rsqrt(mean_over(middle * middle, features) + EPS)
    unit_second = middle * inv_second
    second = lax.all_gather((unit_second * gain_two).astype(jnp.bfloat16), "tp", axis=1, tiled=True)
    up_a = jnp.dot(second, up_a_w, preferred_element_type=jnp.float32)
    up_b = jnp.dot(second, up_b_w, preferred_element_type=jnp.float32)
    swish_a = jax.nn.silu(up_a)
    swished = (swish_a * up_b).astype(jnp.bfloat16)
    output = middle + sum_scatter(jnp.dot(swished, down_w, preferred_element_type=jnp.float32))
    block_out = output.astype(jnp.bfloat16)
    d_swished = contract_cols(full_cot, down_w)
    d_a = (d_swished * up_b * silu_grad(up_a)).astype(jnp.bfloat16)
    d_b = (d_swished * swish_a).astype(jnp.bfloat16)
    d_second = sum_scatter(contract_cols(d_a, up_a_w) + contract_cols(d_b, up_b_w))
    scaled = d_second * gain_two
    middle_norm = inv_second * (scaled - unit_second * mean_over(scaled * unit_second, features))
    gain_two_part = jnp.sum(d_second * unit_second, axis=0)
    d_middle = cotangent.astype(jnp.float32) + middle_norm
    unit_own = shard_tokens * inv_first
    d_branch = lax.all_gather(d_middle.astype(jnp.bfloat16), "tp", axis=1, tiled=True)
    d_mixed = contract_cols(d_branch, out_w)
    back = (d_mixed * activated).astype(jnp.bfloat16)
    d_gate = (d_mixed * memory_f * silu_grad(gate_pre)).astype(jnp.bfloat16)
    d_first = sum_scatter(contract_cols(d_gate, gate_w))
    scaled = d_first * gain_one
    input_norm = inv_first * (scaled - unit_own * mean_over(scaled * unit_own, features))
    gain_one_part = jnp.sum(d_first * unit_own, axis=0)
    parts = lax.psum(jnp.stack([gain_one_part, gain_two_part]), ("fsdp", "ctx"))
    gains = lax.all_gather(parts, "tp", axis=1, tiled=True)
    grad_gain_first, grad_gain_second = gains[0], gains[1]
    sums = (
        grad_scatter(contract_rows(first, d_gate), 0),
        grad_scatter(contract_rows(mixed, d_branch), 1),
        grad_scatter(contract_rows(second, d_a), 0),
        grad_scatter(contract_rows(second, d_b), 0),
        grad_scatter(contract_rows(swished, full_cot), 1),
    )
    return block_out, d_middle, input_norm, back, grad_gain_first, grad_gain_second, sums


def middle_on_line(tokens, memory_tokens, cotangent, gain_first, gain_second, memory_gate, memory_out, hidden_gate, hidden_up, hidden_down):
    width = tokens.shape[1]
    features = 4 * width
    own = lambda array: lax.dynamic_slice_in_dim(array, lax.axis_index("tp") * width, width, 0)[None]
    gain_one, gain_two = own(gain_first), own(gain_second)
    (
        _, full_cot, second, first, gate_pre, mixed, swished, d_a, d_b, gate_w, out_w, block_out, d_middle, d_branch, inv_first, gain_two_part,
    ) = front_call(
        tokens, cotangent, memory_tokens, memory_gate, memory_out, hidden_gate, hidden_up, hidden_down, gain_first[None], gain_two
    )
    unit_own = tokens.astype(jnp.float32) * inv_first
    d_first, back, grad_down, grad_up_a, grad_up_b, grad_out, grad_gate, gains, stats = back_call(
        d_branch, full_cot, swished, second, d_a, d_b, mixed, first, gate_pre, memory_tokens, out_w, gate_w, unit_own, gain_one, gain_two_part
    )
    input_norm = inv_first * (d_first * gain_one - unit_own * (stats[0][:, None] / features))
    grad_gain_first, grad_gain_second = gains[:, 0].reshape(features), gains[:, 1].reshape(features)
    sums = (grad_gate, grad_out.T, grad_up_a, grad_up_b, grad_down.T)
    return block_out, d_middle, input_norm, back, grad_gain_first, grad_gain_second, sums


def shards(
    tokens,
    memory,
    dealing,
    cotangent,
    gain_first,
    gain_second,
    memory_gate,
    memory_out,
    hidden_gate,
    hidden_up,
    hidden_down,
):
    groups = lax.axis_size(("fsdp", "ctx"))
    group_index = lax.axis_index(("fsdp", "ctx"))
    rows = dealing.shape[0]
    block = rows // groups
    order = jnp.argsort(dealing)
    sent_rows = memory[order].reshape(groups, block, memory.shape[1])
    arrived = lax.all_to_all(sent_rows, ("fsdp", "ctx"), split_axis=0, concat_axis=0, tiled=True)
    arrived_ids = lax.all_to_all(
        dealing[order].reshape(groups, block),
        ("fsdp", "ctx"),
        split_axis=0,
        concat_axis=0,
        tiled=True,
    )
    places = arrived_ids.reshape(rows) - group_index * rows
    memory_tokens = arrived.reshape(rows, memory.shape[1])[jnp.argsort(places)]
    on_line = lax.axis_size("fsdp") == 2 and lax.axis_size("ctx") == 4 and lax.axis_size("tp") == 4
    block_out, d_middle, input_norm, back, grad_gain_first, grad_gain_second, sums = (middle_on_line if on_line else middle_of)(
        tokens, memory_tokens, cotangent, gain_first, gain_second, memory_gate, memory_out, hidden_gate, hidden_up, hidden_down
    )
    grad_inputs = d_middle + input_norm
    back_rows = back[places].reshape(groups, block, memory.shape[1])
    returned = lax.all_to_all(back_rows, ("fsdp", "ctx"), split_axis=0, concat_axis=0, tiled=True)
    grad_memory = returned.reshape(rows, memory.shape[1])[jnp.argsort(order)].astype(jnp.float32)
    return (
        block_out,
        grad_inputs,
        grad_memory,
        grad_gain_first,
        grad_gain_second,
        sums[0],
        sums[1],
        sums[2],
        sums[3],
        sums[4],
    )


def solution(mesh):
    in_specs = (
        P(("fsdp", "ctx"), "tp"),
        P(("fsdp", "ctx"), "tp"),
        P(("fsdp", "ctx")),
        P(("fsdp", "ctx"), "tp"),
        P(),
        P(),
        P(("fsdp", "ctx"), "tp"),
        P("tp", ("fsdp", "ctx")),
        P(("fsdp", "ctx"), "tp"),
        P(("fsdp", "ctx"), "tp"),
        P("tp", ("fsdp", "ctx")),
    )
    out_specs = (
        P(("fsdp", "ctx"), "tp"),
        P(("fsdp", "ctx"), "tp"),
        P(("fsdp", "ctx"), "tp"),
        P(),
        P(),
        P(("fsdp", "ctx"), "tp"),
        P("tp", ("fsdp", "ctx")),
        P(("fsdp", "ctx"), "tp"),
        P(("fsdp", "ctx"), "tp"),
        P("tp", ("fsdp", "ctx")),
    )
    return jax.shard_map(shards, mesh=mesh, in_specs=in_specs, out_specs=out_specs, check_vma=False)
```

```python
import jax
import jax.numpy as jnp
from jax import lax
from jax.experimental import pallas as pl
from jax.experimental.pallas import tpu as pltpu
from jax.sharding import PartitionSpec as P

EPS = 1e-06
VMEM_LIMIT = 62 * 2**20


MESH = pl.DeviceIdType.MESH
JOBS = 8


def dot_nt(left, right):
    return lax.dot_general(left, right, (((1,), (1,)), ((), ())), preferred_element_type=jnp.float32)


def dot_tn(left, right):
    return lax.dot_general(left, right, (((0,), (0,)), ((), ())), preferred_element_type=jnp.float32)


class Place:
    def __init__(self):
        self.f, self.c, self.t = lax.axis_index("fsdp"), lax.axis_index("ctx"), lax.axis_index("tp")
        self.y, self.k = self.c // 2, self.c % 2

    def at(self, flip_f, flip_y, flip_k):
        f = self.f + flip_f * (1 - 2 * self.f)
        y = self.y + flip_y * (1 - 2 * self.y)
        k = self.k + flip_k * (1 - 2 * self.k)
        return f, y * 2 + k

    def sibling(self):
        return (*self.at(0, 0, 1), self.t)

    def first(self):
        return (*self.at(1 - self.k, self.k, 0), self.t)

    def second(self):
        return (*self.at(self.k, 1 - self.k, 0), self.t)

    def along(self, t):
        return (self.f, self.c, t)

    def owner(self, slot, flip_k):
        alpha, beta = 1 - slot // 2, 1 - slot % 2
        parity = self.k + flip_k * (1 - 2 * self.k)
        f, c = self.at(alpha * (1 - parity) + beta * parity, beta * (1 - parity) + alpha * parity, flip_k)
        return f * 4 + c


def remote(source, target, send, recv, device):
    return pltpu.make_async_remote_copy(
        src_ref=source, dst_ref=target, send_sem=send, recv_sem=recv, device_id=device, device_id_type=MESH
    )


OTHERS = ((1, 1, 1), (1, 1, 0), (0, 1, 1), (1, 0, 1), (0, 1, 0), (1, 0, 0), (0, 0, 1))


def greet(place):
    barrier = pltpu.get_barrier_semaphore()
    for flips in OTHERS:
        pl.semaphore_signal(barrier, inc=1, device_id=(*place.at(*flips), place.t), device_id_type=MESH)
    for step in range(1, 4):
        pl.semaphore_signal(barrier, inc=1, device_id=place.along((place.t + step) % 4), device_id_type=MESH)
    pl.semaphore_wait(barrier, 10)


class Exchange:
    def __init__(self, place, source, target, send, recv):
        self.place, self.source, self.target, self.send, self.recv = place, source, target, send, recv
        self.me = place.f * 4 + place.c

    def copy(self, index):
        f, c = self.place.at(*OTHERS[index])
        group = f * 4 + c
        out = remote(self.source(group), self.target(self.me), self.send.at[index], self.recv.at[self.me], (f, c, self.place.t))
        back = remote(self.source(group), self.target(group), self.send.at[index], self.recv.at[group], (f, c, self.place.t))
        return out, back

    def stay(self):
        return pltpu.make_async_copy(self.source(self.me), self.target(self.me), self.send.at[7])

    def start(self):
        for index in range(7):
            self.copy(index)[0].start()
        self.stay().start()

    def arrived(self):
        for index in range(7):
            self.copy(index)[1].wait_recv()
        self.stay().wait()

    def finish(self):
        for index in range(7):
            self.copy(index)[0].wait_send()


def chosen(row, first, count):
    places = lax.broadcasted_iota(jnp.int32, (count, row.shape[1]), 0) + first
    return jnp.where(row == places, 1.0, 0.0).astype(jnp.bfloat16)


class Gather:
    def __init__(self, place, full, send, recv, rows, width, own=None):
        self.place, self.full, self.send, self.recv, self.rows, self.width, self.mine = place, full, send, recv, rows, width, own

    def copy(self, chunk, shard, way, hop):
        view = self.full.at[pl.ds(chunk * self.rows, self.rows), pl.ds(pl.multiple_of(shard * self.width, self.width), self.width)]
        device = self.place.along(self.place.t + 1 - 2 * way)
        source = view if hop > 0 or self.mine is None else self.mine.at[pl.ds(chunk * self.rows, self.rows)]
        return remote(source, view, self.send.at[chunk, way, hop], self.recv.at[chunk, shard], device)

    def step(self, chunk, hop):
        t = self.place.t

        @pl.when(t - hop >= 0)
        def _():
            if hop > 0:
                self.copy(chunk, t - hop, 0, hop).wait_recv()
            if hop < 3:
                @pl.when(t < 3)
                def _():
                    self.copy(chunk, t - hop, 0, hop).start()

        @pl.when(t + hop <= 3)
        def _():
            if hop > 0:
                self.copy(chunk, t + hop, 1, hop).wait_recv()
            if hop < 3:
                @pl.when(t > 0)
                def _():
                    self.copy(chunk, t + hop, 1, hop).start()

    def finish(self, chunk):
        t = self.place.t
        for hop in range(3):
            @pl.when((t - hop >= 0) & (t < 3))
            def _():
                self.copy(chunk, t - hop, 0, hop).wait_send()

            @pl.when((t + hop <= 3) & (t > 0))
            def _():
                self.copy(chunk, t + hop, 1, hop).wait_send()


class Scatter:
    def __init__(self, place, slots, send, recv):
        self.place, self.slots, self.send, self.recv = place, slots, send, recv
        self.ring = slots.shape[0]

    def block(self, step):
        t = self.place.t
        low, high = t % 2, t // 2
        return (3 * (1 - high), 2 - 2 * low + high, 1 + low, t)[step]

    def copy(self, chunk, step):
        t, block, ring = self.place.t, self.block(step), chunk % self.ring
        up = (block > t).astype(jnp.int32)
        last_down = (block == t - 1).astype(jnp.int32)
        slot = block + last_down * (4 - block)
        device = self.place.along(t - 1 + 2 * up)
        return remote(self.slots.at[ring, block], self.slots.at[ring, slot], self.send.at[chunk, step], self.recv.at[chunk, slot], device)

    def arrived(self, chunk, slot):
        view = self.slots.at[chunk % self.ring, slot]
        remote(view, view, self.send.at[chunk, 0], self.recv.at[chunk, slot], self.place.along(self.place.t)).wait_recv()

    def step(self, chunk, step, part, inside):
        block, ring = self.block(step), chunk % self.ring
        value = part(block)
        if inside:
            self.arrived(chunk, block)
            value += self.slots[ring, block].astype(jnp.float32)
        self.slots[ring, block] = value.astype(jnp.bfloat16)
        self.copy(chunk, step).start()

    def own(self, chunk, held):
        t, ring = self.place.t, chunk % self.ring

        @pl.when(t > 0)
        def _():
            self.arrived(chunk, t)
            held[...] += self.slots[ring, t].astype(jnp.float32)

        @pl.when(t < 3)
        def _():
            self.arrived(chunk, 4)
            held[...] += self.slots[ring, 4].astype(jnp.float32)

    def finish(self, chunk):
        for step in range(3):
            self.copy(chunk, step).wait_send()


def by_place(place, ends, inside):
    is_end = (place.t == 0) | (place.t == 3)
    pl.when(is_end)(ends)
    pl.when(jnp.logical_not(is_end))(inside)


def to_row(column):
    return jnp.broadcast_to(column, (column.shape[0], 128)).T[:8]


def back_kernel(
    branch_own, cot_in, swi_in, h2_in, da_in, db_in, mixed_in, h1_in, gate_in, mem_in, out_w_in, gate_w_in, xhat_in, gain_ref, gg2_ref, rank_ref, ids_ref,
    dh1_out, memory_out, term_out, returned, hd_out, hg_out, hu_out, mo_out, mg_out, gains_out, stats_out,
    A1, A2, B1, B2, MX, DB, DG, WO, WG, SR, SS, H1S, H1R, H2S, H2R, OS, RZ, GP, MT, TS, XH, HO, GV, GR, GA, SV, SA, PLACES,
    load_sem, gate_sem, ag_send, ag_recv, rs_send, rs_recv, sib_send, sib_recv, h1_send, h1_recv, h2_send, h2_recv,
    out_sem, small_send, small_recv, x_send, x_recv, sib_free, first_free, second_free,
):
    place = Place()
    t = place.t
    chunk_rows, width = XH.shape
    slab = OS.shape[0]
    span = OS.shape[1]
    cols = span // 2
    chunks = 4

    loads = {}

    def load(name, source, target, slot):
        loads[name] = pltpu.make_async_copy(source, target, load_sem.at[slot])
        loads[name].start()

    def need(*names):
        for name in names:
            if name in loads:
                loads.pop(name).wait()

    own_columns = pl.ds(pl.multiple_of(t * width, width), width)
    load("branch", branch_own, DB.at[:, own_columns], 0)
    load("cot", cot_in, A1, 1)
    load("swi", swi_in, B1, 2)
    load("h2", h2_in, A2, 3)
    load("da", da_in, B2, 4)
    load("out_w", out_w_in, WO, 5)
    load("gate_w", gate_w_in, WG, 6)
    load("mixed", mixed_in, MX, 7)
    greet(place)

    gather = Gather(place, DB, ag_send, ag_recv, chunk_rows, width)
    scatter = Scatter(place, RZ, rs_send, rs_recv)
    need("branch")
    for chunk in range(chunks):
        gather.step(chunk, 0)

    jobs = [
        (A1, B1, 0, hd_out, 0), (A1, B1, span, hd_out, span), (A2, B2, 0, hg_out, 0), (A2, B2, span, hg_out, span),
        (A2, B1, 0, hu_out, 0), (A2, B1, span, hu_out, span), (DB, MX, 0, mo_out, 0), (A1, DG, 0, mg_out, 0),
    ]

    def tile(job, group, half):
        left, right, offset = jobs[job][:3]
        columns = pl.ds(pl.multiple_of(offset + half * cols, cols), cols)
        return dot_tn(left[:, pl.ds(pl.multiple_of(group * slab, slab), slab)], right[:, columns])

    def each_half(body):
        @pl.loop(0, 2)
        def _(half):
            body(half, pl.ds(pl.multiple_of(half * cols, cols), cols))

    def sib_copy(job, slot):
        return remote(SS.at[slot], SR.at[job % 3, slot], sib_send.at[slot], sib_recv.at[job, slot], place.sibling())

    def h1_copy(job, slot):
        return remote(H1S.at[job % 2, slot], H1R.at[job % 3, slot], h1_send.at[job % 2, slot], h1_recv.at[job, slot], place.first())

    def h2_copy(job):
        return remote(H2S.at[job % 2], H2R.at[job % 2], h2_send.at[job % 2], h2_recv.at[job], place.second())

    def to_sibling(job):
        if job >= 3:
            pl.semaphore_wait(sib_free, 1)

        @pl.loop(0, 4)
        def _(slot):
            if job >= 1:
                sib_copy(job - 1, slot).wait_send()
            group = place.owner(slot, 1)

            def body(half, at):
                SS[slot, :, at] = tile(job, group, half).astype(jnp.bfloat16)

            each_half(body)
            sib_copy(job, slot).start()

    def to_first(job):
        if job >= 3:
            pl.semaphore_wait(first_free, 1)

        @pl.loop(0, 2)
        def _(slot):
            if job >= 2:
                h1_copy(job - 2, slot).wait_send()
            group = place.owner(slot, 0)
            sib_copy(job, slot).wait_recv()

            def body(half, at):
                H1S[job % 2, slot, :, at] = (tile(job, group, half) + SR[job % 3, slot, :, at].astype(jnp.float32)).astype(jnp.bfloat16)

            each_half(body)
            h1_copy(job, slot).start()

    def to_second(job):
        if job >= 2:
            pl.semaphore_wait(second_free, 1)
            h2_copy(job - 2).wait_send()
        group = place.owner(2, 0)
        sib_copy(job, 2).wait_recv()
        h1_copy(job, 0).wait_recv()

        def body(half, at):
            H2S[job % 2, :, at] = (
                tile(job, group, half) + SR[job % 3, 2, :, at].astype(jnp.float32) + H1R[job % 3, 0, :, at].astype(jnp.float32)
            ).astype(jnp.bfloat16)

        each_half(body)
        h2_copy(job).start()

    def out_copy(job):
        return pltpu.make_async_copy(OS, jobs[job][3].at[:, pl.ds(jobs[job][4], span)], out_sem)

    def to_output(job):
        group = place.owner(3, 0)
        sib_copy(job, 3).wait_recv()
        h1_copy(job, 1).wait_recv()
        h2_copy(job).wait_recv()
        if job >= 1:
            out_copy(job - 1).wait()

        def body(half, at):
            OS[:, at] = (
                tile(job, group, half) + SR[job % 3, 3, :, at].astype(jnp.float32)
                + H1R[job % 3, 1, :, at].astype(jnp.float32) + H2R[job % 2, :, at].astype(jnp.float32)
            )

        each_half(body)
        out_copy(job).start()
        for ahead, free, device in ((3, sib_free, place.sibling()), (3, first_free, place.first()), (2, second_free, place.second())):
            if job + ahead < JOBS:
                pl.semaphore_signal(free, inc=1, device_id=device, device_id_type=MESH)

    def gate_loads(chunk):
        rows = pl.ds(chunk * chunk_rows, chunk_rows)
        return (
            pltpu.make_async_copy(gate_in.at[rows], GP, gate_sem.at[0]),
            pltpu.make_async_copy(mem_in.at[rows], MT, gate_sem.at[1]),
        )

    def term_store(chunk):
        return pltpu.make_async_copy(TS, term_out.at[pl.ds(chunk * chunk_rows, chunk_rows)], gate_sem.at[2])

    def channels(chunk):
        rows = pl.ds(chunk * chunk_rows, chunk_rows)
        for copy in gate_loads(chunk):
            copy.wait()
        if chunk > 0:
            term_store(chunk - 1).wait()

        def body(half, at):
            d_mixed = dot_nt(DB[rows, :], WO[at, :])
            pre = GP[:, at]
            sigma = jax.nn.sigmoid(pre)
            TS[:, at] = (d_mixed * (pre * sigma)).astype(jnp.bfloat16)
            DG[rows, at] = (d_mixed * MT[:, at].astype(jnp.float32) * (sigma * (1.0 + pre * (1.0 - sigma)))).astype(jnp.bfloat16)

        each_half(body)
        term_store(chunk).start()
        if chunk + 1 < chunks:
            for copy in gate_loads(chunk + 1):
                copy.start()

    def first_part(chunk, block):
        return dot_nt(DG[pl.ds(chunk * chunk_rows, chunk_rows), :], WG[pl.ds(pl.multiple_of(block * width, width), width), :])

    def first_step(chunk, step, inside):
        scatter.step(chunk, step, lambda block: first_part(chunk, block), inside)

    def own_copies(chunk):
        rows = pl.ds(chunk * chunk_rows, chunk_rows)
        return (
            pltpu.make_async_copy(xhat_in.at[rows], XH, gate_sem.at[3]),
            pltpu.make_async_copy(HO, dh1_out.at[rows], gate_sem.at[4]),
        )

    def own_step(chunk):
        load_xhat, store = own_copies(chunk)
        load_xhat.start()
        if chunk > 0:
            own_copies(chunk - 1)[1].wait()
        HO[...] = first_part(chunk, t)
        scatter.own(chunk, HO)
        load_xhat.wait()
        product = HO[...] * XH[...]
        if chunk == 0:
            GV[0, 0:1] = jnp.sum(product, axis=0, keepdims=True)
        else:
            GV[0, 0:1] += jnp.sum(product, axis=0, keepdims=True)
        SV[:, pl.ds(chunk * chunk_rows, chunk_rows)] = to_row(jnp.sum(product * gain_ref[...], axis=1, keepdims=True))
        store.start()

    def sum_copy(step):
        device = (place.sibling(), place.first(), place.second())[step]
        return remote(GV.at[step], GR.at[step], small_send.at[step], small_recv.at[step], device)

    def to_line(step, what):
        device = place.along((t + step) % 4)
        if what == 0:
            return remote(SV, SA.at[t], small_send.at[2 + step], small_recv.at[2 + step], device)
        return remote(GV.at[3], GA.at[t], small_send.at[5 + step], small_recv.at[5 + step], device)

    channel_count = span
    block = DB.shape[0] // 8
    exchange = Exchange(
        place,
        lambda group: B2.at[pl.ds(pl.multiple_of(group * block, block), block), pl.ds(channel_count, channel_count)],
        lambda group: returned.at[pl.ds(pl.multiple_of(group * block, block), block)],
        x_send, x_recv,
    )

    def send_terms():
        loads["terms"].wait()
        PLACES[...] = ids_ref[...] - (place.f * 4 + place.c) * DB.shape[0]

        @pl.loop(0, chunks)
        def _(part):
            rows = pl.ds(pl.multiple_of(part * chunk_rows, chunk_rows), chunk_rows)
            total = jnp.zeros((chunk_rows, channel_count), jnp.float32)
            for chunk in range(chunks):
                picked = chosen(PLACES[0:1, rows], chunk * chunk_rows, chunk_rows)
                total += dot_tn(picked, B2[chunk * chunk_rows:(chunk + 1) * chunk_rows, 0:channel_count])
            B2[rows, channel_count:2 * channel_count] = total.astype(jnp.bfloat16)

        exchange.start()

    def memory_grads():
        exchange.arrived()
        copy = pltpu.make_async_copy(returned, A2.at[:, pl.ds(0, channel_count)], load_sem.at[0])
        copy.start()
        copy.wait()

        @pl.loop(0, chunks)
        def _(part):
            rows = pl.ds(pl.multiple_of(part * chunk_rows, chunk_rows), chunk_rows)
            total = jnp.zeros((chunk_rows, channel_count), jnp.float32)
            for chunk in range(chunks):
                picked = chosen(rank_ref[0:1, rows], chunk * chunk_rows, chunk_rows)
                total += dot_tn(picked, A2[chunk * chunk_rows:(chunk + 1) * chunk_rows, 0:channel_count])
            GP[...] = total
            store = pltpu.make_async_copy(GP, memory_out.at[rows], gate_sem.at[0])
            store.start()
            store.wait()

    for copy in gate_loads(0):
        copy.start()

    def steps(ends, inside):
        def run(pairs, inner):
            for chunk, step in pairs:
                first_step(chunk, step, inner)

        by_place(place, lambda: run(ends, False), lambda: run(inside, True))

    def events(iteration, late):
        if (iteration, late) == (1, 0):
            gather.step(0, 1)
            gather.step(1, 1)
        if (iteration, late) == (1, 1):
            gather.step(2, 1)
            gather.step(3, 1)
        if (iteration, late) == (2, 1):
            gather.step(0, 2)
            gather.step(1, 2)
        if (iteration, late) == (3, 0):
            gather.step(2, 2)
            gather.step(3, 2)
            need("out_w", "gate_w")
            gather.step(0, 3)
            channels(0)
        if (iteration, late) == (3, 1):
            gather.step(1, 3)
            channels(1)
            steps([(0, 0), (1, 0)], [])
        if (iteration, late) == (4, 0):
            gather.step(2, 3)
            channels(2)
        if (iteration, late) == (4, 1):
            gather.step(3, 3)
            channels(3)
            steps([(2, 0), (3, 0)], [(0, 0), (1, 0)])
        if (iteration, late) == (5, 0):
            steps([(0, 1), (1, 1)], [(2, 0), (3, 0)])
        if (iteration, late) == (5, 1):
            steps([(2, 1), (3, 1)], [(0, 1), (1, 1)])
            term_store(3).wait()
            load("terms", term_out, B2.at[:, pl.ds(0, channel_count)], 4)
        if (iteration, late) == (6, 0):
            send_terms()
            steps([(0, 2), (1, 2)], [(2, 1), (3, 1), (0, 2), (1, 2)])
        if (iteration, late) == (6, 1):
            steps([(2, 2), (3, 2)], [(2, 2), (3, 2)])
        if (iteration, late) == (7, 0):
            own_step(0)
            own_step(1)
        if (iteration, late) == (7, 1):
            own_step(2)
            own_step(3)
            for step in range(1, 4):
                to_line(step, 0).start()
            GV[0, 1:2] = gg2_ref[...]
            sum_copy(0).start()
        if (iteration, late) == (8, 0):
            memory_grads()
        if late and 8 <= iteration < 11:
            step = iteration - 8
            sum_copy(step).wait_recv()
            GV[step + 1] = GV[step] + GR[step]
            if step < 2:
                sum_copy(step + 1).start()
            else:
                for ahead in range(1, 4):
                    to_line(ahead, 1).start()

    GV[0] = jnp.zeros_like(GV[0])
    for iteration in range(JOBS + 2):
        if iteration < JOBS:
            need(*{0: ("cot", "swi"), 2: ("h2", "da"), 4: ("db",), 6: ("mixed",), 7: ("h1",)}.get(iteration, ()))
            to_sibling(iteration)
            to_first(iteration)
        events(iteration, 0)
        if 1 <= iteration <= JOBS:
            to_second(iteration - 1)
        if iteration >= 2:
            to_output(iteration - 2)
            if iteration == 3:
                load("db", db_in, B1, 2)
                load("h1", h1_in, A1, 1)
        events(iteration, 1)
    events(10, 1)

    for step in range(1, 4):
        to_line(step, 0).wait()
        to_line(step, 1).wait()
    SA[t] = SV[...]
    GA[t] = GV[3]
    stats_out[...] = SA[0] + SA[1] + SA[2] + SA[3]
    gains_out[...] = GA[...]
    for chunk in range(4):
        gather.finish(chunk)
        scatter.finish(chunk)
    for step in range(3):
        sum_copy(step).wait_send()
    for slot in range(4):
        sib_copy(JOBS - 1, slot).wait_send()
    for job in (JOBS - 2, JOBS - 1):
        for slot in range(2):
            h1_copy(job, slot).wait_send()
        h2_copy(job).wait_send()
    exchange.finish()
    own_copies(3)[1].wait()
    out_copy(JOBS - 1).wait()


def back_call(branch_own, cot, swi, h2, da, db, mixed, h1, gate, mem, out_w, gate_w, xhat, gain, gg2, rank, ids):
    rows, features = cot.shape
    channels, hidden = mixed.shape[1], swi.shape[1]
    width, slab, part = features // 4, features // 8, rows // 4
    bf, f32 = jnp.bfloat16, jnp.float32
    shape = jax.ShapeDtypeStruct
    anywhere, vmem = pl.BlockSpec(memory_space=pl.ANY), pl.BlockSpec(memory_space=pltpu.VMEM)
    dma = pltpu.SemaphoreType.DMA
    regular = pltpu.SemaphoreType.REGULAR
    V = pltpu.VMEM
    macs = rows * features * (3 * hidden + 4 * channels)
    return pl.pallas_call(
        back_kernel,
        name="backward",
        out_shape=(
            shape((rows, width), f32), shape((rows, channels), f32), shape((rows, channels), bf), shape((rows, channels), bf),
            shape((slab, hidden), f32), shape((slab, hidden), f32),
            shape((slab, hidden), f32), shape((slab, channels), f32), shape((slab, channels), f32), shape((4, 8, width), f32),
            shape((8, rows), f32),
        ),
        in_specs=[anywhere] * 13 + [vmem] * 4,
        out_specs=(anywhere,) * 9 + (vmem,) * 2,
        scratch_shapes=[
            V((rows, features), bf), V((rows, features), bf), V((rows, hidden), bf), V((rows, hidden), bf), V((rows, channels), bf),
            V((rows, features), bf), V((rows, channels), bf), V((channels, features), bf), V((features, channels), bf),
            V((3, 4, slab, channels), bf), V((4, slab, channels), bf), V((2, 2, slab, channels), bf), V((3, 2, slab, channels), bf),
            V((2, slab, channels), bf), V((2, slab, channels), bf), V((slab, channels), f32), V((4, 5, part, width), bf),
            V((part, channels), f32), V((part, channels), bf), V((part, channels), bf), V((part, width), f32), V((part, width), f32),
            V((4, 8, width), f32), V((3, 8, width), f32), V((4, 8, width), f32), V((8, rows), f32), V((4, 8, rows), f32),
            V((8, rows), jnp.int32), dma((8,)), dma((5,)), dma((4, 2, 3)), dma((4, 4)), dma((4, 3)), dma((4, 5)), dma((4,)), dma((JOBS, 4)), dma((2, 2)),
            dma((JOBS, 2)), dma((2,)), dma((JOBS,)), dma, dma((9,)), dma((9,)), dma((8,)), dma((8,)), regular, regular, regular,
        ],
        compiler_params=pltpu.CompilerParams(collective_id=1, has_side_effects=True, vmem_limit_bytes=VMEM_LIMIT),
        cost_estimate=pl.CostEstimate(flops=2 * macs, bytes_accessed=64 * 2**20, transcendentals=rows * channels),
    )(branch_own, cot, swi, h2, da, db, mixed, h1, gate, mem, out_w, gate_w, xhat, gain, gg2, rank, ids)


class Spread:
    def __init__(self, place, index, shard, view, send, recv, local):
        self.place, self.index, self.shard, self.view, self.send, self.recv = place, index, shard, view, send, recv
        self.local = local

    def group(self, *flips):
        f, c = self.place.at(*flips)
        return f * 4 + c

    def copy(self, group, device, slot):
        view = self.view(group)
        source = self.shard if slot < 3 else view
        return remote(source, view, self.send.at[self.index, slot], self.recv.at[self.index, group], device)

    def routes(self):
        place = self.place
        me, both = self.group(0, 0, 0), self.group(1, 1, 0)
        first, second = self.group(1 - place.k, place.k, 0), self.group(place.k, 1 - place.k, 0)
        return (
            (me, place.first()), (me, place.second()), (me, place.sibling()), (second, place.first()), (first, place.sibling()),
            (second, place.sibling()), (both, place.sibling()),
        )

    def start(self, slot):
        group, device = self.routes()[slot]
        self.copy(group, device, slot).start()

    def arrived(self, group):
        self.copy(group, self.place.sibling(), 3).wait_recv()

    def stay(self):
        return pltpu.make_async_copy(self.shard, self.view(self.group(0, 0, 0)), self.local.at[self.index])

    def phase(self, number):
        routes = self.routes()
        if number == 0:
            for slot in range(3):
                self.start(slot)
            self.stay().start()
        if number == 1:
            self.arrived(routes[3][0])
            self.start(3)
            self.start(5)
            self.arrived(routes[4][0])
            self.start(4)
        if number == 2:
            self.arrived(routes[6][0])
            self.start(6)
        if number == 3:
            for flips in ((0, 0), (0, 1), (1, 0), (1, 1)):
                self.arrived(self.group(*flips, 1))
            self.stay().wait()

    def finish(self):
        for slot, (group, device) in enumerate(self.routes()):
            self.copy(group, device, slot).wait_send()


def to_column(row):
    return jnp.broadcast_to(row, (128, row.shape[1])).T[:, 0:1]


def front_kernel(
    tokens, cotangent, mem_in, gate_w, out_w, up_a_w, up_b_w, down_w, gain1, gain2, deal_row, deal_column,
    tok_full, cot_full, h2_full, h1_out, gate_out, mixed_out, swi_out, da_out, db_out, gate_w_out, out_w_out, block_out, dx1_out, branch_out, mem_out,
    inv_out, gg2_out, rank_out, ids_out,
    WG, WO, WA, WB, WD, Z1, ZN, ZE, XC, CC, H1C, GPS, MXS, MT, SWI, DA, DB, X1, H2O, HO, DHQ, FS, BS, OWN, I2, SV, SA, SV2, SA2, SENT,
    load_sem, store_sem, stage_sem, t_send, t_recv, c_send, c_recv, h_send, h_recv, r_send, r_recv, n_send, n_recv, e_send, e_recv,
    w_send, w_recv, w_local, s_send, s_recv, x_send, x_recv, i_send, i_recv,
):
    place = Place()
    t = place.t
    rows, features = tok_full.shape
    chunk_rows, width = HO.shape
    channels, hidden = MXS.shape[2], SWI.shape[2]
    half = channels // 2
    slab = features // 8
    own_columns = pl.ds(pl.multiple_of(t * width, width), width)

    def rows_of(chunk):
        return pl.ds(chunk * chunk_rows, chunk_rows)

    def columns_of(block, size):
        return pl.ds(pl.multiple_of(block * size, size), size)

    def keep(index, source, target):
        return pltpu.make_async_copy(source, target, stage_sem.at[index])

    own_tokens = keep(0, tokens, tok_full.at[:, own_columns])
    own_cot = keep(1, cotangent, cot_full.at[:, own_columns])
    own_tokens.start()
    own_cot.start()
    greet(place)

    tok_gather = Gather(place, tok_full, t_send, t_recv, chunk_rows, width, tokens)
    cot_gather = Gather(place, cot_full, c_send, c_recv, chunk_rows, width, cotangent)
    h2_gather = Gather(place, h2_full, h_send, h_recv, chunk_rows, width, H2O)
    mix_scatter = Scatter(place, Z1, r_send, r_recv)
    down_scatter = Scatter(place, ZN, n_send, n_recv)
    up_scatter = Scatter(place, ZE, e_send, e_recv)
    spreads = [
        Spread(place, index, shard, view, w_send, w_recv, w_local)
        for index, (shard, view) in enumerate((
            (gate_w, lambda group: WG.at[columns_of(group, slab), :]),
            (out_w, lambda group: WO.at[:, columns_of(group, slab)]),
            (up_a_w, lambda group: WA.at[columns_of(group, slab), :]),
            (up_b_w, lambda group: WB.at[columns_of(group, slab), :]),
            (down_w, lambda group: WD.at[:, columns_of(group, slab)]),
        ))
    ]

    block = rows // 8

    def quarter(ref, index):
        return ref.at[index // 2, :, pl.ds(pl.multiple_of((index % 2) * channels, channels), channels)]

    def eighth(ref, group):
        return ref.at[
            group // 4, pl.ds(pl.multiple_of((group % 2) * block, block), block),
            pl.ds(pl.multiple_of(((group // 2) % 2) * channels, channels), channels),
        ]

    def lanes(ref, group):
        return ref.at[:, pl.ds(pl.multiple_of(group * block, block), block)]

    rows_exchange = Exchange(place, lambda group: eighth(DA, group), lambda group: eighth(SWI, group), x_send, x_recv)
    ids_exchange = Exchange(place, lambda group: lanes(SENT, group), lambda group: lanes(ids_out, group), i_send, i_recv)

    def send_rows():
        loads = [pltpu.make_async_copy(mem_in.at[rows_of(index)], quarter(DB, index), load_sem.at[4 + index]) for index in range(4)]
        for copy in loads:
            copy.start()
        row = deal_row[...]
        rank = jnp.zeros((1, rows), jnp.float32)
        for chunk in range(4):
            rank += jnp.sum(jnp.where(deal_column[rows_of(chunk)] < row, 1.0, 0.0), axis=0, keepdims=True)
        rank_out[...] = jnp.broadcast_to(rank, (8, rows)).astype(jnp.int32)
        spots = lax.broadcasted_iota(jnp.int32, (chunk_rows, rows), 1).astype(jnp.float32)
        ordered = jnp.zeros((1, rows), jnp.float32)
        for chunk in range(4):
            column = deal_column[rows_of(chunk)]
            place_of = jnp.sum(jnp.where(row < column, 1.0, 0.0), axis=1, keepdims=True)
            ordered += jnp.sum(jnp.where(place_of == spots, column.astype(jnp.float32), 0.0), axis=0, keepdims=True)
        SENT[...] = jnp.broadcast_to(ordered, (8, rows)).astype(jnp.int32)
        ids_exchange.start()
        for copy in loads:
            copy.wait()

        @pl.loop(0, 4)
        def _(index):
            total = jnp.zeros((chunk_rows, channels), jnp.float32)
            for other in range(4):
                picked = chosen(rank_out[0:1, rows_of(other)], index * chunk_rows, chunk_rows)
                total += jnp.dot(picked, quarter(DB, other)[...], preferred_element_type=jnp.float32)
            quarter(DA, index)[...] = total.astype(jnp.bfloat16)

        rows_exchange.start()

    def mem_store(chunk):
        return pltpu.make_async_copy(MT, mem_out.at[rows_of(chunk)], load_sem.at[0])

    def take_rows(chunk):
        if chunk == 0:
            ids_exchange.arrived()
            rows_exchange.arrived()
        else:
            mem_store(chunk - 1).wait()
        total = jnp.zeros((chunk_rows, channels), jnp.float32)
        first = rows_exchange.me * rows + chunk * chunk_rows
        for other in range(4):
            picked = chosen(ids_out[0:1, rows_of(other)], first, chunk_rows)
            total += jnp.dot(picked, quarter(SWI, other)[...], preferred_element_type=jnp.float32)
        MT[...] = total.astype(jnp.bfloat16)
        mem_store(chunk).start()

    def h1_store(chunk):
        return pltpu.make_async_copy(H1C, h1_out.at[rows_of(chunk)], store_sem.at[0])

    def gate_store(chunk):
        return pltpu.make_async_copy(GPS, gate_out.at[rows_of(chunk)], store_sem.at[1])

    def mixed_store(chunk):
        return pltpu.make_async_copy(MXS.at[chunk % 2], mixed_out.at[rows_of(chunk)], store_sem.at[2 + chunk % 2])

    def hidden_stores(chunk):
        slot = chunk % 2
        return [
            pltpu.make_async_copy(source.at[slot], target.at[rows_of(chunk)], store_sem.at[4 + 2 * index + slot])
            for index, (source, target) in enumerate(((SWI, swi_out), (DA, da_out), (DB, db_out)))
        ]

    def own_h2_store(chunk):
        return pltpu.make_async_copy(H2O.at[rows_of(chunk)], h2_full.at[rows_of(chunk), own_columns], stage_sem.at[4 + chunk])

    def small_store(source, target, chunk, index):
        return pltpu.make_async_copy(source, target.at[rows_of(chunk)], store_sem.at[index])

    def fetch(source, target, index):
        copy = pltpu.make_async_copy(source, target, load_sem.at[index])
        copy.start()
        return copy

    def stat_copy(chunk, step, which):
        source, target = ((SV, SA), (SV2, SA2))[which]
        columns = rows_of(chunk)
        return remote(
            source.at[:, columns], target.at[t, :, columns], s_send.at[which, chunk, step - 1], s_recv.at[which, chunk, step - 1],
            place.along((t + step) % 4),
        )

    def stats(chunk, which):
        source, target = ((SV, SA), (SV2, SA2))[which]
        for step in range(1, 4):
            stat_copy(chunk, step, which).wait_recv()
        total = source[0:1, rows_of(chunk)]
        for step in range(1, 4):
            total = total + target[(t + step) % 4, 0:1, rows_of(chunk)]
        return to_column(total)

    def memory_unit(chunk):
        if chunk == 0:
            own_tokens.wait()
        load = fetch(tok_full.at[rows_of(chunk)], XC, 1)
        if chunk > 0:
            h1_store(chunk - 1).wait()
        load.wait()
        square = jnp.zeros((chunk_rows, 1), jnp.float32)
        for block in range(4):
            values = XC[:, block * width:(block + 1) * width].astype(jnp.float32)
            square += jnp.sum(values * values, axis=1, keepdims=True)
        inverse = lax.rsqrt(square / features + EPS)
        inv_out[rows_of(chunk)] = inverse
        for block in range(4):
            at = slice(block * width, (block + 1) * width)
            H1C[:, at] = (XC[:, at].astype(jnp.float32) * inverse * gain1[:, at]).astype(jnp.bfloat16)
        h1_store(chunk).start()
        take_rows(chunk)
        if chunk > 0:
            gate_store(chunk - 1).wait()
        if chunk > 1:
            mixed_store(chunk - 2).wait()

        @pl.loop(0, 2)
        def _(part):
            at = columns_of(part, half)
            pre = jnp.dot(H1C[...], WG[:, at], preferred_element_type=jnp.float32)
            GPS[:, at] = pre
            MXS[chunk % 2, :, at] = (MT[:, at].astype(jnp.float32) * (pre * jax.nn.sigmoid(pre))).astype(jnp.bfloat16)

        gate_store(chunk).start()
        mixed_store(chunk).start()

    def mix_part(chunk, block):
        return jnp.dot(MXS[chunk % 2], WO[:, columns_of(block, width)], preferred_element_type=jnp.float32)

    def mix_own(chunk):
        load = fetch(tokens.at[rows_of(chunk)], OWN, 2)
        HO[...] = mix_part(chunk, t)
        mix_scatter.own(chunk, HO)
        load.wait()
        middle = OWN[...].astype(jnp.float32) + HO[...]
        X1[rows_of(chunk)] = middle
        H2O[rows_of(chunk)] = (middle * gain2[...]).astype(jnp.bfloat16)
        own_h2_store(chunk).start()
        SV[:, rows_of(chunk)] = to_row(jnp.sum(middle * middle, axis=1, keepdims=True))
        mix_scatter.finish(chunk)
        h2_gather.step(chunk, 0)
        for step in range(1, 4):
            stat_copy(chunk, step, 0).start()

    def feed_forward(chunk):
        own_h2_store(chunk).wait()
        if chunk == 0:
            own_cot.wait()
        loads = [fetch(h2_full.at[rows_of(chunk)], XC, 1), fetch(cot_full.at[rows_of(chunk)], CC, 3)]
        inverse = lax.rsqrt(stats(chunk, 0) / features + EPS)
        I2[rows_of(chunk)] = inverse
        if chunk > 1:
            for store in hidden_stores(chunk - 2):
                store.wait()
        for load in loads:
            load.wait()

        @pl.loop(0, 4)
        def _(part):
            at = columns_of(part, hidden // 4)
            up_a = jnp.dot(XC[...], WA[:, at], preferred_element_type=jnp.float32) * inverse
            up_b = jnp.dot(XC[...], WB[:, at], preferred_element_type=jnp.float32) * inverse
            d_swi = dot_nt(CC[...], WD[at, :])
            sigma = jax.nn.sigmoid(up_a)
            swish = up_a * sigma
            SWI[chunk % 2, :, at] = (swish * up_b).astype(jnp.bfloat16)
            d_swi = d_swi * inverse
            DA[chunk % 2, :, at] = (d_swi * up_b * (sigma * (1.0 + up_a * (1.0 - sigma)))).astype(jnp.bfloat16)
            DB[chunk % 2, :, at] = (d_swi * swish).astype(jnp.bfloat16)

        for store in hidden_stores(chunk):
            store.start()

    def down_part(chunk, block):
        return jnp.dot(SWI[chunk % 2], WD[:, columns_of(block, width)], preferred_element_type=jnp.float32)

    def up_part(chunk, block):
        at = columns_of(block, width)
        return dot_nt(DA[chunk % 2], WA[at, :]) + dot_nt(DB[chunk % 2], WB[at, :])

    def hidden_own(chunk):
        if chunk > 0:
            small_store(BS.at[0], block_out, chunk - 1, 10).wait()
        HO[...] = up_part(chunk, t)
        up_scatter.own(chunk, HO)
        middle = X1[rows_of(chunk)]
        d_second = HO[...]
        grads = jnp.sum(d_second * middle, axis=0, keepdims=True)
        if chunk == 0:
            gg2_out[...] = grads
        else:
            gg2_out[...] += grads
        scaled = d_second * gain2[...]
        DHQ[...] = scaled
        SV2[:, rows_of(chunk)] = to_row(jnp.sum(scaled * middle, axis=1, keepdims=True) * I2[rows_of(chunk)])
        HO[...] = down_part(chunk, t)
        down_scatter.own(chunk, HO)
        BS[0] = (middle + HO[...]).astype(jnp.bfloat16)
        small_store(BS.at[0], block_out, chunk, 10).start()
        up_scatter.finish(chunk)
        down_scatter.finish(chunk)
        for step in range(1, 4):
            stat_copy(chunk, step, 1).start()

    def close(chunk):
        load = fetch(cotangent.at[rows_of(chunk)], OWN, 2)
        mean = stats(chunk, 1) / features
        if chunk > 0:
            small_store(FS, dx1_out, chunk - 1, 11).wait()
            small_store(BS.at[1], branch_out, chunk - 1, 12).wait()
        load.wait()
        unit = X1[rows_of(chunk)] * I2[rows_of(chunk)]
        total = OWN[...].astype(jnp.float32) + DHQ[...] - unit * mean
        FS[...] = total
        BS[1] = total.astype(jnp.bfloat16)
        small_store(FS, dx1_out, chunk, 11).start()
        small_store(BS.at[1], branch_out, chunk, 12).start()

    def mix_steps(chunk, ends, inside):
        def run(steps, inner):
            for step in steps:
                mix_scatter.step(chunk, step, lambda block: mix_part(chunk, block), inner)

        by_place(place, lambda: run(ends, False), lambda: run(inside, True))

    def hidden_steps(chunk, ends, inside):
        def run(steps, inner):
            for step in steps:
                up_scatter.step(chunk, step, lambda block: up_part(chunk, block), inner)
                down_scatter.step(chunk, step, lambda block: down_part(chunk, block), inner)

        by_place(place, lambda: run(ends, False), lambda: run(inside, True))

    def pumps(turn):
        for index, number in {
            0: ((0, 0),), 1: ((0, 1), (1, 0)), 2: ((0, 2), (1, 1)), 3: ((0, 3), (1, 2), (2, 0), (1, 3)), 5: ((2, 1), (3, 0)),
            6: ((2, 2),), 7: ((2, 3), (3, 1), (4, 0)), 8: ((3, 2),), 9: ((3, 3), (4, 1), (4, 2), (4, 3)),
        }.get(turn, ()):
            spreads[index].phase(number)

    def hops(chunk, event):
        if event in (0, 1, 2):
            tok_gather.step(chunk, event)
        if event in (3, 4, 5, 6):
            cot_gather.step(chunk, event - 3)
        if event in (7, 8):
            h2_gather.step(chunk, event - 6)
        if event == 13:
            close(chunk)

    def light(chunk, event):
        if event == 4:
            mix_steps(chunk, (1,), (0,))
        if event == 5:
            mix_steps(chunk, (2,), (1, 2))
        if event == 6:
            mix_own(chunk)
        if event == 10:
            hidden_steps(chunk, (1,), (0,))
        if event == 11:
            hidden_steps(chunk, (2,), (1, 2))
        if event == 12:
            hidden_own(chunk)

    def heavy(chunk, event):
        if event == 3:
            tok_gather.step(chunk, 3)
            memory_unit(chunk)
            mix_steps(chunk, (0,), ())
        if event == 9:
            h2_gather.step(chunk, 3)
            feed_forward(chunk)
            hidden_steps(chunk, (0,), ())

    weight_stores = [
        pltpu.make_async_copy(WG, gate_w_out, stage_sem.at[2]), pltpu.make_async_copy(WO, out_w_out, stage_sem.at[3]),
    ]
    for turn in range(20):
        pumps(turn)
        if turn == 9:
            rows_exchange.finish()
            ids_exchange.finish()
        if turn == 3:
            for store in weight_stores:
                store.start()
        for action in (hops, light, heavy):
            for chunk in range(4) if action is not heavy else (3, 2, 1, 0):
                action(chunk, turn - 2 * chunk)
        if turn == 0:
            send_rows()

    for store in weight_stores:
        store.wait()
    for spread in spreads:
        spread.finish()
    for chunk in range(4):
        for gather in (tok_gather, cot_gather, h2_gather):
            gather.finish(chunk)
        for which in range(2):
            for step in range(1, 4):
                stat_copy(chunk, step, which).wait_send()
    mem_store(3).wait()
    h1_store(3).wait()
    gate_store(3).wait()
    for chunk in (2, 3):
        mixed_store(chunk).wait()
        for store in hidden_stores(chunk):
            store.wait()
    small_store(BS.at[0], block_out, 3, 10).wait()
    small_store(FS, dx1_out, 3, 11).wait()
    small_store(BS.at[1], branch_out, 3, 12).wait()


def front_call(tokens, cotangent, mem, gate_w, out_w, up_a_w, up_b_w, down_w, gain1, gain2, deal_row, deal_column):
    rows, width = tokens.shape
    features, channels, hidden = 4 * width, mem.shape[1], up_a_w.shape[1]
    part = rows // 4
    bf, f32 = jnp.bfloat16, jnp.float32
    shape = jax.ShapeDtypeStruct
    anywhere, vmem = pl.BlockSpec(memory_space=pl.ANY), pl.BlockSpec(memory_space=pltpu.VMEM)
    dma = pltpu.SemaphoreType.DMA
    V = pltpu.VMEM
    macs = rows * features * (6 * hidden + 2 * channels)
    return pl.pallas_call(
        front_kernel,
        name="forward",
        out_shape=(
            shape((rows, features), bf), shape((rows, features), bf), shape((rows, features), bf), shape((rows, features), bf),
            shape((rows, channels), f32), shape((rows, channels), bf), shape((rows, hidden), bf), shape((rows, hidden), bf),
            shape((rows, hidden), bf), shape((features, channels), bf), shape((channels, features), bf), shape((rows, width), bf),
            shape((rows, width), f32), shape((rows, width), bf), shape((rows, channels), bf), shape((rows, 1), f32), shape((1, width), f32),
            shape((8, rows), jnp.int32), shape((8, rows), jnp.int32),
        ),
        in_specs=[anywhere] * 8 + [vmem] * 4,
        out_specs=(anywhere,) * 15 + (vmem,) * 4,
        scratch_shapes=[
            V((features, channels), bf), V((channels, features), bf), V((features, hidden), bf), V((features, hidden), bf),
            V((hidden, features), bf), V((2, 5, part, width), bf), V((2, 5, part, width), bf), V((2, 5, part, width), bf),
            V((part, features), bf), V((part, features), bf), V((part, features), bf), V((part, channels), f32), V((2, part, channels), bf),
            V((part, channels), bf), V((2, part, hidden), bf), V((2, part, hidden), bf), V((2, part, hidden), bf), V((rows, width), f32),
            V((rows, width), bf), V((part, width), f32), V((part, width), f32), V((part, width), f32), V((2, part, width), bf),
            V((part, width), bf), V((rows, 1), f32), V((8, rows), f32), V((4, 8, rows), f32), V((8, rows), f32), V((4, 8, rows), f32),
            V((8, rows), jnp.int32), dma((8,)), dma((13,)), dma((8,)), dma((4, 2, 3)), dma((4, 4)), dma((4, 2, 3)), dma((4, 4)), dma((4, 2, 3)), dma((4, 4)),
            dma((4, 3)), dma((4, 5)), dma((4, 3)), dma((4, 5)), dma((4, 3)), dma((4, 5)), dma((5, 7)), dma((5, 8)), dma((5,)),
            dma((2, 4, 3)), dma((2, 4, 3)), dma((8,)), dma((8,)), dma((8,)), dma((8,)),
        ],
        compiler_params=pltpu.CompilerParams(collective_id=2, has_side_effects=True, vmem_limit_bytes=VMEM_LIMIT),
        cost_estimate=pl.CostEstimate(flops=2 * macs, bytes_accessed=96 * 2**20, transcendentals=rows * (channels + hidden)),
    )(tokens, cotangent, mem, gate_w, out_w, up_a_w, up_b_w, down_w, gain1, gain2, deal_row, deal_column)


def silu_grad(values):
    sigma = jax.nn.sigmoid(values)
    return sigma * (1.0 + values * (1.0 - sigma))


def normalize(values):
    inverse = lax.rsqrt(jnp.mean(values * values, axis=-1, keepdims=True) + EPS)
    return (values * inverse, inverse)


def contract_rows(left, right):
    return lax.dot_general(
        left, right, (((0,), (0,)), ((), ())), preferred_element_type=jnp.float32
    )


def contract_cols(left, right):
    return lax.dot_general(
        left, right, (((1,), (1,)), ((), ())), preferred_element_type=jnp.float32
    )


def sum_scatter(part):
    return lax.psum_scatter(
        part.astype(jnp.bfloat16), "tp", scatter_dimension=1, tiled=True
    ).astype(jnp.float32)


def mean_over(values, features):
    return lax.psum(jnp.sum(values, axis=-1, keepdims=True), "tp") / features


def grad_scatter(part, dimension):
    return lax.psum_scatter(
        part.astype(jnp.bfloat16), ("fsdp", "ctx"), scatter_dimension=dimension, tiled=True
    ).astype(jnp.float32)


def middle_of(tokens, memory_tokens, cotangent, gain_first, gain_second, memory_gate, memory_out, hidden_gate, hidden_up, hidden_down):
    memory_f = memory_tokens.astype(jnp.float32)
    gathered = (
        lax.all_gather(memory_gate, ("fsdp", "ctx"), axis=0, tiled=True),
        lax.all_gather(memory_out, ("fsdp", "ctx"), axis=1, tiled=True),
        lax.all_gather(hidden_gate, ("fsdp", "ctx"), axis=0, tiled=True),
        lax.all_gather(hidden_up, ("fsdp", "ctx"), axis=0, tiled=True),
        lax.all_gather(hidden_down, ("fsdp", "ctx"), axis=1, tiled=True),
    )
    gate_w, out_w, up_a_w, up_b_w, down_w = gathered
    width = tokens.shape[1]
    column = lax.axis_index("tp") * width
    full_tokens, full_cot = (
        lax.all_gather(tokens, "tp", axis=1, tiled=True),
        lax.all_gather(cotangent, "tp", axis=1, tiled=True),
    )
    inputs = full_tokens.astype(jnp.float32)
    unit_first, inv_first = normalize(inputs)
    first = (unit_first * gain_first).astype(jnp.bfloat16)
    gate_pre = jnp.dot(first, gate_w, preferred_element_type=jnp.float32)
    activated = jax.nn.silu(gate_pre)
    mixed = (memory_f * activated).astype(jnp.bfloat16)
    features = full_tokens.shape[1]
    own = lambda array: lax.dynamic_slice_in_dim(array, column, width, array.ndim - 1)
    gain_one, gain_two = own(gain_first), own(gain_second)
    shard_tokens = tokens.astype(jnp.float32)
    middle = shard_tokens + sum_scatter(jnp.dot(mixed, out_w, preferred_element_type=jnp.float32))
    inv_second = lax.rsqrt(mean_over(middle * middle, features) + EPS)
    unit_second = middle * inv_second
    second = lax.all_gather((unit_second * gain_two).astype(jnp.bfloat16), "tp", axis=1, tiled=True)
    up_a = jnp.dot(second, up_a_w, preferred_element_type=jnp.float32)
    up_b = jnp.dot(second, up_b_w, preferred_element_type=jnp.float32)
    swish_a = jax.nn.silu(up_a)
    swished = (swish_a * up_b).astype(jnp.bfloat16)
    output = middle + sum_scatter(jnp.dot(swished, down_w, preferred_element_type=jnp.float32))
    block_out = output.astype(jnp.bfloat16)
    d_swished = contract_cols(full_cot, down_w)
    d_a = (d_swished * up_b * silu_grad(up_a)).astype(jnp.bfloat16)
    d_b = (d_swished * swish_a).astype(jnp.bfloat16)
    d_second = sum_scatter(contract_cols(d_a, up_a_w) + contract_cols(d_b, up_b_w))
    scaled = d_second * gain_two
    middle_norm = inv_second * (scaled - unit_second * mean_over(scaled * unit_second, features))
    gain_two_part = jnp.sum(d_second * unit_second, axis=0)
    d_middle = cotangent.astype(jnp.float32) + middle_norm
    unit_own = shard_tokens * inv_first
    d_branch = lax.all_gather(d_middle.astype(jnp.bfloat16), "tp", axis=1, tiled=True)
    d_mixed = contract_cols(d_branch, out_w)
    back = (d_mixed * activated).astype(jnp.bfloat16)
    d_gate = (d_mixed * memory_f * silu_grad(gate_pre)).astype(jnp.bfloat16)
    d_first = sum_scatter(contract_cols(d_gate, gate_w))
    scaled = d_first * gain_one
    input_norm = inv_first * (scaled - unit_own * mean_over(scaled * unit_own, features))
    gain_one_part = jnp.sum(d_first * unit_own, axis=0)
    parts = lax.psum(jnp.stack([gain_one_part, gain_two_part]), ("fsdp", "ctx"))
    gains = lax.all_gather(parts, "tp", axis=1, tiled=True)
    grad_gain_first, grad_gain_second = gains[0], gains[1]
    sums = (
        grad_scatter(contract_rows(first, d_gate), 0),
        grad_scatter(contract_rows(mixed, d_branch), 1),
        grad_scatter(contract_rows(second, d_a), 0),
        grad_scatter(contract_rows(second, d_b), 0),
        grad_scatter(contract_rows(swished, full_cot), 1),
    )
    return block_out, d_middle, input_norm, back, grad_gain_first, grad_gain_second, sums


def middle_on_line(
    tokens, memory, dealing, cotangent, gain_first, gain_second, memory_gate, memory_out, hidden_gate, hidden_up, hidden_down
):
    width = tokens.shape[1]
    features = 4 * width
    own = lambda array: lax.dynamic_slice_in_dim(array, lax.axis_index("tp") * width, width, 0)[None]
    gain_one, gain_two = own(gain_first), own(gain_second)
    (
        _, full_cot, second, first, gate_pre, mixed, swished, d_a, d_b, gate_w, out_w, block_out, d_middle, d_branch, memory_tokens,
        inv_first, gain_two_part, rank, ids,
    ) = front_call(
        tokens, cotangent, memory, memory_gate, memory_out, hidden_gate, hidden_up, hidden_down, gain_first[None], gain_two,
        dealing[None], dealing[:, None],
    )
    unit_own = tokens.astype(jnp.float32) * inv_first
    d_first, grad_memory, _, _, grad_down, grad_up_a, grad_up_b, grad_out, grad_gate, gains, stats = back_call(
        d_branch, full_cot, swished, second, d_a, d_b, mixed, first, gate_pre, memory_tokens, out_w, gate_w, unit_own, gain_one,
        gain_two_part, rank, ids,
    )
    grad_inputs = d_middle + inv_first * (d_first * gain_one - unit_own * (stats[0][:, None] / features))
    return (
        block_out, grad_inputs, grad_memory, gains[:, 0].reshape(features), gains[:, 1].reshape(features), grad_gate, grad_out.T,
        grad_up_a, grad_up_b, grad_down.T,
    )


def shards(
    tokens,
    memory,
    dealing,
    cotangent,
    gain_first,
    gain_second,
    memory_gate,
    memory_out,
    hidden_gate,
    hidden_up,
    hidden_down,
):
    if lax.axis_size("fsdp") == 2 and lax.axis_size("ctx") == 4 and lax.axis_size("tp") == 4:
        return middle_on_line(
            tokens, memory, dealing, cotangent, gain_first, gain_second, memory_gate, memory_out, hidden_gate, hidden_up, hidden_down
        )
    groups = lax.axis_size(("fsdp", "ctx"))
    group_index = lax.axis_index(("fsdp", "ctx"))
    rows = dealing.shape[0]
    block = rows // groups
    order = jnp.argsort(dealing)
    sent_rows = memory[order].reshape(groups, block, memory.shape[1])
    arrived = lax.all_to_all(sent_rows, ("fsdp", "ctx"), split_axis=0, concat_axis=0, tiled=True)
    arrived_ids = lax.all_to_all(
        dealing[order].reshape(groups, block),
        ("fsdp", "ctx"),
        split_axis=0,
        concat_axis=0,
        tiled=True,
    )
    places = arrived_ids.reshape(rows) - group_index * rows
    memory_tokens = arrived.reshape(rows, memory.shape[1])[jnp.argsort(places)]
    block_out, d_middle, input_norm, back, grad_gain_first, grad_gain_second, sums = middle_of(
        tokens, memory_tokens, cotangent, gain_first, gain_second, memory_gate, memory_out, hidden_gate, hidden_up, hidden_down
    )
    grad_inputs = d_middle + input_norm
    back_rows = back[places].reshape(groups, block, memory.shape[1])
    returned = lax.all_to_all(back_rows, ("fsdp", "ctx"), split_axis=0, concat_axis=0, tiled=True)
    grad_memory = returned.reshape(rows, memory.shape[1])[jnp.argsort(order)].astype(jnp.float32)
    return (
        block_out,
        grad_inputs,
        grad_memory,
        grad_gain_first,
        grad_gain_second,
        sums[0],
        sums[1],
        sums[2],
        sums[3],
        sums[4],
    )


def solution(mesh):
    in_specs = (
        P(("fsdp", "ctx"), "tp"),
        P(("fsdp", "ctx"), "tp"),
        P(("fsdp", "ctx")),
        P(("fsdp", "ctx"), "tp"),
        P(),
        P(),
        P(("fsdp", "ctx"), "tp"),
        P("tp", ("fsdp", "ctx")),
        P(("fsdp", "ctx"), "tp"),
        P(("fsdp", "ctx"), "tp"),
        P("tp", ("fsdp", "ctx")),
    )
    out_specs = (
        P(("fsdp", "ctx"), "tp"),
        P(("fsdp", "ctx"), "tp"),
        P(("fsdp", "ctx"), "tp"),
        P(),
        P(),
        P(("fsdp", "ctx"), "tp"),
        P("tp", ("fsdp", "ctx")),
        P(("fsdp", "ctx"), "tp"),
        P(("fsdp", "ctx"), "tp"),
        P("tp", ("fsdp", "ctx")),
    )
    return jax.shard_map(shards, mesh=mesh, in_specs=in_specs, out_specs=out_specs, check_vma=False)
```

```python
import functools

import jax
import jax.numpy as jnp
from jax import lax
from jax.experimental import pallas as pl
from jax.experimental.pallas import tpu as pltpu
from jax.sharding import PartitionSpec as P

EPS = 1e-06
VMEM_LIMIT = 62 * 2**20


MESH = pl.DeviceIdType.MESH
JOBS = 8


def dot_nt(left, right):
    return lax.dot_general(left, right, (((1,), (1,)), ((), ())), preferred_element_type=jnp.float32)


def dot_tn(left, right):
    return lax.dot_general(left, right, (((0,), (0,)), ((), ())), preferred_element_type=jnp.float32)


class Place:
    def __init__(self):
        self.f, self.c, self.t = lax.axis_index("fsdp"), lax.axis_index("ctx"), lax.axis_index("tp")
        self.y, self.k = self.c // 2, self.c % 2

    def at(self, flip_f, flip_y, flip_k):
        f = self.f + flip_f * (1 - 2 * self.f)
        y = self.y + flip_y * (1 - 2 * self.y)
        k = self.k + flip_k * (1 - 2 * self.k)
        return f, y * 2 + k

    def sibling(self):
        return (*self.at(0, 0, 1), self.t)

    def first(self):
        return (*self.at(1 - self.k, self.k, 0), self.t)

    def second(self):
        return (*self.at(self.k, 1 - self.k, 0), self.t)

    def along(self, t):
        return (self.f, self.c, t)

    def owner(self, slot, flip_k):
        alpha, beta = 1 - slot // 2, 1 - slot % 2
        parity = self.k + flip_k * (1 - 2 * self.k)
        f, c = self.at(alpha * (1 - parity) + beta * parity, beta * (1 - parity) + alpha * parity, flip_k)
        return f * 4 + c


def remote(source, target, send, recv, device):
    return pltpu.make_async_remote_copy(
        src_ref=source, dst_ref=target, send_sem=send, recv_sem=recv, device_id=device, device_id_type=MESH
    )


OTHERS = ((1, 1, 1), (1, 1, 0), (0, 1, 1), (1, 0, 1), (0, 1, 0), (1, 0, 0), (0, 0, 1))


def greet(place):
    barrier = pltpu.get_barrier_semaphore()
    for flips in OTHERS:
        pl.semaphore_signal(barrier, inc=1, device_id=(*place.at(*flips), place.t), device_id_type=MESH)
    for step in range(1, 4):
        pl.semaphore_signal(barrier, inc=1, device_id=place.along((place.t + step) % 4), device_id_type=MESH)
    pl.semaphore_wait(barrier, 10)


class Exchange:
    def __init__(self, place, source, target, send, recv):
        self.place, self.source, self.target, self.send, self.recv = place, source, target, send, recv
        self.me = place.f * 4 + place.c

    def copy(self, index):
        f, c = self.place.at(*OTHERS[index])
        group = f * 4 + c
        out = remote(self.source(group), self.target(self.me), self.send.at[index], self.recv.at[self.me], (f, c, self.place.t))
        back = remote(self.source(group), self.target(group), self.send.at[index], self.recv.at[group], (f, c, self.place.t))
        return out, back

    def stay(self):
        return pltpu.make_async_copy(self.source(self.me), self.target(self.me), self.send.at[7])

    def start(self):
        for index in range(7):
            self.copy(index)[0].start()
        self.stay().start()

    def arrived(self):
        for index in range(7):
            self.copy(index)[1].wait_recv()
        self.stay().wait()

    def finish(self):
        for index in range(7):
            self.copy(index)[0].wait_send()


def chosen(row, first, count):
    places = lax.broadcasted_iota(jnp.int32, (count, row.shape[1]), 0) + first
    return jnp.where(row == places, 1.0, 0.0).astype(jnp.bfloat16)


class Gather:
    def __init__(self, place, full, send, recv, rows, width, own=None):
        self.place, self.full, self.send, self.recv, self.rows, self.width, self.mine = place, full, send, recv, rows, width, own

    def copy(self, chunk, shard, way, hop):
        view = self.full.at[pl.ds(chunk * self.rows, self.rows), pl.ds(pl.multiple_of(shard * self.width, self.width), self.width)]
        device = self.place.along(self.place.t + 1 - 2 * way)
        source = view if hop > 0 or self.mine is None else self.mine.at[pl.ds(chunk * self.rows, self.rows)]
        return remote(source, view, self.send.at[chunk, way, hop], self.recv.at[chunk, shard], device)

    def step(self, chunk, hop):
        t = self.place.t

        @pl.when(t - hop >= 0)
        def _():
            if hop > 0:
                self.copy(chunk, t - hop, 0, hop).wait_recv()
            if hop < 3:
                @pl.when(t < 3)
                def _():
                    self.copy(chunk, t - hop, 0, hop).start()

        @pl.when(t + hop <= 3)
        def _():
            if hop > 0:
                self.copy(chunk, t + hop, 1, hop).wait_recv()
            if hop < 3:
                @pl.when(t > 0)
                def _():
                    self.copy(chunk, t + hop, 1, hop).start()

    def finish(self, chunk):
        t = self.place.t
        for hop in range(3):
            @pl.when((t - hop >= 0) & (t < 3))
            def _():
                self.copy(chunk, t - hop, 0, hop).wait_send()

            @pl.when((t + hop <= 3) & (t > 0))
            def _():
                self.copy(chunk, t + hop, 1, hop).wait_send()


class Scatter:
    def __init__(self, place, slots, send, recv):
        self.place, self.slots, self.send, self.recv = place, slots, send, recv
        self.ring = slots.shape[0]

    def block(self, step):
        t = self.place.t
        low, high = t % 2, t // 2
        return (3 * (1 - high), 2 - 2 * low + high, 1 + low, t)[step]

    def copy(self, chunk, step):
        t, block, ring = self.place.t, self.block(step), chunk % self.ring
        up = (block > t).astype(jnp.int32)
        last_down = (block == t - 1).astype(jnp.int32)
        slot = block + last_down * (4 - block)
        device = self.place.along(t - 1 + 2 * up)
        return remote(self.slots.at[ring, block], self.slots.at[ring, slot], self.send.at[chunk, step], self.recv.at[chunk, slot], device)

    def arrived(self, chunk, slot):
        view = self.slots.at[chunk % self.ring, slot]
        remote(view, view, self.send.at[chunk, 0], self.recv.at[chunk, slot], self.place.along(self.place.t)).wait_recv()

    def step(self, chunk, step, part, inside):
        block, ring = self.block(step), chunk % self.ring
        value = part(block)
        if inside:
            self.arrived(chunk, block)
            value += self.slots[ring, block].astype(jnp.float32)
        self.slots[ring, block] = value.astype(jnp.bfloat16)
        self.copy(chunk, step).start()

    def own(self, chunk, held):
        t, ring = self.place.t, chunk % self.ring

        @pl.when(t > 0)
        def _():
            self.arrived(chunk, t)
            held[...] += self.slots[ring, t].astype(jnp.float32)

        @pl.when(t < 3)
        def _():
            self.arrived(chunk, 4)
            held[...] += self.slots[ring, 4].astype(jnp.float32)

    def finish(self, chunk):
        for step in range(3):
            self.copy(chunk, step).wait_send()


def by_place(place, ends, inside):
    is_end = (place.t == 0) | (place.t == 3)
    pl.when(is_end)(ends)
    pl.when(jnp.logical_not(is_end))(inside)


def to_row(column):
    return jnp.broadcast_to(column, (column.shape[0], 128)).T[:8]


def back_kernel(
    branch_own, cot_in, swi_in, h2_in, da_in, db_in, mixed_in, h1_in, gate_in, mem_in, out_w_in, gate_w_in, xhat_in, gain_ref, gg2_ref, rank_ref, ids_ref, down_in,
    dh1_out, down_out, memory_out, term_out, returned, hd_out, hg_out, hu_out, mo_out, mg_out, gains_out, stats_out,
    A1, A2, B1, B2, MX, DB, DG, WO, WG, SR, SS, H1S, H1R, H2S, H2R, OS, RZ, GP, MT, XH, HO, GV, GR, GA, SV, SA, PLACES, ZN, NS, NO,
    load_sem, gate_sem, ag_send, ag_recv, rs_send, rs_recv, sib_send, sib_recv, h1_send, h1_recv, h2_send, h2_recv,
    out_sem, small_send, small_recv, x_send, x_recv, n_send, n_recv, n_load, n_free, sib_free, first_free, second_free,
):
    place = Place()
    t = place.t
    chunk_rows, width = XH.shape
    slab = OS.shape[0]
    span = OS.shape[1]
    cols = span // 2
    chunks = 4

    loads = {}

    def load(name, source, target, slot):
        loads[name] = pltpu.make_async_copy(source, target, load_sem.at[slot])
        loads[name].start()

    def need(*names):
        for name in names:
            if name in loads:
                loads.pop(name).wait()

    own_columns = pl.ds(pl.multiple_of(t * width, width), width)
    load("branch", branch_own, DB.at[:, own_columns], 0)
    load("cot", cot_in, A1, 1)
    load("swi", swi_in, B1, 2)
    greet(place)

    gather = Gather(place, DB, ag_send, ag_recv, chunk_rows, width)
    scatter = Scatter(place, RZ, rs_send, rs_recv)
    need("branch")

    jobs = [
        (A1, B1, 0, hd_out, 0), (A1, B1, span, hd_out, span), (A2, B2, 0, hg_out, 0), (A2, B2, span, hg_out, span),
        (A2, B1, 0, hu_out, 0), (A2, B1, span, hu_out, span), (DB, MX, 0, mo_out, 0), (A1, DG, 0, mg_out, 0),
    ]

    def tile(job, group, half):
        left, right, offset = jobs[job][:3]
        columns = pl.ds(pl.multiple_of(offset + half * cols, cols), cols)
        return dot_tn(left[:, pl.ds(pl.multiple_of(group * slab, slab), slab)], right[:, columns])

    def each_half(body):
        @pl.loop(0, 2)
        def _(half):
            body(half, pl.ds(pl.multiple_of(half * cols, cols), cols))

    def sib_copy(job, slot):
        return remote(SS.at[slot], SR.at[job % 3, slot], sib_send.at[slot], sib_recv.at[job, slot], place.sibling())

    def h1_copy(job, slot):
        return remote(H1S.at[job % 2, slot], H1R.at[job % 3, slot], h1_send.at[job % 2, slot], h1_recv.at[job, slot], place.first())

    def h2_copy(job):
        return remote(H2S.at[job % 2], H2R.at[job % 2], h2_send.at[job % 2], h2_recv.at[job], place.second())

    def to_sibling(job):
        if job >= 3:
            pl.semaphore_wait(sib_free, 1)

        @pl.loop(0, 4)
        def _(slot):
            if job >= 1:
                sib_copy(job - 1, slot).wait_send()
            group = place.owner(slot, 1)

            def body(half, at):
                SS[slot, :, at] = tile(job, group, half).astype(jnp.bfloat16)

            each_half(body)
            sib_copy(job, slot).start()

    def to_first(job):
        if job >= 3:
            pl.semaphore_wait(first_free, 1)

        @pl.loop(0, 2)
        def _(slot):
            if job >= 2:
                h1_copy(job - 2, slot).wait_send()
            group = place.owner(slot, 0)
            sib_copy(job, slot).wait_recv()

            def body(half, at):
                H1S[job % 2, slot, :, at] = (tile(job, group, half) + SR[job % 3, slot, :, at].astype(jnp.float32)).astype(jnp.bfloat16)

            each_half(body)
            h1_copy(job, slot).start()

    def to_second(job):
        if job >= 2:
            pl.semaphore_wait(second_free, 1)
            h2_copy(job - 2).wait_send()
        group = place.owner(2, 0)
        sib_copy(job, 2).wait_recv()
        h1_copy(job, 0).wait_recv()

        def body(half, at):
            H2S[job % 2, :, at] = (
                tile(job, group, half) + SR[job % 3, 2, :, at].astype(jnp.float32) + H1R[job % 3, 0, :, at].astype(jnp.float32)
            ).astype(jnp.bfloat16)

        each_half(body)
        h2_copy(job).start()

    def out_copy(job):
        return pltpu.make_async_copy(OS, jobs[job][3].at[:, pl.ds(jobs[job][4], span)], out_sem)

    def to_output(job):
        group = place.owner(3, 0)
        sib_copy(job, 3).wait_recv()
        h1_copy(job, 1).wait_recv()
        h2_copy(job).wait_recv()
        if job >= 1:
            out_copy(job - 1).wait()

        def body(half, at):
            OS[:, at] = (
                tile(job, group, half) + SR[job % 3, 3, :, at].astype(jnp.float32)
                + H1R[job % 3, 1, :, at].astype(jnp.float32) + H2R[job % 2, :, at].astype(jnp.float32)
            )

        each_half(body)
        out_copy(job).start()
        for ahead, free, device in ((3, sib_free, place.sibling()), (3, first_free, place.first()), (2, second_free, place.second())):
            if job + ahead < JOBS:
                pl.semaphore_signal(free, inc=1, device_id=device, device_id_type=MESH)

    def gate_load(chunk):
        return pltpu.make_async_copy(gate_in.at[pl.ds(chunk * chunk_rows, chunk_rows)], GP, gate_sem.at[0])

    def mem_load(chunk):
        return pltpu.make_async_copy(mem_in.at[pl.ds(chunk * chunk_rows, chunk_rows)], MT, gate_sem.at[1])

    def term_store(chunk):
        return pltpu.make_async_copy(MT, term_out.at[pl.ds(chunk * chunk_rows, chunk_rows)], gate_sem.at[2])

    def channels(chunk):
        rows = pl.ds(chunk * chunk_rows, chunk_rows)
        if chunk > 0:
            term_store(chunk - 1).wait()
        mem_load(chunk).start()
        gate_load(chunk).wait()
        mem_load(chunk).wait()

        def body(half, at):
            d_mixed = dot_nt(DB[rows, :], WO[at, :])
            pre = GP[:, at]
            sigma = jax.nn.sigmoid(pre)
            DG[rows, at] = (d_mixed * MT[:, at].astype(jnp.float32) * (sigma * (1.0 + pre * (1.0 - sigma)))).astype(jnp.bfloat16)
            MT[:, at] = (d_mixed * (pre * sigma)).astype(jnp.bfloat16)

        each_half(body)
        term_store(chunk).start()
        if chunk + 1 < chunks:
            gate_load(chunk + 1).start()

    def first_part(chunk, block):
        return dot_nt(DG[pl.ds(chunk * chunk_rows, chunk_rows), :], WG[pl.ds(pl.multiple_of(block * width, width), width), :])

    def first_step(chunk, step, inside):
        scatter.step(chunk, step, lambda block: first_part(chunk, block), inside)

    def own_copies(chunk):
        rows = pl.ds(chunk * chunk_rows, chunk_rows)
        return (
            pltpu.make_async_copy(xhat_in.at[rows], XH, gate_sem.at[3]),
            pltpu.make_async_copy(HO, dh1_out.at[rows], gate_sem.at[4]),
        )

    def own_step(chunk):
        load_xhat, store = own_copies(chunk)
        load_xhat.start()
        if chunk > 0:
            own_copies(chunk - 1)[1].wait()
        HO[...] = first_part(chunk, t)
        scatter.own(chunk, HO)
        load_xhat.wait()
        product = HO[...] * XH[...]
        if chunk == 0:
            GV[0, 0:1] = jnp.sum(product, axis=0, keepdims=True)
        else:
            GV[0, 0:1] += jnp.sum(product, axis=0, keepdims=True)
        SV[:, pl.ds(chunk * chunk_rows, chunk_rows)] = to_row(jnp.sum(product * gain_ref[...], axis=1, keepdims=True))
        store.start()

    def sum_copy(step):
        device = (place.sibling(), place.first(), place.second())[step]
        return remote(GV.at[step], GR.at[step], small_send.at[step], small_recv.at[step], device)

    def to_line(step, what):
        device = place.along((t + step) % 4)
        if what == 0:
            return remote(SV, SA.at[t], small_send.at[2 + step], small_recv.at[2 + step], device)
        return remote(GV.at[3], GA.at[t], small_send.at[5 + step], small_recv.at[5 + step], device)

    down_scatter = Scatter(place, ZN, n_send, n_recv)

    def down_part(chunk, block, target, sem):
        source = down_in.at[pl.ds(chunk * chunk_rows, chunk_rows), pl.ds(pl.multiple_of(block * width, width), width)]
        return pltpu.make_async_copy(source, target, sem)

    def down_store(chunk):
        return pltpu.make_async_copy(NO, down_out.at[pl.ds(chunk * chunk_rows, chunk_rows)], n_load.at[2])

    def down_own(chunk):
        if chunk > 0:
            down_store(chunk - 1).wait()
        load = down_part(chunk, t, NO, n_load.at[3])
        load.start()
        load.wait()
        down_scatter.own(chunk, NO)
        down_store(chunk).start()
        down_scatter.finish(chunk)
        if chunk < 2:
            for step in (-1, 1):
                @pl.when((t + step >= 0) & (t + step <= 3))
                def _():
                    pl.semaphore_signal(
                        n_free.at[(1 - step) // 2], inc=1, device_id=place.along(t + step), device_id_type=MESH
                    )

    is_end = (t == 0) | (t == 3)
    down_order = {inside: [event[1:3] for event in BACK_ORDER if event[0] == "Ns" and event[3] == inside] for inside in (False, True)}

    def only(inside, body):
        pl.when(jnp.logical_not(is_end) if inside else is_end)(body)

    def down_load(inside, index):
        chunk, step = down_order[inside][index]
        return down_part(chunk, down_scatter.block(step), NS.at[index % 2], n_load.at[index % 2])

    def down_step(chunk, step, inside):
        index = down_order[inside].index((chunk, step))
        first_of_chunk = all(other != chunk for other, _ in down_order[inside][:index])

        def body():
            if index == 0:
                down_load(inside, 0).start()
            if index + 1 < 12:
                down_load(inside, index + 1).start()
            if chunk >= 2 and first_of_chunk:
                for side, near in enumerate((t > 0, t < 3)):
                    pl.when(near)(functools.partial(pl.semaphore_wait, n_free.at[side], 1))
            down_load(inside, index).wait()
            down_scatter.step(chunk, step, lambda block: NS[index % 2], inside)

        only(inside, body)

    channel_count = span
    block = DB.shape[0] // 8
    exchange = Exchange(
        place,
        lambda group: B2.at[pl.ds(pl.multiple_of(group * block, block), block), pl.ds(channel_count, channel_count)],
        lambda group: returned.at[pl.ds(pl.multiple_of(group * block, block), block)],
        x_send, x_recv,
    )

    def send_terms():
        term_store(3).wait()
        load("terms", term_out, B2.at[:, pl.ds(0, channel_count)], 4)
        need("terms")
        PLACES[...] = ids_ref[...] - (place.f * 4 + place.c) * DB.shape[0]

        @pl.loop(0, chunks)
        def _(part):
            rows = pl.ds(pl.multiple_of(part * chunk_rows, chunk_rows), chunk_rows)
            total = jnp.zeros((chunk_rows, channel_count), jnp.float32)
            for chunk in range(chunks):
                picked = chosen(PLACES[0:1, rows], chunk * chunk_rows, chunk_rows)
                total += dot_tn(picked, B2[chunk * chunk_rows:(chunk + 1) * chunk_rows, 0:channel_count])
            B2[rows, channel_count:2 * channel_count] = total.astype(jnp.bfloat16)

        exchange.start()

    def memory_grads():
        exchange.arrived()
        copy = pltpu.make_async_copy(returned, A2.at[:, pl.ds(0, channel_count)], load_sem.at[0])
        copy.start()
        copy.wait()

        @pl.loop(0, chunks)
        def _(part):
            rows = pl.ds(pl.multiple_of(part * chunk_rows, chunk_rows), chunk_rows)
            total = jnp.zeros((chunk_rows, channel_count), jnp.float32)
            for chunk in range(chunks):
                picked = chosen(rank_ref[0:1, rows], chunk * chunk_rows, chunk_rows)
                total += dot_tn(picked, A2[chunk * chunk_rows:(chunk + 1) * chunk_rows, 0:channel_count])
            GP[...] = total
            store = pltpu.make_async_copy(GP, memory_out.at[rows], gate_sem.at[0])
            store.start()
            store.wait()

    gate_load(0).start()

    def gains(number):
        if number == 0:
            for step in range(1, 4):
                to_line(step, 0).start()
            GV[0, 1:2] = gg2_ref[...]
            sum_copy(0).start()
            return
        sum_copy(number - 1).wait_recv()
        GV[number] = GV[number - 1] + GR[number - 1]
        if number < 3:
            sum_copy(number).start()
        else:
            for ahead in range(1, 4):
                to_line(ahead, 1).start()

    actions = {
        "D": gather.step, "S1": to_sibling, "S2": to_first, "S3": to_second, "S4": to_output, "Bc": channels, "Bo": own_step,
        "Bs": lambda chunk, step, inside: only(inside, lambda: first_step(chunk, step, inside)), "Ns": down_step, "No": down_own,
        "terms": send_terms, "mgrads": memory_grads, "G": gains,
    }
    wanted = {
        ("S1", 0): ("cot", "swi"), ("S1", 2): ("h2", "da"), ("S1", 4): ("db",), ("S1", 6): ("mixed",), ("S1", 7): ("h1",),
        ("Bc", 0): ("out_w", "gate_w"),
    }
    GV[0] = jnp.zeros_like(GV[0])
    for event in BACK_ORDER:
        need(*wanted.get(event, ()))
        actions[event[0]](*event[1:])
        if event == ("S2", 0):
            load("h2", h2_in, A2, 3)
            load("da", da_in, B2, 4)
            load("out_w", out_w_in, WO, 5)
            load("gate_w", gate_w_in, WG, 6)
            load("mixed", mixed_in, MX, 7)
        if event == ("S4", 1):
            load("db", db_in, B1, 2)
            load("h1", h1_in, A1, 1)

    for step in range(1, 4):
        to_line(step, 0).wait()
        to_line(step, 1).wait()
    SA[t] = SV[...]
    GA[t] = GV[3]
    stats_out[...] = SA[0] + SA[1] + SA[2] + SA[3]
    gains_out[...] = GA[...]
    for chunk in range(4):
        gather.finish(chunk)
        scatter.finish(chunk)
    for step in range(3):
        sum_copy(step).wait_send()
    for slot in range(4):
        sib_copy(JOBS - 1, slot).wait_send()
    for job in (JOBS - 2, JOBS - 1):
        for slot in range(2):
            h1_copy(job, slot).wait_send()
        h2_copy(job).wait_send()
    exchange.finish()
    down_store(3).wait()
    own_copies(3)[1].wait()
    out_copy(JOBS - 1).wait()


def back_call(branch_own, cot, swi, h2, da, db, mixed, h1, gate, mem, out_w, gate_w, xhat, gain, gg2, rank, ids, down):
    rows, features = cot.shape
    channels, hidden = mixed.shape[1], swi.shape[1]
    width, slab, part = features // 4, features // 8, rows // 4
    bf, f32 = jnp.bfloat16, jnp.float32
    shape = jax.ShapeDtypeStruct
    anywhere, vmem = pl.BlockSpec(memory_space=pl.ANY), pl.BlockSpec(memory_space=pltpu.VMEM)
    dma = pltpu.SemaphoreType.DMA
    regular = pltpu.SemaphoreType.REGULAR
    V = pltpu.VMEM
    macs = rows * features * (3 * hidden + 4 * channels)
    return pl.pallas_call(
        back_kernel,
        name="backward",
        out_shape=(
            shape((rows, width), f32), shape((rows, width), f32), shape((rows, channels), f32), shape((rows, channels), bf), shape((rows, channels), bf),
            shape((slab, hidden), f32), shape((slab, hidden), f32),
            shape((slab, hidden), f32), shape((slab, channels), f32), shape((slab, channels), f32), shape((4, 8, width), f32),
            shape((8, rows), f32),
        ),
        in_specs=[anywhere] * 13 + [vmem] * 4 + [anywhere],
        out_specs=(anywhere,) * 10 + (vmem,) * 2,
        scratch_shapes=[
            V((rows, features), bf), V((rows, features), bf), V((rows, hidden), bf), V((rows, hidden), bf), V((rows, channels), bf),
            V((rows, features), bf), V((rows, channels), bf), V((channels, features), bf), V((features, channels), bf),
            V((3, 4, slab, channels), bf), V((4, slab, channels), bf), V((2, 2, slab, channels), bf), V((3, 2, slab, channels), bf),
            V((2, slab, channels), bf), V((2, slab, channels), bf), V((slab, channels), f32), V((4, 5, part, width), bf),
            V((part, channels), f32), V((part, channels), bf), V((part, width), f32), V((part, width), f32),
            V((4, 8, width), f32), V((3, 8, width), f32), V((4, 8, width), f32), V((8, rows), f32), V((4, 8, rows), f32),
            V((8, rows), jnp.int32), V((2, 5, part, width), bf), V((2, part, width), f32), V((part, width), f32), dma((8,)), dma((5,)), dma((4, 2, 3)), dma((4, 4)), dma((4, 3)), dma((4, 5)), dma((4,)), dma((JOBS, 4)), dma((2, 2)),
            dma((JOBS, 2)), dma((2,)), dma((JOBS,)), dma, dma((9,)), dma((9,)), dma((8,)), dma((8,)), dma((4, 3)), dma((4, 5)), dma((4,)), pltpu.SemaphoreType.REGULAR((2,)), regular, regular, regular,
        ],
        compiler_params=pltpu.CompilerParams(collective_id=1, has_side_effects=True, vmem_limit_bytes=VMEM_LIMIT),
        cost_estimate=pl.CostEstimate(flops=2 * macs, bytes_accessed=64 * 2**20, transcendentals=rows * channels),
    )(branch_own, cot, swi, h2, da, db, mixed, h1, gate, mem, out_w, gate_w, xhat, gain, gg2, rank, ids, down)


FRONT_ORDER = (
    ("W", 1, 0), ("T", 0, 0), ("T", 1, 0), ("C", 0, 0), ("W", 0, 0), ("rows",), ("T", 1, 1), ("T", 0, 1), ("C", 1, 0),
    ("W", 1, 1), ("T", 2, 0), ("C", 2, 0), ("W", 0, 1), ("W", 2, 0), ("T", 0, 2), ("T", 0, 3), ("T", 3, 0), ("W", 3, 0),
    ("T", 1, 2), ("W", 1, 2), ("T", 3, 1), ("W", 0, 2), ("C", 0, 1), ("take",), ("T", 2, 1), ("C", 2, 1), ("W", 0, 3),
    ("F1", 0), ("W", 1, 3), ("Rs", 0, 0, False), ("W", 4, 0), ("Rs", 0, 0, True), ("Rs", 0, 1, False), ("T", 1, 3),
    ("T", 3, 2), ("C", 1, 1), ("F1", 1), ("Rs", 1, 0, True), ("W", 2, 1), ("Rs", 1, 0, False), ("Rs", 0, 1, True),
    ("Rs", 1, 2, False), ("T", 2, 2), ("Rs", 1, 1, True), ("Rs", 0, 2, True), ("C", 1, 2), ("Rs", 0, 2, False),
    ("Ro", 0), ("Rs", 1, 2, True), ("Rs", 1, 1, False), ("H", 0, 0), ("Ro", 1), ("H", 1, 0), ("W", 3, 1), ("T", 2, 3),
    ("F1", 2), ("H", 0, 1), ("Rs", 2, 0, False), ("Rs", 2, 0, True), ("H", 1, 1), ("W", 4, 1), ("T", 3, 3), ("F1", 3),
    ("Rs", 3, 0, False), ("C", 0, 2), ("Rs", 2, 1, False), ("H", 0, 2), ("W", 2, 2), ("Rs", 2, 1, True),
    ("Rs", 3, 1, False), ("Rs", 3, 0, True), ("C", 1, 3), ("Rs", 2, 2, False), ("C", 3, 0), ("W", 3, 2), ("H", 1, 2),
    ("Rs", 2, 2, True), ("Rs", 3, 2, True), ("W", 4, 2), ("W", 3, 3), ("Ro", 2), ("C", 2, 2), ("Rs", 3, 2, False),
    ("H", 2, 0), ("C", 3, 1), ("C", 0, 3), ("Rs", 3, 1, True), ("W", 2, 3), ("H", 0, 3), ("W", 4, 3), ("F2", 0),
    ("Es", 0, 0, False), ("Es", 0, 1, False), ("Es", 0, 2, False), ("H", 2, 1), ("H", 1, 3), ("F2", 1),
    ("Es", 1, 0, False), ("Es", 0, 0, True), ("Es", 1, 1, False), ("Es", 0, 2, True), ("H", 2, 2), ("H", 2, 3),
    ("NP", 0), ("Es", 0, 1, True), ("Ro", 3), ("H", 3, 0), ("C", 3, 2), ("C", 2, 3), ("Es", 1, 0, True), ("Eo", 0),
    ("NP", 1), ("close", 0), ("Es", 1, 2, True), ("H", 3, 1), ("Es", 1, 2, False), ("Es", 1, 1, True), ("F2", 2),
    ("Es", 2, 0, False), ("H", 3, 2), ("Eo", 1), ("C", 3, 3), ("Es", 2, 1, False), ("Es", 2, 2, False), ("close", 1),
    ("Es", 2, 2, True), ("Es", 2, 0, True), ("H", 3, 3), ("F2", 3), ("Es", 3, 0, False), ("Es", 3, 1, False),
    ("Es", 2, 1, True), ("Es", 3, 0, True), ("NP", 2), ("Es", 3, 2, False), ("Es", 3, 2, True), ("Es", 3, 1, True),
    ("Eo", 2), ("NP", 3), ("close", 2), ("Eo", 3), ("close", 3),
)
BACK_ORDER = (
    ("D", 0, 0), ("S1", 0), ("D", 1, 0), ("S2", 0), ("Ns", 0, 1, False), ("D", 2, 0), ("Ns", 1, 0, False), ("S1", 1),
    ("D", 3, 0), ("S2", 1), ("S1", 2), ("Ns", 1, 1, False), ("D", 0, 1), ("S3", 0), ("S2", 2), ("D", 0, 2), ("D", 2, 1),
    ("Ns", 0, 0, False), ("D", 0, 3), ("Ns", 0, 2, False), ("Bc", 0), ("S3", 1), ("D", 1, 1), ("S4", 0), ("S1", 3),
    ("S2", 3), ("Ns", 1, 2, False), ("D", 1, 2), ("D", 1, 3), ("D", 2, 2), ("Ns", 0, 0, True), ("Bs", 0, 1, False),
    ("S3", 2), ("Bc", 1), ("D", 3, 1), ("Bs", 1, 0, False), ("S4", 1), ("Bs", 0, 0, False), ("Ns", 1, 0, True),
    ("S1", 4), ("D", 3, 2), ("D", 2, 3), ("S2", 4), ("Bc", 2), ("D", 3, 3), ("S4", 2), ("Bs", 1, 1, False),
    ("Bs", 0, 2, True), ("Bs", 2, 0, False), ("Bc", 3), ("Bs", 3, 0, False), ("Ns", 0, 1, True), ("Ns", 0, 2, True),
    ("S3", 3), ("Bs", 1, 2, False), ("Ns", 1, 1, True), ("Bs", 0, 0, True), ("S3", 4), ("S1", 5), ("No", 0),
    ("Bs", 1, 0, True), ("S2", 5), ("S4", 3), ("S1", 6), ("Bs", 3, 1, False), ("Bs", 2, 1, False), ("Bs", 1, 1, True),
    ("S4", 4), ("Bs", 2, 0, True), ("Ns", 2, 0, False), ("Ns", 1, 2, True), ("Ns", 2, 1, False), ("Bs", 0, 2, False),
    ("S3", 5), ("Bs", 3, 2, False), ("Bs", 3, 0, True), ("terms",), ("S2", 6), ("Bs", 1, 2, True), ("No", 1),
    ("Ns", 3, 0, False), ("Bs", 2, 1, True), ("Bs", 2, 2, False), ("S4", 5), ("Bs", 3, 1, True), ("S1", 7),
    ("Ns", 2, 0, True), ("Ns", 3, 1, False), ("Ns", 2, 2, False), ("Bs", 3, 2, True), ("S2", 7), ("Bs", 0, 1, True),
    ("Bo", 0), ("Ns", 2, 1, True), ("Bs", 2, 2, True), ("Ns", 2, 2, True), ("mgrads",), ("Ns", 3, 2, False),
    ("Ns", 3, 0, True), ("S3", 6), ("Bo", 1), ("Bo", 2), ("Bo", 3), ("G", 0), ("Ns", 3, 2, True), ("Ns", 3, 1, True),
    ("S3", 7), ("G", 1), ("G", 2), ("No", 2), ("G", 3), ("No", 3), ("S4", 6), ("S4", 7),
)


class Spread:
    def __init__(self, place, index, shard, view, send, recv, local):
        self.place, self.index, self.shard, self.view, self.send, self.recv = place, index, shard, view, send, recv
        self.local = local

    def group(self, *flips):
        f, c = self.place.at(*flips)
        return f * 4 + c

    def copy(self, group, device, slot):
        view = self.view(group)
        source = self.shard if slot < 3 else view
        return remote(source, view, self.send.at[self.index, slot], self.recv.at[self.index, group], device)

    def routes(self):
        place = self.place
        me, both = self.group(0, 0, 0), self.group(1, 1, 0)
        first, second = self.group(1 - place.k, place.k, 0), self.group(place.k, 1 - place.k, 0)
        return (
            (me, place.first()), (me, place.second()), (me, place.sibling()), (second, place.first()), (first, place.sibling()),
            (second, place.sibling()), (both, place.sibling()),
        )

    def start(self, slot):
        group, device = self.routes()[slot]
        self.copy(group, device, slot).start()

    def arrived(self, group):
        self.copy(group, self.place.sibling(), 3).wait_recv()

    def stay(self):
        return pltpu.make_async_copy(self.shard, self.view(self.group(0, 0, 0)), self.local.at[self.index])

    def phase(self, number):
        routes = self.routes()
        if number == 0:
            for slot in range(3):
                self.start(slot)
            self.stay().start()
        if number == 1:
            self.arrived(routes[3][0])
            self.start(3)
            self.start(5)
            self.arrived(routes[4][0])
            self.start(4)
        if number == 2:
            self.arrived(routes[6][0])
            self.start(6)
        if number == 3:
            for flips in ((0, 0), (0, 1), (1, 0), (1, 1)):
                self.arrived(self.group(*flips, 1))
            self.stay().wait()

    def finish(self):
        for slot, (group, device) in enumerate(self.routes()):
            self.copy(group, device, slot).wait_send()


def to_column(row):
    return jnp.broadcast_to(row, (128, row.shape[1])).T[:, 0:1]


def front_kernel(
    tokens, cotangent, mem_in, gate_w, out_w, up_a_w, up_b_w, down_w, gain1, gain2, deal_row, deal_column,
    tok_full, cot_full, h2_full, h1_out, gate_out, mixed_out, swi_out, da_out, db_out, gate_w_out, out_w_out, down_out, middle_out, dx1_out, branch_out, mem_out,
    inv_out, gg2_out, rank_out, ids_out,
    WG, WO, WA, WB, WD, Z1, ZE, XC, CC, H1C, GPS, MXS, MT, SWI, DA, DB, X1, H2O, HO, DHQ, FS, NS, BS, OWN, I2, SV, SA, SV2, SA2, SENT,
    load_sem, store_sem, stage_sem, t_send, t_recv, c_send, c_recv, h_send, h_recv, r_send, r_recv, e_send, e_recv,
    w_send, w_recv, w_local, s_send, s_recv, x_send, x_recv, i_send, i_recv, n_sem,
):
    place = Place()
    t = place.t
    rows, features = tok_full.shape
    chunk_rows, width = HO.shape
    channels, hidden = MXS.shape[2], SWI.shape[2]
    half = channels // 2
    slab = features // 8
    own_columns = pl.ds(pl.multiple_of(t * width, width), width)

    def rows_of(chunk):
        return pl.ds(chunk * chunk_rows, chunk_rows)

    def columns_of(block, size):
        return pl.ds(pl.multiple_of(block * size, size), size)

    def keep(index, source, target):
        return pltpu.make_async_copy(source, target, stage_sem.at[index])

    own_tokens = keep(0, tokens, tok_full.at[:, own_columns])
    own_cot = keep(1, cotangent, cot_full.at[:, own_columns])
    own_tokens.start()
    own_cot.start()
    greet(place)

    tok_gather = Gather(place, tok_full, t_send, t_recv, chunk_rows, width, tokens)
    cot_gather = Gather(place, cot_full, c_send, c_recv, chunk_rows, width, cotangent)
    h2_gather = Gather(place, h2_full, h_send, h_recv, chunk_rows, width, H2O)
    mix_scatter = Scatter(place, Z1, r_send, r_recv)
    up_scatter = Scatter(place, ZE, e_send, e_recv)
    spreads = [
        Spread(place, index, shard, view, w_send, w_recv, w_local)
        for index, (shard, view) in enumerate((
            (gate_w, lambda group: WG.at[columns_of(group, slab), :]),
            (out_w, lambda group: WO.at[:, columns_of(group, slab)]),
            (up_a_w, lambda group: WA.at[columns_of(group, slab), :]),
            (up_b_w, lambda group: WB.at[columns_of(group, slab), :]),
            (down_w, lambda group: WD.at[:, columns_of(group, slab)]),
        ))
    ]

    block = rows // 8

    def quarter(ref, index):
        return ref.at[index // 2, :, pl.ds(pl.multiple_of((index % 2) * channels, channels), channels)]

    def eighth(ref, group):
        return ref.at[
            group // 4, pl.ds(pl.multiple_of((group % 2) * block, block), block),
            pl.ds(pl.multiple_of(((group // 2) % 2) * channels, channels), channels),
        ]

    def lanes(ref, group):
        return ref.at[:, pl.ds(pl.multiple_of(group * block, block), block)]

    rows_exchange = Exchange(place, lambda group: eighth(DA, group), lambda group: eighth(SWI, group), x_send, x_recv)
    ids_exchange = Exchange(place, lambda group: lanes(SENT, group), lambda group: lanes(ids_out, group), i_send, i_recv)

    def send_rows():
        loads = [pltpu.make_async_copy(mem_in.at[rows_of(index)], quarter(DB, index), load_sem.at[4 + index]) for index in range(4)]
        for copy in loads:
            copy.start()
        row = deal_row[...]
        rank = jnp.zeros((1, rows), jnp.float32)
        for chunk in range(4):
            rank += jnp.sum(jnp.where(deal_column[rows_of(chunk)] < row, 1.0, 0.0), axis=0, keepdims=True)
        rank_out[...] = jnp.broadcast_to(rank, (8, rows)).astype(jnp.int32)
        spots = lax.broadcasted_iota(jnp.int32, (chunk_rows, rows), 1).astype(jnp.float32)
        ordered = jnp.zeros((1, rows), jnp.float32)
        for chunk in range(4):
            column = deal_column[rows_of(chunk)]
            place_of = jnp.sum(jnp.where(row < column, 1.0, 0.0), axis=1, keepdims=True)
            ordered += jnp.sum(jnp.where(place_of == spots, column.astype(jnp.float32), 0.0), axis=0, keepdims=True)
        SENT[...] = jnp.broadcast_to(ordered, (8, rows)).astype(jnp.int32)
        ids_exchange.start()
        for copy in loads:
            copy.wait()

        @pl.loop(0, 4)
        def _(index):
            total = jnp.zeros((chunk_rows, channels), jnp.float32)
            for other in range(4):
                picked = chosen(rank_out[0:1, rows_of(other)], index * chunk_rows, chunk_rows)
                total += jnp.dot(picked, quarter(DB, other)[...], preferred_element_type=jnp.float32)
            quarter(DA, index)[...] = total.astype(jnp.bfloat16)

        rows_exchange.start()

    def mem_store(chunk):
        return pltpu.make_async_copy(MXS.at[chunk % 2], mem_out.at[rows_of(chunk)], load_sem.at[4 + chunk])

    def take_rows():
        ids_exchange.arrived()
        rows_exchange.arrived()
        for chunk in range(4):
            if chunk > 1:
                mem_store(chunk - 2).wait()
            first = rows_exchange.me * rows + chunk * chunk_rows
            total = jnp.zeros((chunk_rows, channels), jnp.float32)
            for other in range(4):
                picked = chosen(ids_out[0:1, rows_of(other)], first, chunk_rows)
                total += jnp.dot(picked, quarter(SWI, other)[...], preferred_element_type=jnp.float32)
            MXS[chunk % 2] = total.astype(jnp.bfloat16)
            mem_store(chunk).start()
        for chunk in (2, 3):
            mem_store(chunk).wait()
        rows_exchange.finish()
        ids_exchange.finish()

    def h1_store(chunk):
        return pltpu.make_async_copy(H1C, h1_out.at[rows_of(chunk)], store_sem.at[0])

    def gate_store(chunk):
        return pltpu.make_async_copy(GPS, gate_out.at[rows_of(chunk)], store_sem.at[1])

    def mixed_store(chunk):
        return pltpu.make_async_copy(MXS.at[chunk % 2], mixed_out.at[rows_of(chunk)], store_sem.at[2 + chunk % 2])

    def hidden_stores(chunk):
        slot = chunk % 2
        return [
            pltpu.make_async_copy(source.at[slot], target.at[rows_of(chunk)], store_sem.at[4 + 2 * index + slot])
            for index, (source, target) in enumerate(((SWI, swi_out), (DA, da_out), (DB, db_out)))
        ]

    def own_h2_store(chunk):
        return pltpu.make_async_copy(H2O.at[rows_of(chunk)], h2_full.at[rows_of(chunk), own_columns], stage_sem.at[4 + chunk])

    def small_store(source, target, chunk, index):
        return pltpu.make_async_copy(source, target.at[rows_of(chunk)], store_sem.at[index])

    def fetch(source, target, index):
        copy = pltpu.make_async_copy(source, target, load_sem.at[index])
        copy.start()
        return copy

    def stat_copy(chunk, step, which):
        source, target = ((SV, SA), (SV2, SA2))[which]
        columns = rows_of(chunk)
        return remote(
            source.at[:, columns], target.at[t, :, columns], s_send.at[which, chunk, step - 1], s_recv.at[which, chunk, step - 1],
            place.along((t + step) % 4),
        )

    def stats(chunk, which):
        source, target = ((SV, SA), (SV2, SA2))[which]
        for step in range(1, 4):
            stat_copy(chunk, step, which).wait_recv()
        total = source[0:1, rows_of(chunk)]
        for step in range(1, 4):
            total = total + target[(t + step) % 4, 0:1, rows_of(chunk)]
        return to_column(total)

    def memory_unit(chunk):
        if chunk == 0:
            own_tokens.wait()
        load = fetch(tok_full.at[rows_of(chunk)], XC, 1)
        mem_load = fetch(mem_out.at[rows_of(chunk)], MT, 0)
        if chunk > 0:
            h1_store(chunk - 1).wait()
        load.wait()
        square = jnp.zeros((chunk_rows, 1), jnp.float32)
        for block in range(4):
            values = XC[:, block * width:(block + 1) * width].astype(jnp.float32)
            square += jnp.sum(values * values, axis=1, keepdims=True)
        inverse = lax.rsqrt(square / features + EPS)
        inv_out[rows_of(chunk)] = inverse
        for block in range(4):
            at = slice(block * width, (block + 1) * width)
            H1C[:, at] = (XC[:, at].astype(jnp.float32) * inverse * gain1[:, at]).astype(jnp.bfloat16)
        h1_store(chunk).start()
        mem_load.wait()
        if chunk > 0:
            gate_store(chunk - 1).wait()
        if chunk > 1:
            mixed_store(chunk - 2).wait()

        @pl.loop(0, 2)
        def _(part):
            at = columns_of(part, half)
            pre = jnp.dot(H1C[...], WG[:, at], preferred_element_type=jnp.float32)
            GPS[:, at] = pre
            MXS[chunk % 2, :, at] = (MT[:, at].astype(jnp.float32) * (pre * jax.nn.sigmoid(pre))).astype(jnp.bfloat16)

        gate_store(chunk).start()
        mixed_store(chunk).start()

    def mix_part(chunk, block):
        return jnp.dot(MXS[chunk % 2], WO[:, columns_of(block, width)], preferred_element_type=jnp.float32)

    def mix_own(chunk):
        load = fetch(tokens.at[rows_of(chunk)], OWN, 2)
        if chunk > 0:
            small_store(X1.at[rows_of(chunk)], middle_out, chunk - 1, 10).wait()
        HO[...] = mix_part(chunk, t)
        mix_scatter.own(chunk, HO)
        load.wait()
        middle = OWN[...].astype(jnp.float32) + HO[...]
        X1[rows_of(chunk)] = middle
        H2O[rows_of(chunk)] = (middle * gain2[...]).astype(jnp.bfloat16)
        own_h2_store(chunk).start()
        SV[:, rows_of(chunk)] = to_row(jnp.sum(middle * middle, axis=1, keepdims=True))
        small_store(X1.at[rows_of(chunk)], middle_out, chunk, 10).start()
        mix_scatter.finish(chunk)
        for step in range(1, 4):
            stat_copy(chunk, step, 0).start()

    def feed_forward(chunk):
        own_h2_store(chunk).wait()
        if chunk == 0:
            own_cot.wait()
        loads = [fetch(h2_full.at[rows_of(chunk)], XC, 1), fetch(cot_full.at[rows_of(chunk)], CC, 3)]
        inverse = lax.rsqrt(stats(chunk, 0) / features + EPS)
        I2[rows_of(chunk)] = inverse
        if chunk > 1:
            for store in hidden_stores(chunk - 2):
                store.wait()
        for load in loads:
            load.wait()

        @pl.loop(0, 4)
        def _(part):
            at = columns_of(part, hidden // 4)
            up_a = jnp.dot(XC[...], WA[:, at], preferred_element_type=jnp.float32) * inverse
            up_b = jnp.dot(XC[...], WB[:, at], preferred_element_type=jnp.float32) * inverse
            d_swi = dot_nt(CC[...], WD[at, :])
            sigma = jax.nn.sigmoid(up_a)
            swish = up_a * sigma
            SWI[chunk % 2, :, at] = (swish * up_b).astype(jnp.bfloat16)
            d_swi = d_swi * inverse
            DA[chunk % 2, :, at] = (d_swi * up_b * (sigma * (1.0 + up_a * (1.0 - sigma)))).astype(jnp.bfloat16)
            DB[chunk % 2, :, at] = (d_swi * swish).astype(jnp.bfloat16)

        for store in hidden_stores(chunk):
            store.start()

    def down_store(chunk, block):
        return pltpu.make_async_copy(NS.at[block % 2], down_out.at[rows_of(chunk), columns_of(block, width)], n_sem.at[block % 2])

    def down_parts(chunk):
        for block in range(4):
            if chunk > 0 or block > 1:
                down_store(chunk, block).wait()
            NS[block % 2] = jnp.dot(SWI[chunk % 2], WD[:, columns_of(block, width)], preferred_element_type=jnp.float32)
            down_store(chunk, block).start()

    def up_part(chunk, block):
        at = columns_of(block, width)
        return dot_nt(DA[chunk % 2], WA[at, :]) + dot_nt(DB[chunk % 2], WB[at, :])

    def hidden_own(chunk):
        HO[...] = up_part(chunk, t)
        up_scatter.own(chunk, HO)
        middle = X1[rows_of(chunk)]
        d_second = HO[...]
        grads = jnp.sum(d_second * middle, axis=0, keepdims=True)
        if chunk == 0:
            gg2_out[...] = grads
        else:
            gg2_out[...] += grads
        scaled = d_second * gain2[...]
        DHQ[...] = scaled
        SV2[:, rows_of(chunk)] = to_row(jnp.sum(scaled * middle, axis=1, keepdims=True) * I2[rows_of(chunk)])
        up_scatter.finish(chunk)
        for step in range(1, 4):
            stat_copy(chunk, step, 1).start()

    def close(chunk):
        load = fetch(cotangent.at[rows_of(chunk)], OWN, 2)
        mean = stats(chunk, 1) / features
        if chunk > 0:
            small_store(FS, dx1_out, chunk - 1, 11).wait()
            small_store(BS, branch_out, chunk - 1, 12).wait()
        load.wait()
        unit = X1[rows_of(chunk)] * I2[rows_of(chunk)]
        total = OWN[...].astype(jnp.float32) + DHQ[...] - unit * mean
        FS[...] = total
        BS[...] = total.astype(jnp.bfloat16)
        small_store(FS, dx1_out, chunk, 11).start()
        small_store(BS, branch_out, chunk, 12).start()

    weight_stores = [
        pltpu.make_async_copy(WG, gate_w_out, stage_sem.at[2]), pltpu.make_async_copy(WO, out_w_out, stage_sem.at[3]),
    ]
    is_end = (t == 0) | (t == 3)

    def scatter_step(scatter, part, chunk, step, inside):
        pl.when(jnp.logical_not(is_end) if inside else is_end)(
            lambda: scatter.step(chunk, step, lambda block: part(chunk, block), inside)
        )

    actions = {
        "T": tok_gather.step, "C": cot_gather.step, "H": h2_gather.step, "F1": memory_unit, "F2": feed_forward, "Ro": mix_own,
        "Eo": hidden_own, "close": close, "rows": send_rows, "take": take_rows, "NP": down_parts,
        "Rs": functools.partial(scatter_step, mix_scatter, mix_part), "Es": functools.partial(scatter_step, up_scatter, up_part),
    }
    for name, *where in FRONT_ORDER:
        if name == "W":
            index, number = where
            spreads[index].phase(number)
            if number == 3 and index < 2:
                weight_stores[index].start()
        else:
            actions[name](*where)

    for store in weight_stores:
        store.wait()
    for spread in spreads:
        spread.finish()
    for chunk in range(4):
        for gather in (tok_gather, cot_gather, h2_gather):
            gather.finish(chunk)
        for which in range(2):
            for step in range(1, 4):
                stat_copy(chunk, step, which).wait_send()
    h1_store(3).wait()
    gate_store(3).wait()
    for chunk in (2, 3):
        mixed_store(chunk).wait()
        for store in hidden_stores(chunk):
            store.wait()
    small_store(X1.at[rows_of(3)], middle_out, 3, 10).wait()
    for block in (2, 3):
        down_store(3, block).wait()
    small_store(FS, dx1_out, 3, 11).wait()
    small_store(BS, branch_out, 3, 12).wait()


def front_call(tokens, cotangent, mem, gate_w, out_w, up_a_w, up_b_w, down_w, gain1, gain2, deal_row, deal_column):
    rows, width = tokens.shape
    features, channels, hidden = 4 * width, mem.shape[1], up_a_w.shape[1]
    part = rows // 4
    bf, f32 = jnp.bfloat16, jnp.float32
    shape = jax.ShapeDtypeStruct
    anywhere, vmem = pl.BlockSpec(memory_space=pl.ANY), pl.BlockSpec(memory_space=pltpu.VMEM)
    dma = pltpu.SemaphoreType.DMA
    V = pltpu.VMEM
    macs = rows * features * (6 * hidden + 2 * channels)
    return pl.pallas_call(
        front_kernel,
        name="forward",
        out_shape=(
            shape((rows, features), bf), shape((rows, features), bf), shape((rows, features), bf), shape((rows, features), bf),
            shape((rows, channels), f32), shape((rows, channels), bf), shape((rows, hidden), bf), shape((rows, hidden), bf),
            shape((rows, hidden), bf), shape((features, channels), bf), shape((channels, features), bf), shape((rows, features), f32),
            shape((rows, width), f32), shape((rows, width), f32), shape((rows, width), bf), shape((rows, channels), bf), shape((rows, 1), f32), shape((1, width), f32),
            shape((8, rows), jnp.int32), shape((8, rows), jnp.int32),
        ),
        in_specs=[anywhere] * 8 + [vmem] * 4,
        out_specs=(anywhere,) * 16 + (vmem,) * 4,
        scratch_shapes=[
            V((features, channels), bf), V((channels, features), bf), V((features, hidden), bf), V((features, hidden), bf),
            V((hidden, features), bf), V((2, 5, part, width), bf), V((2, 5, part, width), bf),
            V((part, features), bf), V((part, features), bf), V((part, features), bf), V((part, channels), f32), V((2, part, channels), bf),
            V((part, channels), bf), V((2, part, hidden), bf), V((2, part, hidden), bf), V((2, part, hidden), bf), V((rows, width), f32),
            V((rows, width), bf), V((part, width), f32), V((part, width), f32), V((part, width), f32), V((2, part, width), f32), V((part, width), bf),
            V((part, width), bf), V((rows, 1), f32), V((8, rows), f32), V((4, 8, rows), f32), V((8, rows), f32), V((4, 8, rows), f32),
            V((8, rows), jnp.int32), dma((8,)), dma((13,)), dma((8,)), dma((4, 2, 3)), dma((4, 4)), dma((4, 2, 3)), dma((4, 4)), dma((4, 2, 3)), dma((4, 4)),
            dma((4, 3)), dma((4, 5)), dma((4, 3)), dma((4, 5)), dma((5, 7)), dma((5, 8)), dma((5,)),
            dma((2, 4, 3)), dma((2, 4, 3)), dma((8,)), dma((8,)), dma((8,)), dma((8,)), dma((2,)),
        ],
        compiler_params=pltpu.CompilerParams(collective_id=2, has_side_effects=True, vmem_limit_bytes=VMEM_LIMIT),
        cost_estimate=pl.CostEstimate(flops=2 * macs, bytes_accessed=96 * 2**20, transcendentals=rows * (channels + hidden)),
    )(tokens, cotangent, mem, gate_w, out_w, up_a_w, up_b_w, down_w, gain1, gain2, deal_row, deal_column)


def silu_grad(values):
    sigma = jax.nn.sigmoid(values)
    return sigma * (1.0 + values * (1.0 - sigma))


def normalize(values):
    inverse = lax.rsqrt(jnp.mean(values * values, axis=-1, keepdims=True) + EPS)
    return (values * inverse, inverse)


def contract_rows(left, right):
    return lax.dot_general(
        left, right, (((0,), (0,)), ((), ())), preferred_element_type=jnp.float32
    )


def contract_cols(left, right):
    return lax.dot_general(
        left, right, (((1,), (1,)), ((), ())), preferred_element_type=jnp.float32
    )


def sum_scatter(part):
    return lax.psum_scatter(
        part.astype(jnp.bfloat16), "tp", scatter_dimension=1, tiled=True
    ).astype(jnp.float32)


def mean_over(values, features):
    return lax.psum(jnp.sum(values, axis=-1, keepdims=True), "tp") / features


def grad_scatter(part, dimension):
    return lax.psum_scatter(
        part.astype(jnp.bfloat16), ("fsdp", "ctx"), scatter_dimension=dimension, tiled=True
    ).astype(jnp.float32)


def middle_of(tokens, memory_tokens, cotangent, gain_first, gain_second, memory_gate, memory_out, hidden_gate, hidden_up, hidden_down):
    memory_f = memory_tokens.astype(jnp.float32)
    gathered = (
        lax.all_gather(memory_gate, ("fsdp", "ctx"), axis=0, tiled=True),
        lax.all_gather(memory_out, ("fsdp", "ctx"), axis=1, tiled=True),
        lax.all_gather(hidden_gate, ("fsdp", "ctx"), axis=0, tiled=True),
        lax.all_gather(hidden_up, ("fsdp", "ctx"), axis=0, tiled=True),
        lax.all_gather(hidden_down, ("fsdp", "ctx"), axis=1, tiled=True),
    )
    gate_w, out_w, up_a_w, up_b_w, down_w = gathered
    width = tokens.shape[1]
    column = lax.axis_index("tp") * width
    full_tokens, full_cot = (
        lax.all_gather(tokens, "tp", axis=1, tiled=True),
        lax.all_gather(cotangent, "tp", axis=1, tiled=True),
    )
    inputs = full_tokens.astype(jnp.float32)
    unit_first, inv_first = normalize(inputs)
    first = (unit_first * gain_first).astype(jnp.bfloat16)
    gate_pre = jnp.dot(first, gate_w, preferred_element_type=jnp.float32)
    activated = jax.nn.silu(gate_pre)
    mixed = (memory_f * activated).astype(jnp.bfloat16)
    features = full_tokens.shape[1]
    own = lambda array: lax.dynamic_slice_in_dim(array, column, width, array.ndim - 1)
    gain_one, gain_two = own(gain_first), own(gain_second)
    shard_tokens = tokens.astype(jnp.float32)
    middle = shard_tokens + sum_scatter(jnp.dot(mixed, out_w, preferred_element_type=jnp.float32))
    inv_second = lax.rsqrt(mean_over(middle * middle, features) + EPS)
    unit_second = middle * inv_second
    second = lax.all_gather((unit_second * gain_two).astype(jnp.bfloat16), "tp", axis=1, tiled=True)
    up_a = jnp.dot(second, up_a_w, preferred_element_type=jnp.float32)
    up_b = jnp.dot(second, up_b_w, preferred_element_type=jnp.float32)
    swish_a = jax.nn.silu(up_a)
    swished = (swish_a * up_b).astype(jnp.bfloat16)
    output = middle + sum_scatter(jnp.dot(swished, down_w, preferred_element_type=jnp.float32))
    block_out = output.astype(jnp.bfloat16)
    d_swished = contract_cols(full_cot, down_w)
    d_a = (d_swished * up_b * silu_grad(up_a)).astype(jnp.bfloat16)
    d_b = (d_swished * swish_a).astype(jnp.bfloat16)
    d_second = sum_scatter(contract_cols(d_a, up_a_w) + contract_cols(d_b, up_b_w))
    scaled = d_second * gain_two
    middle_norm = inv_second * (scaled - unit_second * mean_over(scaled * unit_second, features))
    gain_two_part = jnp.sum(d_second * unit_second, axis=0)
    d_middle = cotangent.astype(jnp.float32) + middle_norm
    unit_own = shard_tokens * inv_first
    d_branch = lax.all_gather(d_middle.astype(jnp.bfloat16), "tp", axis=1, tiled=True)
    d_mixed = contract_cols(d_branch, out_w)
    back = (d_mixed * activated).astype(jnp.bfloat16)
    d_gate = (d_mixed * memory_f * silu_grad(gate_pre)).astype(jnp.bfloat16)
    d_first = sum_scatter(contract_cols(d_gate, gate_w))
    scaled = d_first * gain_one
    input_norm = inv_first * (scaled - unit_own * mean_over(scaled * unit_own, features))
    gain_one_part = jnp.sum(d_first * unit_own, axis=0)
    parts = lax.psum(jnp.stack([gain_one_part, gain_two_part]), ("fsdp", "ctx"))
    gains = lax.all_gather(parts, "tp", axis=1, tiled=True)
    grad_gain_first, grad_gain_second = gains[0], gains[1]
    sums = (
        grad_scatter(contract_rows(first, d_gate), 0),
        grad_scatter(contract_rows(mixed, d_branch), 1),
        grad_scatter(contract_rows(second, d_a), 0),
        grad_scatter(contract_rows(second, d_b), 0),
        grad_scatter(contract_rows(swished, full_cot), 1),
    )
    return block_out, d_middle, input_norm, back, grad_gain_first, grad_gain_second, sums


def middle_on_line(
    tokens, memory, dealing, cotangent, gain_first, gain_second, memory_gate, memory_out, hidden_gate, hidden_up, hidden_down
):
    width = tokens.shape[1]
    features = 4 * width
    own = lambda array: lax.dynamic_slice_in_dim(array, lax.axis_index("tp") * width, width, 0)[None]
    gain_one, gain_two = own(gain_first), own(gain_second)
    (
        _, full_cot, second, first, gate_pre, mixed, swished, d_a, d_b, gate_w, out_w, down, middle, d_middle, d_branch, memory_tokens,
        inv_first, gain_two_part, rank, ids,
    ) = front_call(
        tokens, cotangent, memory, memory_gate, memory_out, hidden_gate, hidden_up, hidden_down, gain_first[None], gain_two,
        dealing[None], dealing[:, None],
    )
    unit_own = tokens.astype(jnp.float32) * inv_first
    d_first, down_sum, grad_memory, _, _, grad_down, grad_up_a, grad_up_b, grad_out, grad_gate, gains, stats = back_call(
        d_branch, full_cot, swished, second, d_a, d_b, mixed, first, gate_pre, memory_tokens, out_w, gate_w, unit_own, gain_one,
        gain_two_part, rank, ids, down,
    )
    block_out = (middle + down_sum).astype(jnp.bfloat16)
    grad_inputs = d_middle + inv_first * (d_first * gain_one - unit_own * (stats[0][:, None] / features))
    return (
        block_out, grad_inputs, grad_memory, gains[:, 0].reshape(features), gains[:, 1].reshape(features), grad_gate, grad_out.T,
        grad_up_a, grad_up_b, grad_down.T,
    )


def shards(
    tokens,
    memory,
    dealing,
    cotangent,
    gain_first,
    gain_second,
    memory_gate,
    memory_out,
    hidden_gate,
    hidden_up,
    hidden_down,
):
    if lax.axis_size("fsdp") == 2 and lax.axis_size("ctx") == 4 and lax.axis_size("tp") == 4:
        return middle_on_line(
            tokens, memory, dealing, cotangent, gain_first, gain_second, memory_gate, memory_out, hidden_gate, hidden_up, hidden_down
        )
    groups = lax.axis_size(("fsdp", "ctx"))
    group_index = lax.axis_index(("fsdp", "ctx"))
    rows = dealing.shape[0]
    block = rows // groups
    order = jnp.argsort(dealing)
    sent_rows = memory[order].reshape(groups, block, memory.shape[1])
    arrived = lax.all_to_all(sent_rows, ("fsdp", "ctx"), split_axis=0, concat_axis=0, tiled=True)
    arrived_ids = lax.all_to_all(
        dealing[order].reshape(groups, block),
        ("fsdp", "ctx"),
        split_axis=0,
        concat_axis=0,
        tiled=True,
    )
    places = arrived_ids.reshape(rows) - group_index * rows
    memory_tokens = arrived.reshape(rows, memory.shape[1])[jnp.argsort(places)]
    block_out, d_middle, input_norm, back, grad_gain_first, grad_gain_second, sums = middle_of(
        tokens, memory_tokens, cotangent, gain_first, gain_second, memory_gate, memory_out, hidden_gate, hidden_up, hidden_down
    )
    grad_inputs = d_middle + input_norm
    back_rows = back[places].reshape(groups, block, memory.shape[1])
    returned = lax.all_to_all(back_rows, ("fsdp", "ctx"), split_axis=0, concat_axis=0, tiled=True)
    grad_memory = returned.reshape(rows, memory.shape[1])[jnp.argsort(order)].astype(jnp.float32)
    return (
        block_out,
        grad_inputs,
        grad_memory,
        grad_gain_first,
        grad_gain_second,
        sums[0],
        sums[1],
        sums[2],
        sums[3],
        sums[4],
    )


def solution(mesh):
    in_specs = (
        P(("fsdp", "ctx"), "tp"),
        P(("fsdp", "ctx"), "tp"),
        P(("fsdp", "ctx")),
        P(("fsdp", "ctx"), "tp"),
        P(),
        P(),
        P(("fsdp", "ctx"), "tp"),
        P("tp", ("fsdp", "ctx")),
        P(("fsdp", "ctx"), "tp"),
        P(("fsdp", "ctx"), "tp"),
        P("tp", ("fsdp", "ctx")),
    )
    out_specs = (
        P(("fsdp", "ctx"), "tp"),
        P(("fsdp", "ctx"), "tp"),
        P(("fsdp", "ctx"), "tp"),
        P(),
        P(),
        P(("fsdp", "ctx"), "tp"),
        P("tp", ("fsdp", "ctx")),
        P(("fsdp", "ctx"), "tp"),
        P(("fsdp", "ctx"), "tp"),
        P("tp", ("fsdp", "ctx")),
    )
    return jax.shard_map(shards, mesh=mesh, in_specs=in_specs, out_specs=out_specs, check_vma=False)
```

```python
import functools

import jax
import jax.numpy as jnp
from jax import lax
from jax.experimental import pallas as pl
from jax.experimental.pallas import tpu as pltpu
from jax.sharding import PartitionSpec as P

EPS = 1e-06
VMEM_LIMIT = 63 * 2**20 + 2**19


MESH = pl.DeviceIdType.MESH
JOBS = 8


def dot_nt(left, right):
    return lax.dot_general(left, right, (((1,), (1,)), ((), ())), preferred_element_type=jnp.float32)


def dot_tn(left, right):
    return lax.dot_general(left, right, (((0,), (0,)), ((), ())), preferred_element_type=jnp.float32)


class Place:
    def __init__(self):
        self.f, self.c, self.t = lax.axis_index("fsdp"), lax.axis_index("ctx"), lax.axis_index("tp")
        self.y, self.k = self.c // 2, self.c % 2

    def at(self, flip_f, flip_y, flip_k):
        f = self.f + flip_f * (1 - 2 * self.f)
        y = self.y + flip_y * (1 - 2 * self.y)
        k = self.k + flip_k * (1 - 2 * self.k)
        return f, y * 2 + k

    def sibling(self):
        return (*self.at(0, 0, 1), self.t)

    def first(self):
        return (*self.at(1 - self.k, self.k, 0), self.t)

    def second(self):
        return (*self.at(self.k, 1 - self.k, 0), self.t)

    def along(self, t):
        return (self.f, self.c, t)

    def owner(self, slot, flip_k):
        alpha, beta = 1 - slot // 2, 1 - slot % 2
        parity = self.k + flip_k * (1 - 2 * self.k)
        f, c = self.at(alpha * (1 - parity) + beta * parity, beta * (1 - parity) + alpha * parity, flip_k)
        return f * 4 + c


def remote(source, target, send, recv, device):
    return pltpu.make_async_remote_copy(
        src_ref=source, dst_ref=target, send_sem=send, recv_sem=recv, device_id=device, device_id_type=MESH
    )


OTHERS = ((1, 1, 1), (1, 1, 0), (0, 1, 1), (1, 0, 1), (0, 1, 0), (1, 0, 0), (0, 0, 1))


def greet(place):
    barrier = pltpu.get_barrier_semaphore()
    for flips in OTHERS:
        pl.semaphore_signal(barrier, inc=1, device_id=(*place.at(*flips), place.t), device_id_type=MESH)
    for step in range(1, 4):
        pl.semaphore_signal(barrier, inc=1, device_id=place.along((place.t + step) % 4), device_id_type=MESH)
    pl.semaphore_wait(barrier, 10)


class Exchange:
    def __init__(self, place, source, target, send, recv):
        self.place, self.source, self.target, self.send, self.recv = place, source, target, send, recv
        self.me = place.f * 4 + place.c

    def copy(self, index):
        f, c = self.place.at(*OTHERS[index])
        group = f * 4 + c
        out = remote(self.source(group), self.target(self.me), self.send.at[index], self.recv.at[self.me], (f, c, self.place.t))
        back = remote(self.source(group), self.target(group), self.send.at[index], self.recv.at[group], (f, c, self.place.t))
        return out, back

    def stay(self):
        return pltpu.make_async_copy(self.source(self.me), self.target(self.me), self.send.at[7])

    def start(self):
        for index in range(7):
            self.copy(index)[0].start()
        self.stay().start()

    def arrived(self):
        for index in range(7):
            self.copy(index)[1].wait_recv()
        self.stay().wait()

    def finish(self):
        for index in range(7):
            self.copy(index)[0].wait_send()


def chosen(row, first, count):
    places = lax.broadcasted_iota(jnp.int32, (count, row.shape[1]), 0) + first
    return jnp.where(row == places, 1.0, 0.0).astype(jnp.bfloat16)


class Gather:
    def __init__(self, place, full, send, recv, rows, width, own=None):
        self.place, self.full, self.send, self.recv, self.rows, self.width, self.mine = place, full, send, recv, rows, width, own

    def copy(self, chunk, shard, way, hop):
        view = self.full.at[pl.ds(chunk * self.rows, self.rows), pl.ds(pl.multiple_of(shard * self.width, self.width), self.width)]
        device = self.place.along(self.place.t + 1 - 2 * way)
        source = view if hop > 0 or self.mine is None else self.mine.at[pl.ds(chunk * self.rows, self.rows)]
        return remote(source, view, self.send.at[chunk, way, hop], self.recv.at[chunk, shard], device)

    def step(self, chunk, hop):
        t = self.place.t

        @pl.when(t - hop >= 0)
        def _():
            if hop > 0:
                self.copy(chunk, t - hop, 0, hop).wait_recv()
            if hop < 3:
                @pl.when(t < 3)
                def _():
                    self.copy(chunk, t - hop, 0, hop).start()

        @pl.when(t + hop <= 3)
        def _():
            if hop > 0:
                self.copy(chunk, t + hop, 1, hop).wait_recv()
            if hop < 3:
                @pl.when(t > 0)
                def _():
                    self.copy(chunk, t + hop, 1, hop).start()

    def finish(self, chunk):
        t = self.place.t
        for hop in range(3):
            @pl.when((t - hop >= 0) & (t < 3))
            def _():
                self.copy(chunk, t - hop, 0, hop).wait_send()

            @pl.when((t + hop <= 3) & (t > 0))
            def _():
                self.copy(chunk, t + hop, 1, hop).wait_send()


class Scatter:
    def __init__(self, place, slots, send, recv):
        self.place, self.slots, self.send, self.recv = place, slots, send, recv
        self.ring = slots.shape[0]

    def block(self, step):
        t = self.place.t
        low, high = t % 2, t // 2
        return (3 * (1 - high), 2 - 2 * low + high, 1 + low, t)[step]

    def copy(self, chunk, step):
        t, block, ring = self.place.t, self.block(step), chunk % self.ring
        up = (block > t).astype(jnp.int32)
        last_down = (block == t - 1).astype(jnp.int32)
        slot = block + last_down * (4 - block)
        device = self.place.along(t - 1 + 2 * up)
        return remote(self.slots.at[ring, block], self.slots.at[ring, slot], self.send.at[chunk, step], self.recv.at[chunk, slot], device)

    def arrived(self, chunk, slot):
        view = self.slots.at[chunk % self.ring, slot]
        remote(view, view, self.send.at[chunk, 0], self.recv.at[chunk, slot], self.place.along(self.place.t)).wait_recv()

    def step(self, chunk, step, part, inside):
        block, ring = self.block(step), chunk % self.ring
        value = part(block)
        if inside:
            self.arrived(chunk, block)
            value += self.slots[ring, block].astype(jnp.float32)
        self.slots[ring, block] = value.astype(jnp.bfloat16)
        self.copy(chunk, step).start()

    def own(self, chunk, held):
        t, ring = self.place.t, chunk % self.ring

        @pl.when(t > 0)
        def _():
            self.arrived(chunk, t)
            held[...] += self.slots[ring, t].astype(jnp.float32)

        @pl.when(t < 3)
        def _():
            self.arrived(chunk, 4)
            held[...] += self.slots[ring, 4].astype(jnp.float32)

    def finish(self, chunk):
        for step in range(3):
            self.copy(chunk, step).wait_send()


def by_place(place, ends, inside):
    is_end = (place.t == 0) | (place.t == 3)
    pl.when(is_end)(ends)
    pl.when(jnp.logical_not(is_end))(inside)


def to_row(column):
    return jnp.broadcast_to(column, (column.shape[0], 128)).T[:8]


def back_kernel(
    branch_own, cot_in, swi_in, h2_in, da_in, db_in, mixed_in, h1_in, gate_in, mem_in, out_w_in, gate_w_in, xhat_in, gain_ref, gg2_ref, rank_ref, ids_ref, down_in,
    dh1_out, down_out, memory_out, term_out, returned, hd_out, hg_out, hu_out, mo_out, mg_out, gains_out, stats_out,
    A1, A2, B1, B2, MX, DB, DG, WO, WG, SR, SS, H1S, H1R, H2S, H2R, OS, RZ, GP, MT, XH, HO, GV, GR, GA, SV, SA, PLACES, ZN, NS, NO,
    load_sem, gate_sem, ag_send, ag_recv, rs_send, rs_recv, sib_send, sib_recv, h1_send, h1_recv, h2_send, h2_recv,
    out_sem, small_send, small_recv, x_send, x_recv, n_send, n_recv, n_load, n_free, sib_free, first_free, second_free,
):
    place = Place()
    t = place.t
    chunk_rows, width = XH.shape
    slab = OS.shape[0]
    span = OS.shape[1]
    cols = span // 2
    chunks = 4

    loads = {}

    def load(name, source, target, slot):
        loads[name] = pltpu.make_async_copy(source, target, load_sem.at[slot])
        loads[name].start()

    def need(*names):
        for name in names:
            if name in loads:
                loads.pop(name).wait()

    own_columns = pl.ds(pl.multiple_of(t * width, width), width)
    load("branch", branch_own, DB.at[:, own_columns], 0)
    load("cot", cot_in, A1, 1)
    load("swi", swi_in, B1, 2)
    greet(place)

    gather = Gather(place, DB, ag_send, ag_recv, chunk_rows, width)
    scatter = Scatter(place, RZ, rs_send, rs_recv)
    need("branch")

    jobs = [
        (A1, B1, 0, hd_out, 0), (A1, B1, span, hd_out, span), (A2, B2, 0, hg_out, 0), (A2, B2, span, hg_out, span),
        (A2, B1, 0, hu_out, 0), (A2, B1, span, hu_out, span), (DB, MX, 0, mo_out, 0), (A1, DG, 0, mg_out, 0),
    ]

    def tile(job, group, half):
        left, right, offset = jobs[job][:3]
        columns = pl.ds(pl.multiple_of(offset + half * cols, cols), cols)
        return dot_tn(left[:, pl.ds(pl.multiple_of(group * slab, slab), slab)], right[:, columns])

    def each_half(body):
        @pl.loop(0, 2)
        def _(half):
            body(half, pl.ds(pl.multiple_of(half * cols, cols), cols))

    def sib_copy(job, slot):
        return remote(SS.at[slot], SR.at[job % 3, slot], sib_send.at[slot], sib_recv.at[job, slot], place.sibling())

    def h1_copy(job, slot):
        return remote(H1S.at[job % 2, slot], H1R.at[job % 3, slot], h1_send.at[job % 2, slot], h1_recv.at[job, slot], place.first())

    def h2_copy(job):
        return remote(H2S.at[job % 2], H2R.at[job % 2], h2_send.at[job % 2], h2_recv.at[job], place.second())

    def to_sibling(job):
        if job >= 3:
            pl.semaphore_wait(sib_free, 1)

        @pl.loop(0, 4)
        def _(slot):
            if job >= 1:
                sib_copy(job - 1, slot).wait_send()
            group = place.owner(slot, 1)

            def body(half, at):
                SS[slot, :, at] = tile(job, group, half).astype(jnp.bfloat16)

            each_half(body)
            sib_copy(job, slot).start()

    def to_first(job):
        if job >= 3:
            pl.semaphore_wait(first_free, 1)

        @pl.loop(0, 2)
        def _(slot):
            if job >= 2:
                h1_copy(job - 2, slot).wait_send()
            group = place.owner(slot, 0)
            sib_copy(job, slot).wait_recv()

            def body(half, at):
                H1S[job % 2, slot, :, at] = (tile(job, group, half) + SR[job % 3, slot, :, at].astype(jnp.float32)).astype(jnp.bfloat16)

            each_half(body)
            h1_copy(job, slot).start()

    def to_second(job):
        if job >= 2:
            pl.semaphore_wait(second_free, 1)
            h2_copy(job - 2).wait_send()
        group = place.owner(2, 0)
        sib_copy(job, 2).wait_recv()
        h1_copy(job, 0).wait_recv()

        def body(half, at):
            H2S[job % 2, :, at] = (
                tile(job, group, half) + SR[job % 3, 2, :, at].astype(jnp.float32) + H1R[job % 3, 0, :, at].astype(jnp.float32)
            ).astype(jnp.bfloat16)

        each_half(body)
        h2_copy(job).start()

    def out_copy(job):
        return pltpu.make_async_copy(OS, jobs[job][3].at[:, pl.ds(jobs[job][4], span)], out_sem)

    def to_output(job):
        group = place.owner(3, 0)
        sib_copy(job, 3).wait_recv()
        h1_copy(job, 1).wait_recv()
        h2_copy(job).wait_recv()
        if job >= 1:
            out_copy(job - 1).wait()

        def body(half, at):
            OS[:, at] = (
                tile(job, group, half) + SR[job % 3, 3, :, at].astype(jnp.float32)
                + H1R[job % 3, 1, :, at].astype(jnp.float32) + H2R[job % 2, :, at].astype(jnp.float32)
            )

        each_half(body)
        out_copy(job).start()
        for ahead, free, device in ((3, sib_free, place.sibling()), (3, first_free, place.first()), (2, second_free, place.second())):
            if job + ahead < JOBS:
                pl.semaphore_signal(free, inc=1, device_id=device, device_id_type=MESH)

    def gate_load(chunk):
        return pltpu.make_async_copy(gate_in.at[pl.ds(chunk * chunk_rows, chunk_rows)], GP, gate_sem.at[0])

    def mem_load(chunk):
        return pltpu.make_async_copy(mem_in.at[pl.ds(chunk * chunk_rows, chunk_rows)], MT, gate_sem.at[1])

    def term_store(chunk):
        return pltpu.make_async_copy(MT, term_out.at[pl.ds(chunk * chunk_rows, chunk_rows)], gate_sem.at[2])

    def channels(chunk):
        rows = pl.ds(chunk * chunk_rows, chunk_rows)
        if chunk > 0:
            term_store(chunk - 1).wait()
        mem_load(chunk).start()
        gate_load(chunk).wait()
        mem_load(chunk).wait()

        def body(half, at):
            d_mixed = dot_nt(DB[rows, :], WO[at, :])
            pre = GP[:, at]
            sigma = jax.nn.sigmoid(pre)
            DG[rows, at] = (d_mixed * MT[:, at].astype(jnp.float32) * (sigma * (1.0 + pre * (1.0 - sigma)))).astype(jnp.bfloat16)
            MT[:, at] = (d_mixed * (pre * sigma)).astype(jnp.bfloat16)

        each_half(body)
        term_store(chunk).start()
        if chunk + 1 < chunks:
            gate_load(chunk + 1).start()

    def first_part(chunk, block):
        return dot_nt(DG[pl.ds(chunk * chunk_rows, chunk_rows), :], WG[pl.ds(pl.multiple_of(block * width, width), width), :])

    def first_step(chunk, step, inside):
        scatter.step(chunk, step, lambda block: first_part(chunk, block), inside)

    def own_copies(chunk):
        rows = pl.ds(chunk * chunk_rows, chunk_rows)
        return (
            pltpu.make_async_copy(xhat_in.at[rows], XH, gate_sem.at[3]),
            pltpu.make_async_copy(HO, dh1_out.at[rows], gate_sem.at[4]),
        )

    def own_step(chunk):
        load_xhat, store = own_copies(chunk)
        load_xhat.start()
        if chunk > 0:
            own_copies(chunk - 1)[1].wait()
        HO[...] = first_part(chunk, t)
        scatter.own(chunk, HO)
        load_xhat.wait()
        d_first, unit = HO[...], XH[...]
        product = jnp.sum(d_first * unit, axis=0, keepdims=True)
        if chunk == 0:
            GV[0, 0:1] = product
        else:
            GV[0, 0:1] += product
        scaled = d_first * gain_ref[:, own_columns]
        HO[...] = scaled
        SV[:, pl.ds(chunk * chunk_rows, chunk_rows)] = to_row(jnp.sum(scaled * unit, axis=1, keepdims=True))
        store.start()

    def sum_copy(step):
        device = (place.sibling(), place.first(), place.second())[step]
        return remote(GV.at[step], GR.at[step], small_send.at[step], small_recv.at[step], device)

    def to_line(step, what):
        device = place.along((t + step) % 4)
        if what == 0:
            return remote(SV, SA.at[t], small_send.at[2 + step], small_recv.at[2 + step], device)
        return remote(GV.at[3], GA.at[t], small_send.at[5 + step], small_recv.at[5 + step], device)

    down_scatter = Scatter(place, ZN, n_send, n_recv)

    def down_part(chunk, block, target, sem):
        source = down_in.at[pl.ds(chunk * chunk_rows, chunk_rows), pl.ds(pl.multiple_of(block * width, width), width)]
        return pltpu.make_async_copy(source, target, sem)

    def down_store(chunk):
        return pltpu.make_async_copy(NO, down_out.at[pl.ds(chunk * chunk_rows, chunk_rows)], n_load.at[2])

    def down_own(chunk):
        if chunk > 0:
            down_store(chunk - 1).wait()
        load = down_part(chunk, t, NO, n_load.at[3])
        load.start()
        load.wait()
        down_scatter.own(chunk, NO)
        down_store(chunk).start()
        down_scatter.finish(chunk)
        if chunk < 2:
            for step in (-1, 1):
                @pl.when((t + step >= 0) & (t + step <= 3))
                def _():
                    pl.semaphore_signal(
                        n_free.at[(1 - step) // 2], inc=1, device_id=place.along(t + step), device_id_type=MESH
                    )

    is_end = (t == 0) | (t == 3)
    down_order = {inside: [event[1:3] for event in BACK_ORDER if event[0] == "Ns" and event[3] == inside] for inside in (False, True)}

    def only(inside, body):
        pl.when(jnp.logical_not(is_end) if inside else is_end)(body)

    def down_load(inside, index):
        chunk, step = down_order[inside][index]
        return down_part(chunk, down_scatter.block(step), NS.at[index % 2], n_load.at[index % 2])

    def down_step(chunk, step, inside):
        index = down_order[inside].index((chunk, step))
        first_of_chunk = all(other != chunk for other, _ in down_order[inside][:index])

        def body():
            if index == 0:
                down_load(inside, 0).start()
            if index + 1 < 12:
                down_load(inside, index + 1).start()
            if chunk >= 2 and first_of_chunk:
                for side, near in enumerate((t > 0, t < 3)):
                    pl.when(near)(functools.partial(pl.semaphore_wait, n_free.at[side], 1))
            down_load(inside, index).wait()
            down_scatter.step(chunk, step, lambda block: NS[index % 2], inside)

        only(inside, body)

    channel_count = span
    block = DB.shape[0] // 8
    exchange = Exchange(
        place,
        lambda group: B2.at[pl.ds(pl.multiple_of(group * block, block), block), pl.ds(channel_count, channel_count)],
        lambda group: returned.at[pl.ds(pl.multiple_of(group * block, block), block)],
        x_send, x_recv,
    )

    def send_terms():
        term_store(3).wait()
        load("terms", term_out, B2.at[:, pl.ds(0, channel_count)], 4)
        need("terms")
        PLACES[...] = ids_ref[...] - (place.f * 4 + place.c) * DB.shape[0]

        @pl.loop(0, chunks)
        def _(part):
            rows = pl.ds(pl.multiple_of(part * chunk_rows, chunk_rows), chunk_rows)
            total = jnp.zeros((chunk_rows, channel_count), jnp.float32)
            for chunk in range(chunks):
                picked = chosen(PLACES[0:1, rows], chunk * chunk_rows, chunk_rows)
                total += dot_tn(picked, B2[chunk * chunk_rows:(chunk + 1) * chunk_rows, 0:channel_count])
            B2[rows, channel_count:2 * channel_count] = total.astype(jnp.bfloat16)

        exchange.start()

    def memory_grads():
        exchange.arrived()
        copy = pltpu.make_async_copy(returned, A2.at[:, pl.ds(0, channel_count)], load_sem.at[0])
        copy.start()
        copy.wait()

        @pl.loop(0, chunks)
        def _(part):
            rows = pl.ds(pl.multiple_of(part * chunk_rows, chunk_rows), chunk_rows)
            total = jnp.zeros((chunk_rows, channel_count), jnp.float32)
            for chunk in range(chunks):
                picked = chosen(rank_ref[0:1, rows], chunk * chunk_rows, chunk_rows)
                total += dot_tn(picked, A2[chunk * chunk_rows:(chunk + 1) * chunk_rows, 0:channel_count])
            MT[...] = total.astype(jnp.bfloat16)
            store = pltpu.make_async_copy(MT, memory_out.at[rows], gate_sem.at[0])
            store.start()
            store.wait()

    gate_load(0).start()

    def gains(number):
        if number == 0:
            for step in range(1, 4):
                to_line(step, 0).start()
            GV[0, 1:2] = gg2_ref[...]
            sum_copy(0).start()
            return
        sum_copy(number - 1).wait_recv()
        GV[number] = GV[number - 1] + GR[number - 1]
        if number < 3:
            sum_copy(number).start()
        else:
            for ahead in range(1, 4):
                to_line(ahead, 1).start()

    actions = {
        "D": gather.step, "S1": to_sibling, "S2": to_first, "S3": to_second, "S4": to_output, "Bc": channels, "Bo": own_step,
        "Bs": lambda chunk, step, inside: only(inside, lambda: first_step(chunk, step, inside)), "Ns": down_step, "No": down_own,
        "terms": send_terms, "mgrads": memory_grads, "G": gains,
    }
    wanted = {
        ("S1", 0): ("cot", "swi"), ("S1", 2): ("h2", "da"), ("S1", 4): ("db",), ("S1", 6): ("mixed",), ("S1", 7): ("h1",),
        ("Bc", 0): ("out_w", "gate_w"),
    }
    GV[0] = jnp.zeros_like(GV[0])
    for event in BACK_ORDER:
        need(*wanted.get(event, ()))
        actions[event[0]](*event[1:])
        if event == ("S2", 0):
            load("h2", h2_in, A2, 3)
            load("da", da_in, B2, 4)
            load("out_w", out_w_in, WO, 5)
            load("gate_w", gate_w_in, WG, 6)
            load("mixed", mixed_in, MX, 7)
        if event == ("S4", 1):
            load("db", db_in, B1, 2)
            load("h1", h1_in, A1, 1)

    for step in range(1, 4):
        to_line(step, 0).wait()
        to_line(step, 1).wait()
    SA[t] = SV[...]
    GA[t] = GV[3]
    stats_out[...] = SA[0] + SA[1] + SA[2] + SA[3]
    gains_out[...] = GA[...]
    for chunk in range(4):
        gather.finish(chunk)
        scatter.finish(chunk)
    for step in range(3):
        sum_copy(step).wait_send()
    for slot in range(4):
        sib_copy(JOBS - 1, slot).wait_send()
    for job in (JOBS - 2, JOBS - 1):
        for slot in range(2):
            h1_copy(job, slot).wait_send()
        h2_copy(job).wait_send()
    exchange.finish()
    down_store(3).wait()
    own_copies(3)[1].wait()
    out_copy(JOBS - 1).wait()


def back_call(branch_own, cot, swi, h2, da, db, mixed, h1, gate, mem, out_w, gate_w, xhat, gain, gg2, rank, ids, down):
    rows, features = cot.shape
    channels, hidden = mixed.shape[1], swi.shape[1]
    width, slab, part = features // 4, features // 8, rows // 4
    bf, f32 = jnp.bfloat16, jnp.float32
    shape = jax.ShapeDtypeStruct
    anywhere, vmem = pl.BlockSpec(memory_space=pl.ANY), pl.BlockSpec(memory_space=pltpu.VMEM)
    dma = pltpu.SemaphoreType.DMA
    regular = pltpu.SemaphoreType.REGULAR
    V = pltpu.VMEM
    macs = rows * features * (3 * hidden + 4 * channels)
    return pl.pallas_call(
        back_kernel,
        name="backward",
        out_shape=(
            shape((rows, width), f32), shape((rows, width), f32), shape((rows, channels), bf), shape((rows, channels), bf), shape((rows, channels), bf),
            shape((slab, hidden), f32), shape((slab, hidden), f32),
            shape((slab, hidden), f32), shape((slab, channels), f32), shape((slab, channels), f32), shape((4, 8, width), f32),
            shape((8, rows), f32),
        ),
        in_specs=[anywhere] * 13 + [vmem] * 4 + [anywhere],
        out_specs=(anywhere,) * 10 + (vmem,) * 2,
        scratch_shapes=[
            V((rows, features), bf), V((rows, features), bf), V((rows, hidden), bf), V((rows, hidden), bf), V((rows, channels), bf),
            V((rows, features), bf), V((rows, channels), bf), V((channels, features), bf), V((features, channels), bf),
            V((3, 4, slab, channels), bf), V((4, slab, channels), bf), V((2, 2, slab, channels), bf), V((3, 2, slab, channels), bf),
            V((2, slab, channels), bf), V((2, slab, channels), bf), V((slab, channels), f32), V((4, 5, part, width), bf),
            V((part, channels), f32), V((part, channels), bf), V((part, width), f32), V((part, width), f32),
            V((4, 8, width), f32), V((3, 8, width), f32), V((4, 8, width), f32), V((8, rows), f32), V((4, 8, rows), f32),
            V((8, rows), jnp.int32), V((2, 5, part, width), bf), V((2, part, width), f32), V((part, width), f32), dma((8,)), dma((5,)), dma((4, 2, 3)), dma((4, 4)), dma((4, 3)), dma((4, 5)), dma((4,)), dma((JOBS, 4)), dma((2, 2)),
            dma((JOBS, 2)), dma((2,)), dma((JOBS,)), dma, dma((9,)), dma((9,)), dma((8,)), dma((8,)), dma((4, 3)), dma((4, 5)), dma((4,)), pltpu.SemaphoreType.REGULAR((2,)), regular, regular, regular,
        ],
        compiler_params=pltpu.CompilerParams(collective_id=1, has_side_effects=True, vmem_limit_bytes=VMEM_LIMIT),
        cost_estimate=pl.CostEstimate(flops=2 * macs, bytes_accessed=64 * 2**20, transcendentals=rows * channels),
    )(branch_own, cot, swi, h2, da, db, mixed, h1, gate, mem, out_w, gate_w, xhat, gain, gg2, rank, ids, down)


FRONT_ORDER = (
    ("T", 0, 0), ("W", 0, 0), ("T", 1, 0), ("T", 2, 0), ("T", 3, 0), ("W", 1, 0), ("C", 1, 0), ("rows",), ("W", 0, 1),
    ("T", 1, 1), ("W", 1, 1), ("W", 4, 0), ("T", 0, 1), ("C", 2, 0), ("T", 1, 2), ("T", 0, 2), ("C", 0, 0), ("take",),
    ("W", 2, 0), ("T", 2, 1), ("W", 1, 2), ("W", 3, 0), ("C", 2, 1), ("C", 3, 0), ("T", 3, 1), ("T", 0, 3), ("T", 1, 3),
    ("W", 0, 2), ("W", 0, 3), ("W", 1, 3), ("F1", 0), ("Rs", 0, 1, False), ("Rs", 0, 0, False), ("Rs", 0, 2, False),
    ("C", 3, 1), ("F1", 1), ("Rs", 1, 0, False), ("Rs", 0, 0, True), ("C", 1, 1), ("T", 2, 2), ("Rs", 1, 0, True),
    ("T", 3, 2), ("Rs", 1, 1, False), ("Rs", 0, 2, True), ("W", 4, 1), ("Rs", 1, 2, False), ("T", 3, 3),
    ("Rs", 1, 2, True), ("Rs", 0, 1, True), ("Rs", 1, 1, True), ("Ro", 0), ("H", 0, 0), ("C", 0, 1), ("W", 2, 1),
    ("H", 0, 1), ("T", 2, 3), ("F1", 2), ("Rs", 2, 0, False), ("C", 0, 2), ("Rs", 2, 1, False), ("C", 1, 2),
    ("Rs", 2, 2, False), ("Rs", 2, 0, True), ("Ro", 1), ("H", 1, 0), ("W", 3, 1), ("W", 4, 2), ("F1", 3),
    ("Rs", 2, 1, True), ("W", 2, 2), ("Rs", 2, 2, True), ("H", 1, 1), ("Rs", 3, 0, False), ("Rs", 3, 1, False),
    ("W", 3, 2), ("Rs", 3, 0, True), ("H", 0, 2), ("C", 1, 3), ("W", 2, 3), ("H", 1, 2), ("W", 4, 3), ("Ro", 2),
    ("Rs", 3, 1, True), ("Rs", 3, 2, True), ("H", 2, 0), ("C", 0, 3), ("Rs", 3, 2, False), ("H", 0, 3), ("W", 3, 3),
    ("F2", 0), ("Es", 0, 0, False), ("Es", 0, 1, False), ("H", 2, 1), ("Ro", 3), ("C", 2, 2), ("H", 3, 0), ("H", 1, 3),
    ("F2", 1), ("Es", 1, 0, False), ("Es", 1, 1, False), ("Es", 0, 2, True), ("Es", 0, 2, False), ("H", 2, 2),
    ("Es", 1, 2, False), ("Es", 0, 0, True), ("C", 3, 2), ("H", 3, 1), ("C", 2, 3), ("H", 2, 3), ("F2", 2),
    ("Es", 2, 1, False), ("Es", 2, 0, False), ("Es", 0, 1, True), ("Es", 1, 2, True), ("H", 3, 2), ("Es", 2, 2, False),
    ("NP", 0), ("Es", 1, 0, True), ("Eo", 0), ("H", 3, 3), ("C", 3, 3), ("F2", 3), ("close", 0), ("Es", 3, 0, False),
    ("Es", 2, 0, True), ("Es", 2, 2, True), ("Es", 3, 1, False), ("Es", 1, 1, True), ("NP", 1), ("NP", 2), ("Eo", 1),
    ("Es", 3, 0, True), ("Es", 2, 1, True), ("Es", 3, 2, True), ("Es", 3, 2, False), ("Es", 3, 1, True), ("close", 1),
    ("Eo", 2), ("NP", 3), ("close", 2), ("Eo", 3), ("close", 3),
)
BACK_ORDER = (
    ("D", 0, 0), ("S1", 0), ("D", 1, 0), ("S2", 0), ("Ns", 0, 1, False), ("D", 2, 0), ("Ns", 1, 0, False), ("S1", 1),
    ("D", 3, 0), ("S2", 1), ("S1", 2), ("Ns", 1, 1, False), ("D", 0, 1), ("S3", 0), ("S2", 2), ("D", 0, 2), ("D", 2, 1),
    ("Ns", 0, 0, False), ("D", 0, 3), ("Ns", 0, 2, False), ("Bc", 0), ("S3", 1), ("D", 1, 1), ("S4", 0), ("S1", 3),
    ("S2", 3), ("Ns", 1, 2, False), ("D", 1, 2), ("D", 1, 3), ("D", 2, 2), ("Ns", 0, 0, True), ("Bs", 0, 1, False),
    ("S3", 2), ("Bc", 1), ("D", 3, 1), ("Bs", 1, 0, False), ("S4", 1), ("Bs", 0, 0, False), ("Ns", 1, 0, True),
    ("S1", 4), ("D", 3, 2), ("D", 2, 3), ("S2", 4), ("Bc", 2), ("D", 3, 3), ("S4", 2), ("Bs", 1, 1, False),
    ("Bs", 0, 2, True), ("Bs", 2, 0, False), ("Bc", 3), ("Bs", 3, 0, False), ("Ns", 0, 1, True), ("Ns", 0, 2, True),
    ("S3", 3), ("Bs", 1, 2, False), ("Ns", 1, 1, True), ("Bs", 0, 0, True), ("S3", 4), ("S1", 5), ("No", 0),
    ("Bs", 1, 0, True), ("S2", 5), ("S4", 3), ("S1", 6), ("Bs", 3, 1, False), ("Bs", 2, 1, False), ("Bs", 1, 1, True),
    ("S4", 4), ("Bs", 2, 0, True), ("Ns", 2, 0, False), ("Ns", 1, 2, True), ("Ns", 2, 1, False), ("Bs", 0, 2, False),
    ("S3", 5), ("Bs", 3, 2, False), ("Bs", 3, 0, True), ("terms",), ("S2", 6), ("Bs", 1, 2, True), ("No", 1),
    ("Ns", 3, 0, False), ("Bs", 2, 1, True), ("Bs", 2, 2, False), ("S4", 5), ("Bs", 3, 1, True), ("S1", 7),
    ("Ns", 2, 0, True), ("Ns", 3, 1, False), ("Ns", 2, 2, False), ("Bs", 3, 2, True), ("S2", 7), ("Bs", 0, 1, True),
    ("Bo", 0), ("Ns", 2, 1, True), ("Bs", 2, 2, True), ("Ns", 2, 2, True), ("mgrads",), ("Ns", 3, 2, False),
    ("Ns", 3, 0, True), ("S3", 6), ("Bo", 1), ("Bo", 2), ("Bo", 3), ("G", 0), ("Ns", 3, 2, True), ("Ns", 3, 1, True),
    ("S3", 7), ("G", 1), ("G", 2), ("No", 2), ("G", 3), ("No", 3), ("S4", 6), ("S4", 7),
)


class Spread:
    def __init__(self, place, index, shard, view, send, recv, local):
        self.place, self.index, self.shard, self.view, self.send, self.recv = place, index, shard, view, send, recv
        self.local = local

    def group(self, *flips):
        f, c = self.place.at(*flips)
        return f * 4 + c

    def copy(self, group, device, slot):
        view = self.view(group)
        source = self.shard if slot < 3 else view
        return remote(source, view, self.send.at[self.index, slot], self.recv.at[self.index, group], device)

    def routes(self):
        place = self.place
        me, both = self.group(0, 0, 0), self.group(1, 1, 0)
        first, second = self.group(1 - place.k, place.k, 0), self.group(place.k, 1 - place.k, 0)
        return (
            (me, place.first()), (me, place.second()), (me, place.sibling()), (second, place.first()), (first, place.sibling()),
            (second, place.sibling()), (both, place.sibling()),
        )

    def start(self, slot):
        group, device = self.routes()[slot]
        self.copy(group, device, slot).start()

    def arrived(self, group):
        self.copy(group, self.place.sibling(), 3).wait_recv()

    def stay(self):
        return pltpu.make_async_copy(self.shard, self.view(self.group(0, 0, 0)), self.local.at[self.index])

    def phase(self, number):
        routes = self.routes()
        if number == 0:
            for slot in range(3):
                self.start(slot)
            self.stay().start()
        if number == 1:
            self.arrived(routes[3][0])
            self.start(3)
            self.start(5)
            self.arrived(routes[4][0])
            self.start(4)
        if number == 2:
            self.arrived(routes[6][0])
            self.start(6)
        if number == 3:
            for flips in ((0, 0), (0, 1), (1, 0), (1, 1)):
                self.arrived(self.group(*flips, 1))
            self.stay().wait()

    def finish(self):
        for slot, (group, device) in enumerate(self.routes()):
            self.copy(group, device, slot).wait_send()


def to_column(row):
    return jnp.broadcast_to(row, (128, row.shape[1])).T[:, 0:1]


def front_kernel(
    tokens, cotangent, mem_in, gate_w, out_w, up_a_w, up_b_w, down_w, gain1, gain2, deal_row,
    tok_full, cot_full, h2_full, h1_out, gate_out, mixed_out, swi_out, da_out, db_out, gate_w_out, out_w_out, down_out, middle_out, dx1_out, branch_out, mem_out, xhat_out,
    inv_out, gg2_out, rank_out, ids_out,
    WG, WO, WA, WB, WD, Z1, ZE, XC, CC, H1C, GPS, MXS, MT, SWI, DA, DB, X1, H2O, HO, DHQ, FS, NS, BS, I2, SV, SA, SV2, SA2, SENT,
    load_sem, store_sem, stage_sem, t_send, t_recv, c_send, c_recv, h_send, h_recv, r_send, r_recv, e_send, e_recv,
    w_send, w_recv, w_local, s_send, s_recv, x_send, x_recv, i_send, i_recv, n_sem,
):
    place = Place()
    t = place.t
    rows, features = tok_full.shape
    chunk_rows, width = HO.shape
    channels, hidden = MXS.shape[2], SWI.shape[2]
    half = channels // 2
    slab = features // 8
    own_columns = pl.ds(pl.multiple_of(t * width, width), width)

    def rows_of(chunk):
        return pl.ds(chunk * chunk_rows, chunk_rows)

    def columns_of(block, size):
        return pl.ds(pl.multiple_of(block * size, size), size)

    def keep(index, source, target):
        return pltpu.make_async_copy(source, target, stage_sem.at[index])

    own_tokens = keep(0, tokens, tok_full.at[:, own_columns])
    own_cot = keep(1, cotangent, cot_full.at[:, own_columns])
    own_tokens.start()
    own_cot.start()
    greet(place)

    tok_gather = Gather(place, tok_full, t_send, t_recv, chunk_rows, width, tokens)
    cot_gather = Gather(place, cot_full, c_send, c_recv, chunk_rows, width, cotangent)
    h2_gather = Gather(place, h2_full, h_send, h_recv, chunk_rows, width, H2O)
    mix_scatter = Scatter(place, Z1, r_send, r_recv)
    up_scatter = Scatter(place, ZE, e_send, e_recv)
    spreads = [
        Spread(place, index, shard, view, w_send, w_recv, w_local)
        for index, (shard, view) in enumerate((
            (gate_w, lambda group: WG.at[columns_of(group, slab), :]),
            (out_w, lambda group: WO.at[:, columns_of(group, slab)]),
            (up_a_w, lambda group: WA.at[columns_of(group, slab), :]),
            (up_b_w, lambda group: WB.at[columns_of(group, slab), :]),
            (down_w, lambda group: WD.at[:, columns_of(group, slab)]),
        ))
    ]

    block = rows // 8

    def quarter(ref, index):
        return ref.at[index // 2, :, pl.ds(pl.multiple_of((index % 2) * channels, channels), channels)]

    def eighth(ref, group):
        return ref.at[
            group // 4, pl.ds(pl.multiple_of((group % 2) * block, block), block),
            pl.ds(pl.multiple_of(((group // 2) % 2) * channels, channels), channels),
        ]

    def lanes(ref, group):
        return ref.at[:, pl.ds(pl.multiple_of(group * block, block), block)]

    rows_exchange = Exchange(place, lambda group: eighth(DA, group), lambda group: eighth(SWI, group), x_send, x_recv)
    ids_exchange = Exchange(place, lambda group: lanes(SENT, group), lambda group: lanes(ids_out, group), i_send, i_recv)

    def send_rows():
        loads = [pltpu.make_async_copy(mem_in.at[rows_of(index)], quarter(DB, index), load_sem.at[4 + index]) for index in range(4)]
        for copy in loads:
            copy.start()
        row = deal_row[...].astype(jnp.float32)
        columns = [to_column(row[:, index * chunk_rows:(index + 1) * chunk_rows]) for index in range(4)]
        rank = jnp.zeros((1, rows), jnp.float32)
        for chunk in range(4):
            rank += jnp.sum(jnp.where(columns[chunk] < row, 1.0, 0.0), axis=0, keepdims=True)
        rank_out[...] = jnp.broadcast_to(rank, (8, rows)).astype(jnp.int32)
        spots = lax.broadcasted_iota(jnp.int32, (chunk_rows, rows), 1).astype(jnp.float32)
        ordered = jnp.zeros((1, rows), jnp.float32)
        for chunk in range(4):
            column = columns[chunk]
            place_of = jnp.sum(jnp.where(row < column, 1.0, 0.0), axis=1, keepdims=True)
            ordered += jnp.sum(jnp.where(place_of == spots, column, 0.0), axis=0, keepdims=True)
        SENT[...] = jnp.broadcast_to(ordered, (8, rows)).astype(jnp.int32)
        ids_exchange.start()
        for copy in loads:
            copy.wait()

        @pl.loop(0, 4)
        def _(index):
            total = jnp.zeros((chunk_rows, channels), jnp.float32)
            for other in range(4):
                picked = chosen(rank_out[0:1, rows_of(other)], index * chunk_rows, chunk_rows)
                total += jnp.dot(picked, quarter(DB, other)[...], preferred_element_type=jnp.float32)
            quarter(DA, index)[...] = total.astype(jnp.bfloat16)

        rows_exchange.start()

    def mem_store(chunk):
        return pltpu.make_async_copy(MXS.at[chunk % 2], mem_out.at[rows_of(chunk)], load_sem.at[4 + chunk])

    def take_rows():
        ids_exchange.arrived()
        rows_exchange.arrived()
        for chunk in range(4):
            if chunk > 1:
                mem_store(chunk - 2).wait()
            first = rows_exchange.me * rows + chunk * chunk_rows
            total = jnp.zeros((chunk_rows, channels), jnp.float32)
            for other in range(4):
                picked = chosen(ids_out[0:1, rows_of(other)], first, chunk_rows)
                total += jnp.dot(picked, quarter(SWI, other)[...], preferred_element_type=jnp.float32)
            MXS[chunk % 2] = total.astype(jnp.bfloat16)
            mem_store(chunk).start()
        for chunk in (2, 3):
            mem_store(chunk).wait()
        rows_exchange.finish()
        ids_exchange.finish()

    def h1_store(chunk):
        return pltpu.make_async_copy(H1C, h1_out.at[rows_of(chunk)], store_sem.at[0])

    def gate_store(chunk):
        return pltpu.make_async_copy(GPS, gate_out.at[rows_of(chunk)], store_sem.at[1])

    def mixed_store(chunk):
        return pltpu.make_async_copy(MXS.at[chunk % 2], mixed_out.at[rows_of(chunk)], store_sem.at[2 + chunk % 2])

    def hidden_stores(chunk):
        slot = chunk % 3
        return [
            pltpu.make_async_copy(source.at[slot], target.at[rows_of(chunk)], store_sem.at[4 + 3 * index + slot])
            for index, (source, target) in enumerate(((SWI, swi_out), (DA, da_out), (DB, db_out)))
        ]

    def own_h2_store(chunk):
        return pltpu.make_async_copy(H2O.at[rows_of(chunk)], h2_full.at[rows_of(chunk), own_columns], stage_sem.at[4 + chunk])

    def small_store(source, target, chunk, index):
        return pltpu.make_async_copy(source, target.at[rows_of(chunk)], store_sem.at[index])

    def fetch(source, target, index):
        copy = pltpu.make_async_copy(source, target, load_sem.at[index])
        copy.start()
        return copy

    def stat_copy(chunk, step, which):
        source, target = ((SV, SA), (SV2, SA2))[which]
        columns = rows_of(chunk)
        return remote(
            source.at[:, columns], target.at[t, :, columns], s_send.at[which, chunk, step - 1], s_recv.at[which, chunk, step - 1],
            place.along((t + step) % 4),
        )

    def stats(chunk, which):
        source, target = ((SV, SA), (SV2, SA2))[which]
        for step in range(1, 4):
            stat_copy(chunk, step, which).wait_recv()
        total = source[0:1, rows_of(chunk)]
        for step in range(1, 4):
            total = total + target[(t + step) % 4, 0:1, rows_of(chunk)]
        return to_column(total)

    def memory_unit(chunk):
        if chunk == 0:
            own_tokens.wait()
        load = fetch(tok_full.at[rows_of(chunk)], XC, 1)
        mem_load = fetch(mem_out.at[rows_of(chunk)], MT, 0)
        if chunk > 0:
            h1_store(chunk - 1).wait()
        load.wait()
        square = jnp.zeros((chunk_rows, 1), jnp.float32)
        for block in range(4):
            values = XC[:, block * width:(block + 1) * width].astype(jnp.float32)
            square += jnp.sum(values * values, axis=1, keepdims=True)
        inverse = lax.rsqrt(square / features + EPS)
        inv_out[:, rows_of(chunk)] = to_row(inverse)
        HO[...] = XC[:, own_columns].astype(jnp.float32) * inverse
        small_store(HO, xhat_out, chunk, 16).start()
        for block in range(4):
            at = slice(block * width, (block + 1) * width)
            H1C[:, at] = (XC[:, at].astype(jnp.float32) * inverse * gain1[:, at]).astype(jnp.bfloat16)
        h1_store(chunk).start()
        mem_load.wait()
        if chunk > 0:
            gate_store(chunk - 1).wait()
        if chunk > 1:
            mixed_store(chunk - 2).wait()

        @pl.loop(0, 2)
        def _(part):
            at = columns_of(part, half)
            pre = jnp.dot(H1C[...], WG[:, at], preferred_element_type=jnp.float32)
            GPS[:, at] = pre
            MXS[chunk % 2, :, at] = (MT[:, at].astype(jnp.float32) * (pre * jax.nn.sigmoid(pre))).astype(jnp.bfloat16)

        gate_store(chunk).start()
        mixed_store(chunk).start()
        small_store(HO, xhat_out, chunk, 16).wait()

    def mix_part(chunk, block):
        return jnp.dot(MXS[chunk % 2], WO[:, columns_of(block, width)], preferred_element_type=jnp.float32)

    def mix_own(chunk):
        load = fetch(tokens.at[rows_of(chunk)], CC.at[:, 0:width], 2)
        if chunk > 0:
            small_store(X1.at[rows_of(chunk)], middle_out, chunk - 1, 13).wait()
        HO[...] = mix_part(chunk, t)
        mix_scatter.own(chunk, HO)
        load.wait()
        middle = CC[:, 0:width].astype(jnp.float32) + HO[...]
        X1[rows_of(chunk)] = middle
        H2O[rows_of(chunk)] = (middle * gain2[:, own_columns]).astype(jnp.bfloat16)
        own_h2_store(chunk).start()
        SV[:, rows_of(chunk)] = to_row(jnp.sum(middle * middle, axis=1, keepdims=True))
        small_store(X1.at[rows_of(chunk)], middle_out, chunk, 13).start()
        mix_scatter.finish(chunk)
        for step in range(1, 4):
            stat_copy(chunk, step, 0).start()

    def feed_forward(chunk):
        own_h2_store(chunk).wait()
        if chunk == 0:
            own_cot.wait()
        loads = [fetch(h2_full.at[rows_of(chunk)], XC, 1), fetch(cot_full.at[rows_of(chunk)], CC, 3)]
        inverse = lax.rsqrt(stats(chunk, 0) / features + EPS)
        I2[:, rows_of(chunk)] = to_row(inverse)
        if chunk > 2:
            for store in hidden_stores(chunk - 3):
                store.wait()
        for load in loads:
            load.wait()

        @pl.loop(0, 4)
        def _(part):
            at = columns_of(part, hidden // 4)
            up_a = jnp.dot(XC[...], WA[:, at], preferred_element_type=jnp.float32) * inverse
            up_b = jnp.dot(XC[...], WB[:, at], preferred_element_type=jnp.float32) * inverse
            d_swi = dot_nt(CC[...], WD[at, :])
            sigma = jax.nn.sigmoid(up_a)
            swish = up_a * sigma
            SWI[chunk % 3, :, at] = (swish * up_b).astype(jnp.bfloat16)
            d_swi = d_swi * inverse
            DA[chunk % 3, :, at] = (d_swi * up_b * (sigma * (1.0 + up_a * (1.0 - sigma)))).astype(jnp.bfloat16)
            DB[chunk % 3, :, at] = (d_swi * swish).astype(jnp.bfloat16)

        for store in hidden_stores(chunk):
            store.start()

    def down_store(chunk, block):
        return pltpu.make_async_copy(NS.at[block % 2], down_out.at[rows_of(chunk), columns_of(block, width)], n_sem.at[block % 2])

    def down_parts(chunk):
        for block in range(4):
            if chunk > 0 or block > 1:
                down_store(chunk, block).wait()
            NS[block % 2] = jnp.dot(SWI[chunk % 3], WD[:, columns_of(block, width)], preferred_element_type=jnp.float32)
            down_store(chunk, block).start()

    def up_part(chunk, block):
        at = columns_of(block, width)
        return dot_nt(DA[chunk % 3], WA[at, :]) + dot_nt(DB[chunk % 3], WB[at, :])

    def hidden_own(chunk):
        HO[...] = up_part(chunk, t)
        up_scatter.own(chunk, HO)
        middle = X1[rows_of(chunk)]
        d_second = HO[...]
        grads = jnp.sum(d_second * middle, axis=0, keepdims=True)
        if chunk == 0:
            gg2_out[...] = grads
        else:
            gg2_out[...] += grads
        scaled = d_second * gain2[:, own_columns]
        DHQ[...] = scaled
        SV2[:, rows_of(chunk)] = to_row(jnp.sum(scaled * middle, axis=1, keepdims=True) * to_column(I2[0:1, rows_of(chunk)]))
        up_scatter.finish(chunk)
        for step in range(1, 4):
            stat_copy(chunk, step, 1).start()

    def close(chunk):
        load = fetch(cotangent.at[rows_of(chunk)], CC.at[:, 0:width], 2)
        mean = stats(chunk, 1) / features
        if chunk > 0:
            small_store(FS, dx1_out, chunk - 1, 14).wait()
            small_store(BS, branch_out, chunk - 1, 15).wait()
        load.wait()
        unit = X1[rows_of(chunk)] * to_column(I2[0:1, rows_of(chunk)])
        total = CC[:, 0:width].astype(jnp.float32) + DHQ[...] - unit * mean
        FS[...] = total
        BS[...] = total.astype(jnp.bfloat16)
        small_store(FS, dx1_out, chunk, 14).start()
        small_store(BS, branch_out, chunk, 15).start()

    weight_stores = [
        pltpu.make_async_copy(WG, gate_w_out, stage_sem.at[2]), pltpu.make_async_copy(WO, out_w_out, stage_sem.at[3]),
    ]
    is_end = (t == 0) | (t == 3)

    def scatter_step(scatter, part, chunk, step, inside):
        pl.when(jnp.logical_not(is_end) if inside else is_end)(
            lambda: scatter.step(chunk, step, lambda block: part(chunk, block), inside)
        )

    actions = {
        "T": tok_gather.step, "C": cot_gather.step, "H": h2_gather.step, "F1": memory_unit, "F2": feed_forward, "Ro": mix_own,
        "Eo": hidden_own, "close": close, "rows": send_rows, "take": take_rows, "NP": down_parts,
        "Rs": functools.partial(scatter_step, mix_scatter, mix_part), "Es": functools.partial(scatter_step, up_scatter, up_part),
    }
    for name, *where in FRONT_ORDER:
        if name == "W":
            index, number = where
            spreads[index].phase(number)
            if number == 3 and index < 2:
                weight_stores[index].start()
        else:
            actions[name](*where)

    for store in weight_stores:
        store.wait()
    for spread in spreads:
        spread.finish()
    for chunk in range(4):
        for gather in (tok_gather, cot_gather, h2_gather):
            gather.finish(chunk)
        for which in range(2):
            for step in range(1, 4):
                stat_copy(chunk, step, which).wait_send()
    h1_store(3).wait()
    gate_store(3).wait()
    for chunk in (2, 3):
        mixed_store(chunk).wait()
    for chunk in (1, 2, 3):
        for store in hidden_stores(chunk):
            store.wait()
    small_store(X1.at[rows_of(3)], middle_out, 3, 13).wait()
    for block in (2, 3):
        down_store(3, block).wait()
    small_store(FS, dx1_out, 3, 14).wait()
    small_store(BS, branch_out, 3, 15).wait()


def front_call(tokens, cotangent, mem, gate_w, out_w, up_a_w, up_b_w, down_w, gain1, gain2, deal_row):
    rows, width = tokens.shape
    features, channels, hidden = 4 * width, mem.shape[1], up_a_w.shape[1]
    part = rows // 4
    bf, f32 = jnp.bfloat16, jnp.float32
    shape = jax.ShapeDtypeStruct
    anywhere, vmem = pl.BlockSpec(memory_space=pl.ANY), pl.BlockSpec(memory_space=pltpu.VMEM)
    dma = pltpu.SemaphoreType.DMA
    V = pltpu.VMEM
    macs = rows * features * (6 * hidden + 2 * channels)
    return pl.pallas_call(
        front_kernel,
        name="forward",
        out_shape=(
            shape((rows, features), bf), shape((rows, features), bf), shape((rows, features), bf), shape((rows, features), bf),
            shape((rows, channels), f32), shape((rows, channels), bf), shape((rows, hidden), bf), shape((rows, hidden), bf),
            shape((rows, hidden), bf), shape((features, channels), bf), shape((channels, features), bf), shape((rows, features), f32),
            shape((rows, width), f32), shape((rows, width), f32), shape((rows, width), bf), shape((rows, channels), bf), shape((rows, width), f32), shape((8, rows), f32),
            shape((1, width), f32),
            shape((8, rows), jnp.int32), shape((8, rows), jnp.int32),
        ),
        in_specs=[anywhere] * 8 + [vmem] * 3,
        out_specs=(anywhere,) * 17 + (vmem,) * 4,
        scratch_shapes=[
            V((features, channels), bf), V((channels, features), bf), V((features, hidden), bf), V((features, hidden), bf),
            V((hidden, features), bf), V((2, 5, part, width), bf), V((3, 5, part, width), bf),
            V((part, features), bf), V((part, features), bf), V((part, features), bf), V((part, channels), f32), V((2, part, channels), bf),
            V((part, channels), bf), V((3, part, hidden), bf), V((3, part, hidden), bf), V((3, part, hidden), bf), V((rows, width), f32),
            V((rows, width), bf), V((part, width), f32), V((part, width), f32), V((part, width), f32), V((2, part, width), f32), V((part, width), bf),
            V((8, rows), f32), V((8, rows), f32), V((4, 8, rows), f32), V((8, rows), f32), V((4, 8, rows), f32),
            V((8, rows), jnp.int32), dma((8,)), dma((17,)), dma((8,)), dma((4, 2, 3)), dma((4, 4)), dma((4, 2, 3)), dma((4, 4)), dma((4, 2, 3)), dma((4, 4)),
            dma((4, 3)), dma((4, 5)), dma((4, 3)), dma((4, 5)), dma((5, 7)), dma((5, 8)), dma((5,)),
            dma((2, 4, 3)), dma((2, 4, 3)), dma((8,)), dma((8,)), dma((8,)), dma((8,)), dma((2,)),
        ],
        compiler_params=pltpu.CompilerParams(collective_id=2, has_side_effects=True, vmem_limit_bytes=VMEM_LIMIT),
        cost_estimate=pl.CostEstimate(flops=2 * macs, bytes_accessed=96 * 2**20, transcendentals=rows * (channels + hidden)),
    )(tokens, cotangent, mem, gate_w, out_w, up_a_w, up_b_w, down_w, gain1, gain2, deal_row)


def silu_grad(values):
    sigma = jax.nn.sigmoid(values)
    return sigma * (1.0 + values * (1.0 - sigma))


def normalize(values):
    inverse = lax.rsqrt(jnp.mean(values * values, axis=-1, keepdims=True) + EPS)
    return (values * inverse, inverse)


def contract_rows(left, right):
    return lax.dot_general(
        left, right, (((0,), (0,)), ((), ())), preferred_element_type=jnp.float32
    )


def contract_cols(left, right):
    return lax.dot_general(
        left, right, (((1,), (1,)), ((), ())), preferred_element_type=jnp.float32
    )


def sum_scatter(part):
    return lax.psum_scatter(
        part.astype(jnp.bfloat16), "tp", scatter_dimension=1, tiled=True
    ).astype(jnp.float32)


def mean_over(values, features):
    return lax.psum(jnp.sum(values, axis=-1, keepdims=True), "tp") / features


def grad_scatter(part, dimension):
    return lax.psum_scatter(
        part.astype(jnp.bfloat16), ("fsdp", "ctx"), scatter_dimension=dimension, tiled=True
    ).astype(jnp.float32)


def middle_of(tokens, memory_tokens, cotangent, gain_first, gain_second, memory_gate, memory_out, hidden_gate, hidden_up, hidden_down):
    memory_f = memory_tokens.astype(jnp.float32)
    gathered = (
        lax.all_gather(memory_gate, ("fsdp", "ctx"), axis=0, tiled=True),
        lax.all_gather(memory_out, ("fsdp", "ctx"), axis=1, tiled=True),
        lax.all_gather(hidden_gate, ("fsdp", "ctx"), axis=0, tiled=True),
        lax.all_gather(hidden_up, ("fsdp", "ctx"), axis=0, tiled=True),
        lax.all_gather(hidden_down, ("fsdp", "ctx"), axis=1, tiled=True),
    )
    gate_w, out_w, up_a_w, up_b_w, down_w = gathered
    width = tokens.shape[1]
    column = lax.axis_index("tp") * width
    full_tokens, full_cot = (
        lax.all_gather(tokens, "tp", axis=1, tiled=True),
        lax.all_gather(cotangent, "tp", axis=1, tiled=True),
    )
    inputs = full_tokens.astype(jnp.float32)
    unit_first, inv_first = normalize(inputs)
    first = (unit_first * gain_first).astype(jnp.bfloat16)
    gate_pre = jnp.dot(first, gate_w, preferred_element_type=jnp.float32)
    activated = jax.nn.silu(gate_pre)
    mixed = (memory_f * activated).astype(jnp.bfloat16)
    features = full_tokens.shape[1]
    own = lambda array: lax.dynamic_slice_in_dim(array, column, width, array.ndim - 1)
    gain_one, gain_two = own(gain_first), own(gain_second)
    shard_tokens = tokens.astype(jnp.float32)
    middle = shard_tokens + sum_scatter(jnp.dot(mixed, out_w, preferred_element_type=jnp.float32))
    inv_second = lax.rsqrt(mean_over(middle * middle, features) + EPS)
    unit_second = middle * inv_second
    second = lax.all_gather((unit_second * gain_two).astype(jnp.bfloat16), "tp", axis=1, tiled=True)
    up_a = jnp.dot(second, up_a_w, preferred_element_type=jnp.float32)
    up_b = jnp.dot(second, up_b_w, preferred_element_type=jnp.float32)
    swish_a = jax.nn.silu(up_a)
    swished = (swish_a * up_b).astype(jnp.bfloat16)
    output = middle + sum_scatter(jnp.dot(swished, down_w, preferred_element_type=jnp.float32))
    block_out = output.astype(jnp.bfloat16)
    d_swished = contract_cols(full_cot, down_w)
    d_a = (d_swished * up_b * silu_grad(up_a)).astype(jnp.bfloat16)
    d_b = (d_swished * swish_a).astype(jnp.bfloat16)
    d_second = sum_scatter(contract_cols(d_a, up_a_w) + contract_cols(d_b, up_b_w))
    scaled = d_second * gain_two
    middle_norm = inv_second * (scaled - unit_second * mean_over(scaled * unit_second, features))
    gain_two_part = jnp.sum(d_second * unit_second, axis=0)
    d_middle = cotangent.astype(jnp.float32) + middle_norm
    unit_own = shard_tokens * inv_first
    d_branch = lax.all_gather(d_middle.astype(jnp.bfloat16), "tp", axis=1, tiled=True)
    d_mixed = contract_cols(d_branch, out_w)
    back = (d_mixed * activated).astype(jnp.bfloat16)
    d_gate = (d_mixed * memory_f * silu_grad(gate_pre)).astype(jnp.bfloat16)
    d_first = sum_scatter(contract_cols(d_gate, gate_w))
    scaled = d_first * gain_one
    input_norm = inv_first * (scaled - unit_own * mean_over(scaled * unit_own, features))
    gain_one_part = jnp.sum(d_first * unit_own, axis=0)
    parts = lax.psum(jnp.stack([gain_one_part, gain_two_part]), ("fsdp", "ctx"))
    gains = lax.all_gather(parts, "tp", axis=1, tiled=True)
    grad_gain_first, grad_gain_second = gains[0], gains[1]
    sums = (
        grad_scatter(contract_rows(first, d_gate), 0),
        grad_scatter(contract_rows(mixed, d_branch), 1),
        grad_scatter(contract_rows(second, d_a), 0),
        grad_scatter(contract_rows(second, d_b), 0),
        grad_scatter(contract_rows(swished, full_cot), 1),
    )
    return block_out, d_middle, input_norm, back, grad_gain_first, grad_gain_second, sums


def middle_on_line(
    tokens, memory, dealing, cotangent, gain_first, gain_second, memory_gate, memory_out, hidden_gate, hidden_up, hidden_down
):
    width = tokens.shape[1]
    features = 4 * width
    (
        _, full_cot, second, first, gate_pre, mixed, swished, d_a, d_b, gate_w, out_w, down, middle, d_middle, d_branch, memory_tokens,
        unit_own, inv_first, gain_two_part, rank, ids,
    ) = front_call(
        tokens, cotangent, memory, memory_gate, memory_out, hidden_gate, hidden_up, hidden_down, gain_first[None], gain_second[None],
        dealing[None],
    )
    scaled, down_sum, grad_memory, _, _, grad_down, grad_up_a, grad_up_b, grad_out, grad_gate, gains, stats = back_call(
        d_branch, full_cot, swished, second, d_a, d_b, mixed, first, gate_pre, memory_tokens, out_w, gate_w, unit_own, gain_first[None],
        gain_two_part, rank, ids, down,
    )
    block_out = (middle + down_sum).astype(jnp.bfloat16)
    grad_inputs = d_middle + inv_first[0][:, None] * (scaled - unit_own * (stats[0][:, None] / features))
    grad_memory = grad_memory.astype(jnp.float32)
    return (
        block_out, grad_inputs, grad_memory, gains[:, 0].reshape(features), gains[:, 1].reshape(features), grad_gate, grad_out.T,
        grad_up_a, grad_up_b, grad_down.T,
    )


def shards(
    tokens,
    memory,
    dealing,
    cotangent,
    gain_first,
    gain_second,
    memory_gate,
    memory_out,
    hidden_gate,
    hidden_up,
    hidden_down,
):
    if lax.axis_size("fsdp") == 2 and lax.axis_size("ctx") == 4 and lax.axis_size("tp") == 4:
        return middle_on_line(
            tokens, memory, dealing, cotangent, gain_first, gain_second, memory_gate, memory_out, hidden_gate, hidden_up, hidden_down
        )
    groups = lax.axis_size(("fsdp", "ctx"))
    group_index = lax.axis_index(("fsdp", "ctx"))
    rows = dealing.shape[0]
    block = rows // groups
    order = jnp.argsort(dealing)
    sent_rows = memory[order].reshape(groups, block, memory.shape[1])
    arrived = lax.all_to_all(sent_rows, ("fsdp", "ctx"), split_axis=0, concat_axis=0, tiled=True)
    arrived_ids = lax.all_to_all(
        dealing[order].reshape(groups, block),
        ("fsdp", "ctx"),
        split_axis=0,
        concat_axis=0,
        tiled=True,
    )
    places = arrived_ids.reshape(rows) - group_index * rows
    memory_tokens = arrived.reshape(rows, memory.shape[1])[jnp.argsort(places)]
    block_out, d_middle, input_norm, back, grad_gain_first, grad_gain_second, sums = middle_of(
        tokens, memory_tokens, cotangent, gain_first, gain_second, memory_gate, memory_out, hidden_gate, hidden_up, hidden_down
    )
    grad_inputs = d_middle + input_norm
    back_rows = back[places].reshape(groups, block, memory.shape[1])
    returned = lax.all_to_all(back_rows, ("fsdp", "ctx"), split_axis=0, concat_axis=0, tiled=True)
    grad_memory = returned.reshape(rows, memory.shape[1])[jnp.argsort(order)].astype(jnp.float32)
    return (
        block_out,
        grad_inputs,
        grad_memory,
        grad_gain_first,
        grad_gain_second,
        sums[0],
        sums[1],
        sums[2],
        sums[3],
        sums[4],
    )


def solution(mesh):
    in_specs = (
        P(("fsdp", "ctx"), "tp"),
        P(("fsdp", "ctx"), "tp"),
        P(("fsdp", "ctx")),
        P(("fsdp", "ctx"), "tp"),
        P(),
        P(),
        P(("fsdp", "ctx"), "tp"),
        P("tp", ("fsdp", "ctx")),
        P(("fsdp", "ctx"), "tp"),
        P(("fsdp", "ctx"), "tp"),
        P("tp", ("fsdp", "ctx")),
    )
    out_specs = (
        P(("fsdp", "ctx"), "tp"),
        P(("fsdp", "ctx"), "tp"),
        P(("fsdp", "ctx"), "tp"),
        P(),
        P(),
        P(("fsdp", "ctx"), "tp"),
        P("tp", ("fsdp", "ctx")),
        P(("fsdp", "ctx"), "tp"),
        P(("fsdp", "ctx"), "tp"),
        P("tp", ("fsdp", "ctx")),
    )
    return jax.shard_map(shards, mesh=mesh, in_specs=in_specs, out_specs=out_specs, check_vma=False)
```

```python
import functools

import jax
import jax.numpy as jnp
from jax import lax
from jax.experimental import pallas as pl
from jax.experimental.pallas import tpu as pltpu
from jax.sharding import PartitionSpec as P

EPS = 1e-06
VMEM_LIMIT = 63 * 2**20 + 2**19


MESH = pl.DeviceIdType.MESH
JOBS = 8


def dot_nt(left, right):
    return lax.dot_general(left, right, (((1,), (1,)), ((), ())), preferred_element_type=jnp.float32)


def dot_tn(left, right):
    return lax.dot_general(left, right, (((0,), (0,)), ((), ())), preferred_element_type=jnp.float32)


class Place:
    def __init__(self):
        self.f, self.c, self.t = lax.axis_index("fsdp"), lax.axis_index("ctx"), lax.axis_index("tp")
        self.y, self.k = self.c // 2, self.c % 2

    def at(self, flip_f, flip_y, flip_k):
        f = self.f + flip_f * (1 - 2 * self.f)
        y = self.y + flip_y * (1 - 2 * self.y)
        k = self.k + flip_k * (1 - 2 * self.k)
        return f, y * 2 + k

    def sibling(self):
        return (*self.at(0, 0, 1), self.t)

    def first(self):
        return (*self.at(1 - self.k, self.k, 0), self.t)

    def second(self):
        return (*self.at(self.k, 1 - self.k, 0), self.t)

    def along(self, t):
        return (self.f, self.c, t)

    def owner(self, slot, flip_k):
        alpha, beta = 1 - slot // 2, 1 - slot % 2
        parity = self.k + flip_k * (1 - 2 * self.k)
        f, c = self.at(alpha * (1 - parity) + beta * parity, beta * (1 - parity) + alpha * parity, flip_k)
        return f * 4 + c


def remote(source, target, send, recv, device):
    return pltpu.make_async_remote_copy(
        src_ref=source, dst_ref=target, send_sem=send, recv_sem=recv, device_id=device, device_id_type=MESH
    )


OTHERS = ((1, 1, 1), (1, 1, 0), (0, 1, 1), (1, 0, 1), (0, 1, 0), (1, 0, 0), (0, 0, 1))


def greet(place):
    barrier = pltpu.get_barrier_semaphore()
    for flips in OTHERS:
        pl.semaphore_signal(barrier, inc=1, device_id=(*place.at(*flips), place.t), device_id_type=MESH)
    for step in range(1, 4):
        pl.semaphore_signal(barrier, inc=1, device_id=place.along((place.t + step) % 4), device_id_type=MESH)
    pl.semaphore_wait(barrier, 10)


class Exchange:
    def __init__(self, place, source, target, send, recv):
        self.place, self.source, self.target, self.send, self.recv = place, source, target, send, recv
        self.me = place.f * 4 + place.c

    def copy(self, index):
        f, c = self.place.at(*OTHERS[index])
        group = f * 4 + c
        out = remote(self.source(group), self.target(self.me), self.send.at[index], self.recv.at[self.me], (f, c, self.place.t))
        back = remote(self.source(group), self.target(group), self.send.at[index], self.recv.at[group], (f, c, self.place.t))
        return out, back

    def stay(self):
        return pltpu.make_async_copy(self.source(self.me), self.target(self.me), self.send.at[7])

    def start(self):
        for index in range(7):
            self.copy(index)[0].start()
        self.stay().start()

    def arrived(self):
        for index in range(7):
            self.copy(index)[1].wait_recv()
        self.stay().wait()

    def finish(self):
        for index in range(7):
            self.copy(index)[0].wait_send()


def chosen(row, first, count):
    places = lax.broadcasted_iota(jnp.int32, (count, row.shape[1]), 0) + first
    return jnp.where(row == places, 1.0, 0.0).astype(jnp.bfloat16)


class Gather:
    def __init__(self, place, full, send, recv, rows, width, own=None):
        self.place, self.full, self.send, self.recv, self.rows, self.width, self.mine = place, full, send, recv, rows, width, own

    def copy(self, chunk, shard, way, hop):
        view = self.full.at[pl.ds(chunk * self.rows, self.rows), pl.ds(pl.multiple_of(shard * self.width, self.width), self.width)]
        device = self.place.along(self.place.t + 1 - 2 * way)
        source = view if hop > 0 or self.mine is None else self.mine.at[pl.ds(chunk * self.rows, self.rows)]
        return remote(source, view, self.send.at[chunk, way, hop], self.recv.at[chunk, shard], device)

    def step(self, chunk, hop):
        t = self.place.t

        @pl.when(t - hop >= 0)
        def _():
            if hop > 0:
                self.copy(chunk, t - hop, 0, hop).wait_recv()
            if hop < 3:
                @pl.when(t < 3)
                def _():
                    self.copy(chunk, t - hop, 0, hop).start()

        @pl.when(t + hop <= 3)
        def _():
            if hop > 0:
                self.copy(chunk, t + hop, 1, hop).wait_recv()
            if hop < 3:
                @pl.when(t > 0)
                def _():
                    self.copy(chunk, t + hop, 1, hop).start()

    def finish(self, chunk):
        t = self.place.t
        for hop in range(3):
            @pl.when((t - hop >= 0) & (t < 3))
            def _():
                self.copy(chunk, t - hop, 0, hop).wait_send()

            @pl.when((t + hop <= 3) & (t > 0))
            def _():
                self.copy(chunk, t + hop, 1, hop).wait_send()


class Scatter:
    def __init__(self, place, slots, send, recv):
        self.place, self.slots, self.send, self.recv = place, slots, send, recv
        self.ring = slots.shape[0]

    def block(self, step):
        t = self.place.t
        low, high = t % 2, t // 2
        return (3 * (1 - high), 2 - 2 * low + high, 1 + low, t)[step]

    def copy(self, chunk, step):
        t, block, ring = self.place.t, self.block(step), chunk % self.ring
        up = (block > t).astype(jnp.int32)
        last_down = (block == t - 1).astype(jnp.int32)
        slot = block + last_down * (4 - block)
        device = self.place.along(t - 1 + 2 * up)
        return remote(self.slots.at[ring, block], self.slots.at[ring, slot], self.send.at[chunk, step], self.recv.at[chunk, slot], device)

    def arrived(self, chunk, slot):
        view = self.slots.at[chunk % self.ring, slot]
        remote(view, view, self.send.at[chunk, 0], self.recv.at[chunk, slot], self.place.along(self.place.t)).wait_recv()

    def step(self, chunk, step, part, inside):
        block, ring = self.block(step), chunk % self.ring
        value = part(block)
        if inside:
            self.arrived(chunk, block)
            value += self.slots[ring, block].astype(jnp.float32)
        self.slots[ring, block] = value.astype(jnp.bfloat16)
        self.copy(chunk, step).start()

    def own(self, chunk, held):
        t, ring = self.place.t, chunk % self.ring

        @pl.when(t > 0)
        def _():
            self.arrived(chunk, t)
            held[...] += self.slots[ring, t].astype(jnp.float32)

        @pl.when(t < 3)
        def _():
            self.arrived(chunk, 4)
            held[...] += self.slots[ring, 4].astype(jnp.float32)

    def finish(self, chunk):
        for step in range(3):
            self.copy(chunk, step).wait_send()


def by_place(place, ends, inside):
    is_end = (place.t == 0) | (place.t == 3)
    pl.when(is_end)(ends)
    pl.when(jnp.logical_not(is_end))(inside)


def to_row(column):
    return jnp.broadcast_to(column, (column.shape[0], 128)).T[:8]


def back_kernel(
    branch_own, cot_in, swi_in, h2_in, da_in, db_in, mixed_in, h1_in, gate_in, mem_in, out_w_in, gate_w_in, xhat_in, gain_ref, gg2_ref, rank_ref, ids_ref, down_in,
    dh1_out, down_out, memory_out, term_out, returned, hd_out, hg_out, hu_out, mo_out, mg_out, gains_out, stats_out,
    A1, A2, B1, B2, MX, DB, DG, WO, WG, SR, SS, H1S, H1R, H2S, H2R, OS, RZ, GP, MT, XH, HO, GV, GR, GA, SV, SA, PLACES, ZN, NS, NO,
    load_sem, gate_sem, ag_send, ag_recv, rs_send, rs_recv, sib_send, sib_recv, h1_send, h1_recv, h2_send, h2_recv,
    out_sem, small_send, small_recv, x_send, x_recv, n_send, n_recv, n_load, n_free, sib_free, first_free, second_free,
):
    place = Place()
    t = place.t
    chunk_rows, width = XH.shape
    slab = OS.shape[0]
    span = OS.shape[1]
    cols = span // 2
    chunks = 4

    loads = {}

    def load(name, source, target, slot):
        loads[name] = pltpu.make_async_copy(source, target, load_sem.at[slot])
        loads[name].start()

    def need(*names):
        for name in names:
            if name in loads:
                loads.pop(name).wait()

    own_columns = pl.ds(pl.multiple_of(t * width, width), width)
    load("branch", branch_own, DB.at[:, own_columns], 0)
    load("cot", cot_in, A1, 1)
    load("swi", swi_in.at[:, 0:span], B1.at[:, 0:span], 2)
    greet(place)

    gather = Gather(place, DB, ag_send, ag_recv, chunk_rows, width)
    scatter = Scatter(place, RZ, rs_send, rs_recv)
    need("branch")

    jobs = [
        (A1, B1, 0, hd_out, 0), (A1, B1, span, hd_out, span), (A2, B2, 0, hg_out, 0), (A2, B2, span, hg_out, span),
        (A2, B1, 0, hu_out, 0), (A2, B1, span, hu_out, span), (DB, MX, 0, mo_out, 0), (A1, DG, 0, mg_out, 0),
    ]

    def tile(job, group, half):
        left, right, offset = jobs[job][:3]
        columns = pl.ds(pl.multiple_of(offset + half * cols, cols), cols)
        return dot_tn(left[:, pl.ds(pl.multiple_of(group * slab, slab), slab)], right[:, columns])

    def each_half(body):
        @pl.loop(0, 2)
        def _(half):
            body(half, pl.ds(pl.multiple_of(half * cols, cols), cols))

    def sib_copy(job, slot):
        return remote(SS.at[slot], SR.at[job % 3, slot], sib_send.at[slot], sib_recv.at[job, slot], place.sibling())

    def h1_copy(job, slot):
        return remote(H1S.at[job % 2, slot], H1R.at[job % 3, slot], h1_send.at[job % 2, slot], h1_recv.at[job, slot], place.first())

    def h2_copy(job):
        return remote(H2S.at[job % 2], H2R.at[job % 2], h2_send.at[job % 2], h2_recv.at[job], place.second())

    def to_sibling(job):
        if job >= 3:
            pl.semaphore_wait(sib_free, 1)

        @pl.loop(0, 4)
        def _(slot):
            if job >= 1:
                sib_copy(job - 1, slot).wait_send()
            group = place.owner(slot, 1)

            def body(half, at):
                SS[slot, :, at] = tile(job, group, half).astype(jnp.bfloat16)

            each_half(body)
            sib_copy(job, slot).start()

    def to_first(job):
        if job >= 3:
            pl.semaphore_wait(first_free, 1)

        @pl.loop(0, 2)
        def _(slot):
            if job >= 2:
                h1_copy(job - 2, slot).wait_send()
            group = place.owner(slot, 0)
            sib_copy(job, slot).wait_recv()

            def body(half, at):
                H1S[job % 2, slot, :, at] = (tile(job, group, half) + SR[job % 3, slot, :, at].astype(jnp.float32)).astype(jnp.bfloat16)

            each_half(body)
            h1_copy(job, slot).start()

    def to_second(job):
        if job >= 2:
            pl.semaphore_wait(second_free, 1)
            h2_copy(job - 2).wait_send()
        group = place.owner(2, 0)
        sib_copy(job, 2).wait_recv()
        h1_copy(job, 0).wait_recv()

        def body(half, at):
            H2S[job % 2, :, at] = (
                tile(job, group, half) + SR[job % 3, 2, :, at].astype(jnp.float32) + H1R[job % 3, 0, :, at].astype(jnp.float32)
            ).astype(jnp.bfloat16)

        each_half(body)
        h2_copy(job).start()

    def out_copy(job):
        return pltpu.make_async_copy(OS, jobs[job][3].at[:, pl.ds(jobs[job][4], span)], out_sem)

    def to_output(job):
        group = place.owner(3, 0)
        sib_copy(job, 3).wait_recv()
        h1_copy(job, 1).wait_recv()
        h2_copy(job).wait_recv()
        if job >= 1:
            out_copy(job - 1).wait()

        def body(half, at):
            OS[:, at] = (
                tile(job, group, half) + SR[job % 3, 3, :, at].astype(jnp.float32)
                + H1R[job % 3, 1, :, at].astype(jnp.float32) + H2R[job % 2, :, at].astype(jnp.float32)
            )

        each_half(body)
        out_copy(job).start()
        for ahead, free, device in ((3, sib_free, place.sibling()), (3, first_free, place.first()), (2, second_free, place.second())):
            if job + ahead < JOBS:
                pl.semaphore_signal(free, inc=1, device_id=device, device_id_type=MESH)

    def gate_load(chunk):
        return pltpu.make_async_copy(gate_in.at[pl.ds(chunk * chunk_rows, chunk_rows)], GP, gate_sem.at[0])

    def mem_load(chunk):
        return pltpu.make_async_copy(mem_in.at[pl.ds(chunk * chunk_rows, chunk_rows)], MT, gate_sem.at[1])

    def term_store(chunk):
        return pltpu.make_async_copy(MT, term_out.at[pl.ds(chunk * chunk_rows, chunk_rows)], gate_sem.at[2])

    def channels(chunk):
        rows = pl.ds(chunk * chunk_rows, chunk_rows)
        if chunk > 0:
            term_store(chunk - 1).wait()
        mem_load(chunk).start()
        gate_load(chunk).wait()
        mem_load(chunk).wait()

        def body(half, at):
            d_mixed = dot_nt(DB[rows, :], WO[at, :])
            pre = GP[:, at]
            sigma = jax.nn.sigmoid(pre)
            DG[rows, at] = (d_mixed * MT[:, at].astype(jnp.float32) * (sigma * (1.0 + pre * (1.0 - sigma)))).astype(jnp.bfloat16)
            MT[:, at] = (d_mixed * (pre * sigma)).astype(jnp.bfloat16)

        each_half(body)
        term_store(chunk).start()
        if chunk + 1 < chunks:
            gate_load(chunk + 1).start()

    def first_part(chunk, block):
        return dot_nt(DG[pl.ds(chunk * chunk_rows, chunk_rows), :], WG[pl.ds(pl.multiple_of(block * width, width), width), :])

    def first_step(chunk, step, inside):
        scatter.step(chunk, step, lambda block: first_part(chunk, block), inside)

    def own_copies(chunk):
        rows = pl.ds(chunk * chunk_rows, chunk_rows)
        return (
            pltpu.make_async_copy(xhat_in.at[rows], XH, gate_sem.at[3]),
            pltpu.make_async_copy(HO, dh1_out.at[rows], gate_sem.at[4]),
        )

    def own_step(chunk):
        load_xhat, store = own_copies(chunk)
        load_xhat.start()
        if chunk > 0:
            own_copies(chunk - 1)[1].wait()
        HO[...] = first_part(chunk, t)
        scatter.own(chunk, HO)
        load_xhat.wait()
        d_first, unit = HO[...], XH[...]
        product = jnp.sum(d_first * unit, axis=0, keepdims=True)
        if chunk == 0:
            GV[0, 0:1] = product
        else:
            GV[0, 0:1] += product
        scaled = d_first * gain_ref[:, own_columns]
        HO[...] = scaled
        SV[:, pl.ds(chunk * chunk_rows, chunk_rows)] = to_row(jnp.sum(scaled * unit, axis=1, keepdims=True))
        store.start()

    def sum_copy(step):
        device = (place.sibling(), place.first(), place.second())[step]
        return remote(GV.at[step], GR.at[step], small_send.at[step], small_recv.at[step], device)

    def to_line(step, what):
        device = place.along((t + step) % 4)
        if what == 0:
            return remote(SV, SA.at[t], small_send.at[2 + step], small_recv.at[2 + step], device)
        return remote(GV.at[3], GA.at[t], small_send.at[5 + step], small_recv.at[5 + step], device)

    down_scatter = Scatter(place, ZN, n_send, n_recv)

    def down_part(chunk, block, target, sem):
        source = down_in.at[pl.ds(chunk * chunk_rows, chunk_rows), pl.ds(pl.multiple_of(block * width, width), width)]
        return pltpu.make_async_copy(source, target, sem)

    def down_store(chunk):
        return pltpu.make_async_copy(NO, down_out.at[pl.ds(chunk * chunk_rows, chunk_rows)], n_load.at[2])

    def down_own(chunk):
        if chunk > 0:
            down_store(chunk - 1).wait()
        load = down_part(chunk, t, NO, n_load.at[3])
        load.start()
        load.wait()
        down_scatter.own(chunk, NO)
        down_store(chunk).start()
        down_scatter.finish(chunk)
        if chunk < 2:
            for step in (-1, 1):
                @pl.when((t + step >= 0) & (t + step <= 3))
                def _():
                    pl.semaphore_signal(
                        n_free.at[(1 - step) // 2], inc=1, device_id=place.along(t + step), device_id_type=MESH
                    )

    is_end = (t == 0) | (t == 3)
    down_order = {inside: [event[1:3] for event in BACK_ORDER if event[0] == "Ns" and event[3] == inside] for inside in (False, True)}

    def only(inside, body):
        pl.when(jnp.logical_not(is_end) if inside else is_end)(body)

    def down_load(inside, index):
        chunk, step = down_order[inside][index]
        return down_part(chunk, down_scatter.block(step), NS.at[index % 2], n_load.at[index % 2])

    def down_step(chunk, step, inside):
        index = down_order[inside].index((chunk, step))
        first_of_chunk = all(other != chunk for other, _ in down_order[inside][:index])

        def body():
            if index == 0:
                down_load(inside, 0).start()
            if index + 1 < 12:
                down_load(inside, index + 1).start()
            if chunk >= 2 and first_of_chunk:
                for side, near in enumerate((t > 0, t < 3)):
                    pl.when(near)(functools.partial(pl.semaphore_wait, n_free.at[side], 1))
            down_load(inside, index).wait()
            down_scatter.step(chunk, step, lambda block: NS[index % 2], inside)

        only(inside, body)

    channel_count = span
    block = DB.shape[0] // 8
    exchange = Exchange(
        place,
        lambda group: B2.at[pl.ds(pl.multiple_of(group * block, block), block), pl.ds(channel_count, channel_count)],
        lambda group: returned.at[pl.ds(pl.multiple_of(group * block, block), block)],
        x_send, x_recv,
    )

    def send_terms():
        term_store(3).wait()
        load("terms", term_out, B2.at[:, pl.ds(0, channel_count)], 4)
        need("terms")
        PLACES[...] = ids_ref[...] - (place.f * 4 + place.c) * DB.shape[0]

        @pl.loop(0, chunks)
        def _(part):
            rows = pl.ds(pl.multiple_of(part * chunk_rows, chunk_rows), chunk_rows)
            total = jnp.zeros((chunk_rows, channel_count), jnp.float32)
            for chunk in range(chunks):
                picked = chosen(PLACES[0:1, rows], chunk * chunk_rows, chunk_rows)
                total += dot_tn(picked, B2[chunk * chunk_rows:(chunk + 1) * chunk_rows, 0:channel_count])
            B2[rows, channel_count:2 * channel_count] = total.astype(jnp.bfloat16)

        exchange.start()

    def memory_grads():
        exchange.arrived()
        copy = pltpu.make_async_copy(returned, A2.at[:, pl.ds(0, channel_count)], load_sem.at[0])
        copy.start()
        copy.wait()

        @pl.loop(0, chunks)
        def _(part):
            rows = pl.ds(pl.multiple_of(part * chunk_rows, chunk_rows), chunk_rows)
            total = jnp.zeros((chunk_rows, channel_count), jnp.float32)
            for chunk in range(chunks):
                picked = chosen(rank_ref[0:1, rows], chunk * chunk_rows, chunk_rows)
                total += dot_tn(picked, A2[chunk * chunk_rows:(chunk + 1) * chunk_rows, 0:channel_count])
            MT[...] = total.astype(jnp.bfloat16)
            store = pltpu.make_async_copy(MT, memory_out.at[rows], gate_sem.at[0])
            store.start()
            store.wait()

    gate_load(0).start()

    def gains(number):
        if number == 0:
            for step in range(1, 4):
                to_line(step, 0).start()
            GV[0, 1:2] = gg2_ref[...]
            sum_copy(0).start()
            return
        sum_copy(number - 1).wait_recv()
        GV[number] = GV[number - 1] + GR[number - 1]
        if number < 3:
            sum_copy(number).start()
        else:
            for ahead in range(1, 4):
                to_line(ahead, 1).start()

    actions = {
        "D": gather.step, "S1": to_sibling, "S2": to_first, "S3": to_second, "S4": to_output, "Bc": channels, "Bo": own_step,
        "Bs": lambda chunk, step, inside: only(inside, lambda: first_step(chunk, step, inside)), "Ns": down_step, "No": down_own,
        "terms": send_terms, "mgrads": memory_grads, "G": gains,
    }
    wanted = {
        ("S1", 0): ("cot", "swi"), ("S1", 1): ("swi_rest",), ("S1", 2): ("h2", "da"), ("S1", 4): ("db",), ("S1", 6): ("mixed",), ("S1", 7): ("h1",),
        ("Bc", 0): ("out_w", "gate_w"),
    }
    GV[0] = jnp.zeros_like(GV[0])
    for event in BACK_ORDER:
        need(*wanted.get(event, ()))
        actions[event[0]](*event[1:])
        if event == ("S1", 0):
            load("swi_rest", swi_in.at[:, span:2 * span], B1.at[:, span:2 * span], 8)
        if event == ("S2", 0):
            load("h2", h2_in, A2, 3)
            load("da", da_in, B2, 4)
            load("out_w", out_w_in, WO, 5)
            load("gate_w", gate_w_in, WG, 6)
            load("mixed", mixed_in, MX, 7)
        if event == ("S4", 1):
            load("db", db_in, B1, 2)
            load("h1", h1_in, A1, 1)

    for step in range(1, 4):
        to_line(step, 0).wait()
        to_line(step, 1).wait()
    SA[t] = SV[...]
    GA[t] = GV[3]
    stats_out[...] = SA[0] + SA[1] + SA[2] + SA[3]
    gains_out[...] = GA[...]
    for chunk in range(4):
        gather.finish(chunk)
        scatter.finish(chunk)
    for step in range(3):
        sum_copy(step).wait_send()
    for slot in range(4):
        sib_copy(JOBS - 1, slot).wait_send()
    for job in (JOBS - 2, JOBS - 1):
        for slot in range(2):
            h1_copy(job, slot).wait_send()
        h2_copy(job).wait_send()
    exchange.finish()
    down_store(3).wait()
    own_copies(3)[1].wait()
    out_copy(JOBS - 1).wait()


def back_call(branch_own, cot, swi, h2, da, db, mixed, h1, gate, mem, out_w, gate_w, xhat, gain, gg2, rank, ids, down):
    rows, features = cot.shape
    channels, hidden = mixed.shape[1], swi.shape[1]
    width, slab, part = features // 4, features // 8, rows // 4
    bf, f32 = jnp.bfloat16, jnp.float32
    shape = jax.ShapeDtypeStruct
    anywhere, vmem = pl.BlockSpec(memory_space=pl.ANY), pl.BlockSpec(memory_space=pltpu.VMEM)
    dma = pltpu.SemaphoreType.DMA
    regular = pltpu.SemaphoreType.REGULAR
    V = pltpu.VMEM
    macs = rows * features * (3 * hidden + 4 * channels)
    return pl.pallas_call(
        back_kernel,
        name="backward",
        out_shape=(
            shape((rows, width), f32), shape((rows, width), f32), shape((rows, channels), bf), shape((rows, channels), bf), shape((rows, channels), bf),
            shape((slab, hidden), f32), shape((slab, hidden), f32),
            shape((slab, hidden), f32), shape((slab, channels), f32), shape((slab, channels), f32), shape((4, 8, width), f32),
            shape((8, rows), f32),
        ),
        in_specs=[anywhere] * 13 + [vmem] * 4 + [anywhere],
        out_specs=(anywhere,) * 10 + (vmem,) * 2,
        scratch_shapes=[
            V((rows, features), bf), V((rows, features), bf), V((rows, hidden), bf), V((rows, hidden), bf), V((rows, channels), bf),
            V((rows, features), bf), V((rows, channels), bf), V((channels, features), bf), V((features, channels), bf),
            V((3, 4, slab, channels), bf), V((4, slab, channels), bf), V((2, 2, slab, channels), bf), V((3, 2, slab, channels), bf),
            V((2, slab, channels), bf), V((2, slab, channels), bf), V((slab, channels), f32), V((4, 5, part, width), bf),
            V((part, channels), f32), V((part, channels), bf), V((part, width), f32), V((part, width), f32),
            V((4, 8, width), f32), V((3, 8, width), f32), V((4, 8, width), f32), V((8, rows), f32), V((4, 8, rows), f32),
            V((8, rows), jnp.int32), V((2, 5, part, width), bf), V((2, part, width), f32), V((part, width), f32), dma((9,)), dma((5,)), dma((4, 2, 3)), dma((4, 4)), dma((4, 3)), dma((4, 5)), dma((4,)), dma((JOBS, 4)), dma((2, 2)),
            dma((JOBS, 2)), dma((2,)), dma((JOBS,)), dma, dma((9,)), dma((9,)), dma((8,)), dma((8,)), dma((4, 3)), dma((4, 5)), dma((4,)), pltpu.SemaphoreType.REGULAR((2,)), regular, regular, regular,
        ],
        compiler_params=pltpu.CompilerParams(collective_id=1, has_side_effects=True, vmem_limit_bytes=VMEM_LIMIT),
        cost_estimate=pl.CostEstimate(flops=2 * macs, bytes_accessed=64 * 2**20, transcendentals=rows * channels),
    )(branch_own, cot, swi, h2, da, db, mixed, h1, gate, mem, out_w, gate_w, xhat, gain, gg2, rank, ids, down)


FRONT_ORDER = (
    ("T", 0, 0), ("W", 0, 0), ("T", 1, 0), ("T", 2, 0), ("T", 3, 0), ("W", 1, 0), ("C", 1, 0), ("rows",), ("W", 0, 1),
    ("T", 1, 1), ("W", 1, 1), ("W", 4, 0), ("T", 0, 1), ("C", 2, 0), ("T", 1, 2), ("T", 0, 2), ("C", 0, 0), ("take",),
    ("W", 2, 0), ("T", 2, 1), ("W", 1, 2), ("W", 3, 0), ("C", 2, 1), ("C", 3, 0), ("T", 3, 1), ("T", 0, 3), ("T", 1, 3),
    ("W", 0, 2), ("W", 0, 3), ("W", 1, 3), ("F1", 0), ("Rs", 0, 1, False), ("Rs", 0, 0, False), ("Rs", 0, 2, False),
    ("C", 3, 1), ("F1", 1), ("Rs", 1, 0, False), ("Rs", 0, 0, True), ("C", 1, 1), ("T", 2, 2), ("Rs", 1, 0, True),
    ("T", 3, 2), ("Rs", 1, 1, False), ("Rs", 0, 2, True), ("W", 4, 1), ("Rs", 1, 2, False), ("T", 3, 3),
    ("Rs", 1, 2, True), ("Rs", 0, 1, True), ("Rs", 1, 1, True), ("Ro", 0), ("H", 0, 0), ("C", 0, 1), ("W", 2, 1),
    ("H", 0, 1), ("T", 2, 3), ("F1", 2), ("Rs", 2, 0, False), ("C", 0, 2), ("Rs", 2, 1, False), ("C", 1, 2),
    ("Rs", 2, 2, False), ("Rs", 2, 0, True), ("Ro", 1), ("H", 1, 0), ("W", 3, 1), ("W", 4, 2), ("F1", 3),
    ("Rs", 2, 1, True), ("W", 2, 2), ("Rs", 2, 2, True), ("H", 1, 1), ("Rs", 3, 0, False), ("Rs", 3, 1, False),
    ("W", 3, 2), ("Rs", 3, 0, True), ("H", 0, 2), ("C", 1, 3), ("W", 2, 3), ("H", 1, 2), ("W", 4, 3), ("Ro", 2),
    ("Rs", 3, 1, True), ("Rs", 3, 2, True), ("H", 2, 0), ("C", 0, 3), ("Rs", 3, 2, False), ("H", 0, 3), ("W", 3, 3),
    ("F2", 0), ("Es", 0, 0, False), ("Es", 0, 1, False), ("H", 2, 1), ("Ro", 3), ("C", 2, 2), ("H", 3, 0), ("H", 1, 3),
    ("F2", 1), ("Es", 1, 0, False), ("Es", 1, 1, False), ("Es", 0, 2, True), ("Es", 0, 2, False), ("H", 2, 2),
    ("Es", 1, 2, False), ("Es", 0, 0, True), ("C", 3, 2), ("H", 3, 1), ("C", 2, 3), ("H", 2, 3), ("F2", 2),
    ("Es", 2, 1, False), ("Es", 2, 0, False), ("Es", 0, 1, True), ("Es", 1, 2, True), ("H", 3, 2), ("Es", 2, 2, False),
    ("NP", 0), ("Es", 1, 0, True), ("Eo", 0), ("H", 3, 3), ("C", 3, 3), ("F2", 3), ("close", 0), ("Es", 3, 0, False),
    ("Es", 2, 0, True), ("Es", 2, 2, True), ("Es", 3, 1, False), ("Es", 1, 1, True), ("NP", 1), ("NP", 2), ("Eo", 1),
    ("Es", 3, 0, True), ("Es", 2, 1, True), ("Es", 3, 2, True), ("Es", 3, 2, False), ("Es", 3, 1, True), ("close", 1),
    ("Eo", 2), ("NP", 3), ("close", 2), ("Eo", 3), ("close", 3),
)
BACK_ORDER = (
    ("D", 0, 0), ("S1", 0), ("D", 1, 0), ("S2", 0), ("Ns", 0, 1, False), ("D", 2, 0), ("Ns", 1, 0, False), ("S1", 1),
    ("D", 3, 0), ("S2", 1), ("S1", 2), ("Ns", 1, 1, False), ("D", 0, 1), ("S3", 0), ("S2", 2), ("D", 0, 2), ("D", 2, 1),
    ("Ns", 0, 0, False), ("D", 0, 3), ("Ns", 0, 2, False), ("Bc", 0), ("S3", 1), ("D", 1, 1), ("S4", 0), ("S1", 3),
    ("S2", 3), ("Ns", 1, 2, False), ("D", 1, 2), ("D", 1, 3), ("D", 2, 2), ("Ns", 0, 0, True), ("Bs", 0, 1, False),
    ("S3", 2), ("Bc", 1), ("D", 3, 1), ("Bs", 1, 0, False), ("S4", 1), ("Bs", 0, 0, False), ("Ns", 1, 0, True),
    ("S1", 4), ("D", 3, 2), ("D", 2, 3), ("S2", 4), ("Bc", 2), ("D", 3, 3), ("S4", 2), ("Bs", 1, 1, False),
    ("Bs", 0, 2, True), ("Bs", 2, 0, False), ("Bc", 3), ("Bs", 3, 0, False), ("Ns", 0, 1, True), ("Ns", 0, 2, True),
    ("S3", 3), ("Bs", 1, 2, False), ("Ns", 1, 1, True), ("Bs", 0, 0, True), ("S3", 4), ("S1", 5), ("No", 0),
    ("Bs", 1, 0, True), ("S2", 5), ("S4", 3), ("S1", 6), ("Bs", 3, 1, False), ("Bs", 2, 1, False), ("Bs", 1, 1, True),
    ("S4", 4), ("Bs", 2, 0, True), ("Ns", 2, 0, False), ("Ns", 1, 2, True), ("Ns", 2, 1, False), ("Bs", 0, 2, False),
    ("S3", 5), ("Bs", 3, 2, False), ("Bs", 3, 0, True), ("terms",), ("S2", 6), ("Bs", 1, 2, True), ("No", 1),
    ("Ns", 3, 0, False), ("Bs", 2, 1, True), ("Bs", 2, 2, False), ("S4", 5), ("Bs", 3, 1, True), ("S1", 7),
    ("Ns", 2, 0, True), ("Ns", 3, 1, False), ("Ns", 2, 2, False), ("Bs", 3, 2, True), ("S2", 7), ("Bs", 0, 1, True),
    ("Bo", 0), ("Ns", 2, 1, True), ("Bs", 2, 2, True), ("Ns", 2, 2, True), ("mgrads",), ("Ns", 3, 2, False),
    ("Ns", 3, 0, True), ("S3", 6), ("Bo", 1), ("Bo", 2), ("Bo", 3), ("G", 0), ("Ns", 3, 2, True), ("Ns", 3, 1, True),
    ("S3", 7), ("G", 1), ("G", 2), ("No", 2), ("G", 3), ("No", 3), ("S4", 6), ("S4", 7),
)


class Spread:
    def __init__(self, place, index, shard, view, send, recv, local):
        self.place, self.index, self.shard, self.view, self.send, self.recv = place, index, shard, view, send, recv
        self.local = local

    def group(self, *flips):
        f, c = self.place.at(*flips)
        return f * 4 + c

    def copy(self, group, device, slot):
        view = self.view(group)
        source = self.shard if slot < 3 else view
        return remote(source, view, self.send.at[self.index, slot], self.recv.at[self.index, group], device)

    def routes(self):
        place = self.place
        me, both = self.group(0, 0, 0), self.group(1, 1, 0)
        first, second = self.group(1 - place.k, place.k, 0), self.group(place.k, 1 - place.k, 0)
        return (
            (me, place.first()), (me, place.second()), (me, place.sibling()), (second, place.first()), (first, place.sibling()),
            (second, place.sibling()), (both, place.sibling()),
        )

    def start(self, slot):
        group, device = self.routes()[slot]
        self.copy(group, device, slot).start()

    def arrived(self, group):
        self.copy(group, self.place.sibling(), 3).wait_recv()

    def stay(self):
        return pltpu.make_async_copy(self.shard, self.view(self.group(0, 0, 0)), self.local.at[self.index])

    def phase(self, number):
        routes = self.routes()
        if number == 0:
            for slot in range(3):
                self.start(slot)
            self.stay().start()
        if number == 1:
            self.arrived(routes[3][0])
            self.start(3)
            self.start(5)
            self.arrived(routes[4][0])
            self.start(4)
        if number == 2:
            self.arrived(routes[6][0])
            self.start(6)
        if number == 3:
            for flips in ((0, 0), (0, 1), (1, 0), (1, 1)):
                self.arrived(self.group(*flips, 1))
            self.stay().wait()

    def finish(self):
        for slot, (group, device) in enumerate(self.routes()):
            self.copy(group, device, slot).wait_send()


def to_column(row):
    return jnp.broadcast_to(row, (128, row.shape[1])).T[:, 0:1]


def front_kernel(
    tokens, cotangent, mem_in, gate_w, out_w, up_a_w, up_b_w, down_w, gain1, gain2, deal_row,
    tok_full, cot_full, h2_full, h1_out, gate_out, mixed_out, swi_out, da_out, db_out, gate_w_out, out_w_out, down_out, middle_out, dx1_out, branch_out, mem_out, xhat_out,
    inv_out, gg2_out, rank_out, ids_out,
    WG, WO, WA, WB, WD, Z1, ZE, XC, CC, H1C, GPS, MXS, MT, SWI, DA, DB, X1, H2O, HO, DHQ, FS, NS, BS, I2, SV, SA, SV2, SA2, SENT,
    load_sem, store_sem, stage_sem, t_send, t_recv, c_send, c_recv, h_send, h_recv, r_send, r_recv, e_send, e_recv,
    w_send, w_recv, w_local, s_send, s_recv, x_send, x_recv, i_send, i_recv, n_sem,
):
    place = Place()
    t = place.t
    rows, features = tok_full.shape
    chunk_rows, width = HO.shape
    channels, hidden = MXS.shape[2], SWI.shape[2]
    half = channels // 2
    slab = features // 8
    own_columns = pl.ds(pl.multiple_of(t * width, width), width)

    def rows_of(chunk):
        return pl.ds(chunk * chunk_rows, chunk_rows)

    def columns_of(block, size):
        return pl.ds(pl.multiple_of(block * size, size), size)

    def keep(index, source, target):
        return pltpu.make_async_copy(source, target, stage_sem.at[index])

    own_tokens = keep(0, tokens, tok_full.at[:, own_columns])
    own_cot = keep(1, cotangent, cot_full.at[:, own_columns])
    own_tokens.start()
    own_cot.start()
    greet(place)

    tok_gather = Gather(place, tok_full, t_send, t_recv, chunk_rows, width, tokens)
    cot_gather = Gather(place, cot_full, c_send, c_recv, chunk_rows, width, cotangent)
    h2_gather = Gather(place, h2_full, h_send, h_recv, chunk_rows, width, H2O)
    mix_scatter = Scatter(place, Z1, r_send, r_recv)
    up_scatter = Scatter(place, ZE, e_send, e_recv)
    spreads = [
        Spread(place, index, shard, view, w_send, w_recv, w_local)
        for index, (shard, view) in enumerate((
            (gate_w, lambda group: WG.at[columns_of(group, slab), :]),
            (out_w, lambda group: WO.at[:, columns_of(group, slab)]),
            (up_a_w, lambda group: WA.at[columns_of(group, slab), :]),
            (up_b_w, lambda group: WB.at[columns_of(group, slab), :]),
            (down_w, lambda group: WD.at[:, columns_of(group, slab)]),
        ))
    ]

    block = rows // 8

    def quarter(ref, index):
        return ref.at[index // 2, :, pl.ds(pl.multiple_of((index % 2) * channels, channels), channels)]

    def eighth(ref, group):
        return ref.at[
            group // 4, pl.ds(pl.multiple_of((group % 2) * block, block), block),
            pl.ds(pl.multiple_of(((group // 2) % 2) * channels, channels), channels),
        ]

    def lanes(ref, group):
        return ref.at[:, pl.ds(pl.multiple_of(group * block, block), block)]

    rows_exchange = Exchange(place, lambda group: eighth(DA, group), lambda group: eighth(SWI, group), x_send, x_recv)
    ids_exchange = Exchange(place, lambda group: lanes(SENT, group), lambda group: lanes(ids_out, group), i_send, i_recv)

    def send_rows():
        loads = [pltpu.make_async_copy(mem_in.at[rows_of(index)], quarter(DB, index), load_sem.at[4 + index]) for index in range(4)]
        for copy in loads:
            copy.start()
        row = deal_row[...].astype(jnp.float32)
        columns = [to_column(row[:, index * chunk_rows:(index + 1) * chunk_rows]) for index in range(4)]
        rank = jnp.zeros((1, rows), jnp.float32)
        for chunk in range(4):
            rank += jnp.sum(jnp.where(columns[chunk] < row, 1.0, 0.0), axis=0, keepdims=True)
        rank_out[...] = jnp.broadcast_to(rank, (8, rows)).astype(jnp.int32)
        spots = lax.broadcasted_iota(jnp.int32, (chunk_rows, rows), 1).astype(jnp.float32)
        ordered = jnp.zeros((1, rows), jnp.float32)
        for chunk in range(4):
            column = columns[chunk]
            place_of = jnp.sum(jnp.where(row < column, 1.0, 0.0), axis=1, keepdims=True)
            ordered += jnp.sum(jnp.where(place_of == spots, column, 0.0), axis=0, keepdims=True)
        SENT[...] = jnp.broadcast_to(ordered, (8, rows)).astype(jnp.int32)
        ids_exchange.start()
        for copy in loads:
            copy.wait()

        @pl.loop(0, 4)
        def _(index):
            total = jnp.zeros((chunk_rows, channels), jnp.float32)
            for other in range(4):
                picked = chosen(rank_out[0:1, rows_of(other)], index * chunk_rows, chunk_rows)
                total += jnp.dot(picked, quarter(DB, other)[...], preferred_element_type=jnp.float32)
            quarter(DA, index)[...] = total.astype(jnp.bfloat16)

        rows_exchange.start()

    def mem_store(chunk):
        return pltpu.make_async_copy(MXS.at[chunk % 2], mem_out.at[rows_of(chunk)], load_sem.at[4 + chunk])

    def take_rows():
        ids_exchange.arrived()
        rows_exchange.arrived()
        for chunk in range(4):
            if chunk > 1:
                mem_store(chunk - 2).wait()
            first = rows_exchange.me * rows + chunk * chunk_rows
            total = jnp.zeros((chunk_rows, channels), jnp.float32)
            for other in range(4):
                picked = chosen(ids_out[0:1, rows_of(other)], first, chunk_rows)
                total += jnp.dot(picked, quarter(SWI, other)[...], preferred_element_type=jnp.float32)
            MXS[chunk % 2] = total.astype(jnp.bfloat16)
            mem_store(chunk).start()
        for chunk in (2, 3):
            mem_store(chunk).wait()
        rows_exchange.finish()
        ids_exchange.finish()

    def h1_store(chunk):
        return pltpu.make_async_copy(H1C, h1_out.at[rows_of(chunk)], store_sem.at[0])

    def gate_store(chunk):
        return pltpu.make_async_copy(GPS, gate_out.at[rows_of(chunk)], store_sem.at[1])

    def mixed_store(chunk):
        return pltpu.make_async_copy(MXS.at[chunk % 2], mixed_out.at[rows_of(chunk)], store_sem.at[2 + chunk % 2])

    def hidden_stores(chunk):
        slot = chunk % 3
        return [
            pltpu.make_async_copy(source.at[slot], target.at[rows_of(chunk)], store_sem.at[4 + 3 * index + slot])
            for index, (source, target) in enumerate(((SWI, swi_out), (DA, da_out), (DB, db_out)))
        ]

    def own_h2_store(chunk):
        return pltpu.make_async_copy(H2O.at[rows_of(chunk)], h2_full.at[rows_of(chunk), own_columns], stage_sem.at[4 + chunk])

    def small_store(source, target, chunk, index):
        return pltpu.make_async_copy(source, target.at[rows_of(chunk)], store_sem.at[index])

    def fetch(source, target, index):
        copy = pltpu.make_async_copy(source, target, load_sem.at[index])
        copy.start()
        return copy

    def stat_copy(chunk, step, which):
        source, target = ((SV, SA), (SV2, SA2))[which]
        columns = rows_of(chunk)
        return remote(
            source.at[:, columns], target.at[t, :, columns], s_send.at[which, chunk, step - 1], s_recv.at[which, chunk, step - 1],
            place.along((t + step) % 4),
        )

    def stats(chunk, which):
        source, target = ((SV, SA), (SV2, SA2))[which]
        for step in range(1, 4):
            stat_copy(chunk, step, which).wait_recv()
        total = source[0:1, rows_of(chunk)]
        for step in range(1, 4):
            total = total + target[(t + step) % 4, 0:1, rows_of(chunk)]
        return to_column(total)

    def memory_unit(chunk):
        if chunk == 0:
            own_tokens.wait()
        load = fetch(tok_full.at[rows_of(chunk)], XC, 1)
        mem_load = fetch(mem_out.at[rows_of(chunk)], MT, 0)
        if chunk > 0:
            h1_store(chunk - 1).wait()
        load.wait()
        square = jnp.zeros((chunk_rows, 1), jnp.float32)
        for block in range(4):
            values = XC[:, block * width:(block + 1) * width].astype(jnp.float32)
            square += jnp.sum(values * values, axis=1, keepdims=True)
        inverse = lax.rsqrt(square / features + EPS)
        inv_out[:, rows_of(chunk)] = to_row(inverse)
        HO[...] = XC[:, own_columns].astype(jnp.float32) * inverse
        small_store(HO, xhat_out, chunk, 16).start()
        for block in range(4):
            at = slice(block * width, (block + 1) * width)
            H1C[:, at] = (XC[:, at].astype(jnp.float32) * inverse * gain1[:, at]).astype(jnp.bfloat16)
        h1_store(chunk).start()
        mem_load.wait()
        if chunk > 0:
            gate_store(chunk - 1).wait()
        if chunk > 1:
            mixed_store(chunk - 2).wait()

        @pl.loop(0, 2)
        def _(part):
            at = columns_of(part, half)
            pre = jnp.dot(H1C[...], WG[:, at], preferred_element_type=jnp.float32)
            GPS[:, at] = pre
            MXS[chunk % 2, :, at] = (MT[:, at].astype(jnp.float32) * (pre * jax.nn.sigmoid(pre))).astype(jnp.bfloat16)

        gate_store(chunk).start()
        mixed_store(chunk).start()
        small_store(HO, xhat_out, chunk, 16).wait()

    def mix_part(chunk, block):
        return jnp.dot(MXS[chunk % 2], WO[:, columns_of(block, width)], preferred_element_type=jnp.float32)

    def mix_own(chunk):
        load = fetch(tokens.at[rows_of(chunk)], CC.at[:, 0:width], 2)
        if chunk > 0:
            small_store(X1.at[rows_of(chunk)], middle_out, chunk - 1, 13).wait()
        HO[...] = mix_part(chunk, t)
        mix_scatter.own(chunk, HO)
        load.wait()
        middle = CC[:, 0:width].astype(jnp.float32) + HO[...]
        X1[rows_of(chunk)] = middle
        H2O[rows_of(chunk)] = (middle * gain2[:, own_columns]).astype(jnp.bfloat16)
        own_h2_store(chunk).start()
        SV[:, rows_of(chunk)] = to_row(jnp.sum(middle * middle, axis=1, keepdims=True))
        small_store(X1.at[rows_of(chunk)], middle_out, chunk, 13).start()
        mix_scatter.finish(chunk)
        for step in range(1, 4):
            stat_copy(chunk, step, 0).start()

    def feed_forward(chunk):
        own_h2_store(chunk).wait()
        if chunk == 0:
            own_cot.wait()
        loads = [fetch(h2_full.at[rows_of(chunk)], XC, 1), fetch(cot_full.at[rows_of(chunk)], CC, 3)]
        inverse = lax.rsqrt(stats(chunk, 0) / features + EPS)
        I2[:, rows_of(chunk)] = to_row(inverse)
        if chunk > 2:
            for store in hidden_stores(chunk - 3):
                store.wait()
        for load in loads:
            load.wait()

        @pl.loop(0, 4)
        def _(part):
            at = columns_of(part, hidden // 4)
            up_a = jnp.dot(XC[...], WA[:, at], preferred_element_type=jnp.float32) * inverse
            up_b = jnp.dot(XC[...], WB[:, at], preferred_element_type=jnp.float32) * inverse
            d_swi = dot_nt(CC[...], WD[at, :])
            sigma = jax.nn.sigmoid(up_a)
            swish = up_a * sigma
            SWI[chunk % 3, :, at] = (swish * up_b).astype(jnp.bfloat16)
            d_swi = d_swi * inverse
            DA[chunk % 3, :, at] = (d_swi * up_b * (sigma * (1.0 + up_a * (1.0 - sigma)))).astype(jnp.bfloat16)
            DB[chunk % 3, :, at] = (d_swi * swish).astype(jnp.bfloat16)

        for store in hidden_stores(chunk):
            store.start()

    def down_store(chunk, block):
        return pltpu.make_async_copy(NS.at[block % 2], down_out.at[rows_of(chunk), columns_of(block, width)], n_sem.at[block % 2])

    def down_parts(chunk):
        for block in range(4):
            if chunk > 0 or block > 1:
                down_store(chunk, block).wait()
            NS[block % 2] = jnp.dot(SWI[chunk % 3], WD[:, columns_of(block, width)], preferred_element_type=jnp.float32)
            down_store(chunk, block).start()

    def up_part(chunk, block):
        at = columns_of(block, width)
        return dot_nt(DA[chunk % 3], WA[at, :]) + dot_nt(DB[chunk % 3], WB[at, :])

    def hidden_own(chunk):
        HO[...] = up_part(chunk, t)
        up_scatter.own(chunk, HO)
        middle = X1[rows_of(chunk)]
        d_second = HO[...]
        grads = jnp.sum(d_second * middle, axis=0, keepdims=True)
        if chunk == 0:
            gg2_out[...] = grads
        else:
            gg2_out[...] += grads
        scaled = d_second * gain2[:, own_columns]
        DHQ[...] = scaled
        SV2[:, rows_of(chunk)] = to_row(jnp.sum(scaled * middle, axis=1, keepdims=True) * to_column(I2[0:1, rows_of(chunk)]))
        up_scatter.finish(chunk)
        for step in range(1, 4):
            stat_copy(chunk, step, 1).start()

    def close(chunk):
        load = fetch(cotangent.at[rows_of(chunk)], CC.at[:, 0:width], 2)
        mean = stats(chunk, 1) / features
        if chunk > 0:
            small_store(FS, dx1_out, chunk - 1, 14).wait()
            small_store(BS, branch_out, chunk - 1, 15).wait()
        load.wait()
        unit = X1[rows_of(chunk)] * to_column(I2[0:1, rows_of(chunk)])
        total = CC[:, 0:width].astype(jnp.float32) + DHQ[...] - unit * mean
        FS[...] = total
        BS[...] = total.astype(jnp.bfloat16)
        small_store(FS, dx1_out, chunk, 14).start()
        small_store(BS, branch_out, chunk, 15).start()

    weight_stores = [
        pltpu.make_async_copy(WG, gate_w_out, stage_sem.at[2]), pltpu.make_async_copy(WO, out_w_out, stage_sem.at[3]),
    ]
    is_end = (t == 0) | (t == 3)

    def scatter_step(scatter, part, chunk, step, inside):
        pl.when(jnp.logical_not(is_end) if inside else is_end)(
            lambda: scatter.step(chunk, step, lambda block: part(chunk, block), inside)
        )

    actions = {
        "T": tok_gather.step, "C": cot_gather.step, "H": h2_gather.step, "F1": memory_unit, "F2": feed_forward, "Ro": mix_own,
        "Eo": hidden_own, "close": close, "rows": send_rows, "take": take_rows, "NP": down_parts,
        "Rs": functools.partial(scatter_step, mix_scatter, mix_part), "Es": functools.partial(scatter_step, up_scatter, up_part),
    }
    for name, *where in FRONT_ORDER:
        if name == "W":
            index, number = where
            spreads[index].phase(number)
            if number == 3 and index < 2:
                weight_stores[index].start()
        else:
            actions[name](*where)

    for store in weight_stores:
        store.wait()
    for spread in spreads:
        spread.finish()
    for chunk in range(4):
        for gather in (tok_gather, cot_gather, h2_gather):
            gather.finish(chunk)
        for which in range(2):
            for step in range(1, 4):
                stat_copy(chunk, step, which).wait_send()
    h1_store(3).wait()
    gate_store(3).wait()
    for chunk in (2, 3):
        mixed_store(chunk).wait()
    for chunk in (1, 2, 3):
        for store in hidden_stores(chunk):
            store.wait()
    small_store(X1.at[rows_of(3)], middle_out, 3, 13).wait()
    for block in (2, 3):
        down_store(3, block).wait()
    small_store(FS, dx1_out, 3, 14).wait()
    small_store(BS, branch_out, 3, 15).wait()


def front_call(tokens, cotangent, mem, gate_w, out_w, up_a_w, up_b_w, down_w, gain1, gain2, deal_row):
    rows, width = tokens.shape
    features, channels, hidden = 4 * width, mem.shape[1], up_a_w.shape[1]
    part = rows // 4
    bf, f32 = jnp.bfloat16, jnp.float32
    shape = jax.ShapeDtypeStruct
    anywhere, vmem = pl.BlockSpec(memory_space=pl.ANY), pl.BlockSpec(memory_space=pltpu.VMEM)
    dma = pltpu.SemaphoreType.DMA
    V = pltpu.VMEM
    macs = rows * features * (6 * hidden + 2 * channels)
    return pl.pallas_call(
        front_kernel,
        name="forward",
        out_shape=(
            shape((rows, features), bf), shape((rows, features), bf), shape((rows, features), bf), shape((rows, features), bf),
            shape((rows, channels), f32), shape((rows, channels), bf), shape((rows, hidden), bf), shape((rows, hidden), bf),
            shape((rows, hidden), bf), shape((features, channels), bf), shape((channels, features), bf), shape((rows, features), f32),
            shape((rows, width), f32), shape((rows, width), f32), shape((rows, width), bf), shape((rows, channels), bf), shape((rows, width), f32), shape((8, rows), f32),
            shape((1, width), f32),
            shape((8, rows), jnp.int32), shape((8, rows), jnp.int32),
        ),
        in_specs=[anywhere] * 8 + [vmem] * 3,
        out_specs=(anywhere,) * 17 + (vmem,) * 4,
        scratch_shapes=[
            V((features, channels), bf), V((channels, features), bf), V((features, hidden), bf), V((features, hidden), bf),
            V((hidden, features), bf), V((2, 5, part, width), bf), V((3, 5, part, width), bf),
            V((part, features), bf), V((part, features), bf), V((part, features), bf), V((part, channels), f32), V((2, part, channels), bf),
            V((part, channels), bf), V((3, part, hidden), bf), V((3, part, hidden), bf), V((3, part, hidden), bf), V((rows, width), f32),
            V((rows, width), bf), V((part, width), f32), V((part, width), f32), V((part, width), f32), V((2, part, width), f32), V((part, width), bf),
            V((8, rows), f32), V((8, rows), f32), V((4, 8, rows), f32), V((8, rows), f32), V((4, 8, rows), f32),
            V((8, rows), jnp.int32), dma((8,)), dma((17,)), dma((8,)), dma((4, 2, 3)), dma((4, 4)), dma((4, 2, 3)), dma((4, 4)), dma((4, 2, 3)), dma((4, 4)),
            dma((4, 3)), dma((4, 5)), dma((4, 3)), dma((4, 5)), dma((5, 7)), dma((5, 8)), dma((5,)),
            dma((2, 4, 3)), dma((2, 4, 3)), dma((8,)), dma((8,)), dma((8,)), dma((8,)), dma((2,)),
        ],
        compiler_params=pltpu.CompilerParams(collective_id=2, has_side_effects=True, vmem_limit_bytes=VMEM_LIMIT),
        cost_estimate=pl.CostEstimate(flops=2 * macs, bytes_accessed=96 * 2**20, transcendentals=rows * (channels + hidden)),
    )(tokens, cotangent, mem, gate_w, out_w, up_a_w, up_b_w, down_w, gain1, gain2, deal_row)


def silu_grad(values):
    sigma = jax.nn.sigmoid(values)
    return sigma * (1.0 + values * (1.0 - sigma))


def normalize(values):
    inverse = lax.rsqrt(jnp.mean(values * values, axis=-1, keepdims=True) + EPS)
    return (values * inverse, inverse)


def contract_rows(left, right):
    return lax.dot_general(
        left, right, (((0,), (0,)), ((), ())), preferred_element_type=jnp.float32
    )


def contract_cols(left, right):
    return lax.dot_general(
        left, right, (((1,), (1,)), ((), ())), preferred_element_type=jnp.float32
    )


def sum_scatter(part):
    return lax.psum_scatter(
        part.astype(jnp.bfloat16), "tp", scatter_dimension=1, tiled=True
    ).astype(jnp.float32)


def mean_over(values, features):
    return lax.psum(jnp.sum(values, axis=-1, keepdims=True), "tp") / features


def grad_scatter(part, dimension):
    return lax.psum_scatter(
        part.astype(jnp.bfloat16), ("fsdp", "ctx"), scatter_dimension=dimension, tiled=True
    ).astype(jnp.float32)


def middle_of(tokens, memory_tokens, cotangent, gain_first, gain_second, memory_gate, memory_out, hidden_gate, hidden_up, hidden_down):
    memory_f = memory_tokens.astype(jnp.float32)
    gathered = (
        lax.all_gather(memory_gate, ("fsdp", "ctx"), axis=0, tiled=True),
        lax.all_gather(memory_out, ("fsdp", "ctx"), axis=1, tiled=True),
        lax.all_gather(hidden_gate, ("fsdp", "ctx"), axis=0, tiled=True),
        lax.all_gather(hidden_up, ("fsdp", "ctx"), axis=0, tiled=True),
        lax.all_gather(hidden_down, ("fsdp", "ctx"), axis=1, tiled=True),
    )
    gate_w, out_w, up_a_w, up_b_w, down_w = gathered
    width = tokens.shape[1]
    column = lax.axis_index("tp") * width
    full_tokens, full_cot = (
        lax.all_gather(tokens, "tp", axis=1, tiled=True),
        lax.all_gather(cotangent, "tp", axis=1, tiled=True),
    )
    inputs = full_tokens.astype(jnp.float32)
    unit_first, inv_first = normalize(inputs)
    first = (unit_first * gain_first).astype(jnp.bfloat16)
    gate_pre = jnp.dot(first, gate_w, preferred_element_type=jnp.float32)
    activated = jax.nn.silu(gate_pre)
    mixed = (memory_f * activated).astype(jnp.bfloat16)
    features = full_tokens.shape[1]
    own = lambda array: lax.dynamic_slice_in_dim(array, column, width, array.ndim - 1)
    gain_one, gain_two = own(gain_first), own(gain_second)
    shard_tokens = tokens.astype(jnp.float32)
    middle = shard_tokens + sum_scatter(jnp.dot(mixed, out_w, preferred_element_type=jnp.float32))
    inv_second = lax.rsqrt(mean_over(middle * middle, features) + EPS)
    unit_second = middle * inv_second
    second = lax.all_gather((unit_second * gain_two).astype(jnp.bfloat16), "tp", axis=1, tiled=True)
    up_a = jnp.dot(second, up_a_w, preferred_element_type=jnp.float32)
    up_b = jnp.dot(second, up_b_w, preferred_element_type=jnp.float32)
    swish_a = jax.nn.silu(up_a)
    swished = (swish_a * up_b).astype(jnp.bfloat16)
    output = middle + sum_scatter(jnp.dot(swished, down_w, preferred_element_type=jnp.float32))
    block_out = output.astype(jnp.bfloat16)
    d_swished = contract_cols(full_cot, down_w)
    d_a = (d_swished * up_b * silu_grad(up_a)).astype(jnp.bfloat16)
    d_b = (d_swished * swish_a).astype(jnp.bfloat16)
    d_second = sum_scatter(contract_cols(d_a, up_a_w) + contract_cols(d_b, up_b_w))
    scaled = d_second * gain_two
    middle_norm = inv_second * (scaled - unit_second * mean_over(scaled * unit_second, features))
    gain_two_part = jnp.sum(d_second * unit_second, axis=0)
    d_middle = cotangent.astype(jnp.float32) + middle_norm
    unit_own = shard_tokens * inv_first
    d_branch = lax.all_gather(d_middle.astype(jnp.bfloat16), "tp", axis=1, tiled=True)
    d_mixed = contract_cols(d_branch, out_w)
    back = (d_mixed * activated).astype(jnp.bfloat16)
    d_gate = (d_mixed * memory_f * silu_grad(gate_pre)).astype(jnp.bfloat16)
    d_first = sum_scatter(contract_cols(d_gate, gate_w))
    scaled = d_first * gain_one
    input_norm = inv_first * (scaled - unit_own * mean_over(scaled * unit_own, features))
    gain_one_part = jnp.sum(d_first * unit_own, axis=0)
    parts = lax.psum(jnp.stack([gain_one_part, gain_two_part]), ("fsdp", "ctx"))
    gains = lax.all_gather(parts, "tp", axis=1, tiled=True)
    grad_gain_first, grad_gain_second = gains[0], gains[1]
    sums = (
        grad_scatter(contract_rows(first, d_gate), 0),
        grad_scatter(contract_rows(mixed, d_branch), 1),
        grad_scatter(contract_rows(second, d_a), 0),
        grad_scatter(contract_rows(second, d_b), 0),
        grad_scatter(contract_rows(swished, full_cot), 1),
    )
    return block_out, d_middle, input_norm, back, grad_gain_first, grad_gain_second, sums


def middle_on_line(
    tokens, memory, dealing, cotangent, gain_first, gain_second, memory_gate, memory_out, hidden_gate, hidden_up, hidden_down
):
    width = tokens.shape[1]
    features = 4 * width
    (
        _, full_cot, second, first, gate_pre, mixed, swished, d_a, d_b, gate_w, out_w, down, middle, d_middle, d_branch, memory_tokens,
        unit_own, inv_first, gain_two_part, rank, ids,
    ) = front_call(
        tokens, cotangent, memory, memory_gate, memory_out, hidden_gate, hidden_up, hidden_down, gain_first[None], gain_second[None],
        dealing[None],
    )
    scaled, down_sum, grad_memory, _, _, grad_down, grad_up_a, grad_up_b, grad_out, grad_gate, gains, stats = back_call(
        d_branch, full_cot, swished, second, d_a, d_b, mixed, first, gate_pre, memory_tokens, out_w, gate_w, unit_own, gain_first[None],
        gain_two_part, rank, ids, down,
    )
    block_out = (middle + down_sum).astype(jnp.bfloat16)
    grad_inputs = d_middle + inv_first[0][:, None] * (scaled - unit_own * (stats[0][:, None] / features))
    grad_memory = grad_memory.astype(jnp.float32)
    return (
        block_out, grad_inputs, grad_memory, gains[:, 0].reshape(features), gains[:, 1].reshape(features), grad_gate, grad_out.T,
        grad_up_a, grad_up_b, grad_down.T,
    )


def shards(
    tokens,
    memory,
    dealing,
    cotangent,
    gain_first,
    gain_second,
    memory_gate,
    memory_out,
    hidden_gate,
    hidden_up,
    hidden_down,
):
    if lax.axis_size("fsdp") == 2 and lax.axis_size("ctx") == 4 and lax.axis_size("tp") == 4:
        return middle_on_line(
            tokens, memory, dealing, cotangent, gain_first, gain_second, memory_gate, memory_out, hidden_gate, hidden_up, hidden_down
        )
    groups = lax.axis_size(("fsdp", "ctx"))
    group_index = lax.axis_index(("fsdp", "ctx"))
    rows = dealing.shape[0]
    block = rows // groups
    order = jnp.argsort(dealing)
    sent_rows = memory[order].reshape(groups, block, memory.shape[1])
    arrived = lax.all_to_all(sent_rows, ("fsdp", "ctx"), split_axis=0, concat_axis=0, tiled=True)
    arrived_ids = lax.all_to_all(
        dealing[order].reshape(groups, block),
        ("fsdp", "ctx"),
        split_axis=0,
        concat_axis=0,
        tiled=True,
    )
    places = arrived_ids.reshape(rows) - group_index * rows
    memory_tokens = arrived.reshape(rows, memory.shape[1])[jnp.argsort(places)]
    block_out, d_middle, input_norm, back, grad_gain_first, grad_gain_second, sums = middle_of(
        tokens, memory_tokens, cotangent, gain_first, gain_second, memory_gate, memory_out, hidden_gate, hidden_up, hidden_down
    )
    grad_inputs = d_middle + input_norm
    back_rows = back[places].reshape(groups, block, memory.shape[1])
    returned = lax.all_to_all(back_rows, ("fsdp", "ctx"), split_axis=0, concat_axis=0, tiled=True)
    grad_memory = returned.reshape(rows, memory.shape[1])[jnp.argsort(order)].astype(jnp.float32)
    return (
        block_out,
        grad_inputs,
        grad_memory,
        grad_gain_first,
        grad_gain_second,
        sums[0],
        sums[1],
        sums[2],
        sums[3],
        sums[4],
    )


def solution(mesh):
    in_specs = (
        P(("fsdp", "ctx"), "tp"),
        P(("fsdp", "ctx"), "tp"),
        P(("fsdp", "ctx")),
        P(("fsdp", "ctx"), "tp"),
        P(),
        P(),
        P(("fsdp", "ctx"), "tp"),
        P("tp", ("fsdp", "ctx")),
        P(("fsdp", "ctx"), "tp"),
        P(("fsdp", "ctx"), "tp"),
        P("tp", ("fsdp", "ctx")),
    )
    out_specs = (
        P(("fsdp", "ctx"), "tp"),
        P(("fsdp", "ctx"), "tp"),
        P(("fsdp", "ctx"), "tp"),
        P(),
        P(),
        P(("fsdp", "ctx"), "tp"),
        P("tp", ("fsdp", "ctx")),
        P(("fsdp", "ctx"), "tp"),
        P(("fsdp", "ctx"), "tp"),
        P("tp", ("fsdp", "ctx")),
    )
    return jax.shard_map(shards, mesh=mesh, in_specs=in_specs, out_specs=out_specs, check_vma=False)
```
